32 devices in a mesh: slab: 8 (over z, x), freq: 4 (over y, core).
Axes of the slice: x: 2, y: 2, z: 4, core: 2. Of those that a mesh axis runs over, the one named last changes fastest.
Arguments:
- source: bfloat16 [4, 2, 3, 64, 64, 128], P('freq', None, None, 'slab'), may hold values from -6 to 6
- omega: float32 [4], P('freq'), may hold values from 0.2 to 5
- sigma_blocks: float32 [256], replicated, may hold values from 0.25 to 4
- block_ids: int32 [64, 64, 128], P('slab'), may hold values from 0 to 255
- rec_owner: int32 [1024, 1], P('slab'), may hold values from 0 to 7; in each aligned block of 128 rows (0 to 127, 128 to 255, ...) at most 32 rows name the same one
- rec_edge: int32 [1024], P('slab'), may hold values from 0 to 196607
- observed: float32 [4, 2, 1024], P('freq', None, 'slab'), may hold values from -4 to 4
Outputs:
- forward_field: float32 [4, 2, 3, 64, 64, 128], P('freq', None, None, 'slab')
- adjoint_field: float32 [4, 2, 3, 64, 64, 128], P('freq', None, None, 'slab')
- gradient: float32 [256], replicated
The draws below stay inside these ranges and needn't reach their ends.
Inputs may be any that keep to these rules, and one draw needn't show every extreme that they name: `rec_owner`: among the receiver rows of one slab device no slab is named more than 32 times; in some device's rows one slab is named exactly 32 times.
All inputs are finite; a program needn't handle non-finite values.
Results may differ from the reference program's by a relative error of at most 0.0003.
Values sent between devices are 32-bit elements; how exact they have to be, the bound alone decides.
A program may use at most 256 MiB of HBM per device.

```python
import math
import jax
import jax.numpy as jnp
import numpy as np
from jax import lax

CX = 8
NY = 64
NZ = 128
SWEEPS = 4
REC_DEV = 128
BLK_REG = 32
CAP = 32
NX = 64
NPAIR = 4
NREC = 1024
NBLK = 256
EDGES = 196608
N_SLAB = 8


def draw_block_ids(key, part):
    plane_index = jnp.arange(NX, dtype=jnp.int32)[:, None, None]
    region = (plane_index + CX // 2) // CX % N_SLAB
    inner_block = jax.random.randint(key, (NX, NY, NZ), 0, BLK_REG, dtype=jnp.int32)
    return (region * BLK_REG + inner_block).astype(jnp.int32)


def set_ends(values, own_key, least, top_value):
    dims = values.shape
    index_at = [jax.random.randint(jax.random.fold_in(own_key, axis), (), 0, dims[axis]) for axis in range(len(dims))]
    values = values.at[tuple(index_at)].set(least)
    longest = dims.index(max(dims))
    index_at[longest] = (index_at[longest] + 1) % dims[longest]
    return values.at[tuple(index_at)].set(top_value)


def level_of(rng, extent, pieces, smallest, high):
    loudness, own = 1.0, jax.random.fold_in(rng, 6)
    for position, shards_of in pieces:
        draws = jnp.exp(jax.random.uniform(jax.random.fold_in(own, position), (shards_of,), jnp.float32, smallest / len(pieces), high / len(pieces)))
        loudness = loudness * jnp.repeat(draws, extent[position] // shards_of).reshape([-1 if axis == position else 1 for axis in range(len(extent))])
    return loudness


def deal_out(key, own, number, rows, count, top, bound, skew):
    order = jax.random.permutation(key, count)
    heavy_load, common = shares(count, rows * top, bound, skew, True), shares(count, rows * top, bound, skew, False)
    places = jnp.arange(count)

    def named(tallies, offset_by):
        used = int((tallies > 0).sum())
        fixed = max(1, used // 4)
        shifted = fixed + (places - fixed + offset_by * (used - fixed)) % max(1, count - fixed)
        return jnp.zeros((count,), jnp.int32).at[order[jnp.where(places < fixed, places, shifted)]].set(jnp.asarray(tallies, jnp.int32))

    tallies = jnp.where(number % 4 == 0, named(heavy_load, number // 4), named(common, number - number // 4 - 1))
    mixed = jax.random.permutation(jax.random.fold_in(own, 3), count)
    source_of, sink = mixed[0:count // 2 * 2:2], mixed[1:count // 2 * 2:2]
    margin = jnp.minimum(tallies[source_of] - 1, bound - tallies[sink]) // 2
    margin = jnp.where((source_of == order[0]) | (sink == order[0]) | (tallies[sink] == 0), 0, jnp.maximum(margin, 0))
    shifted = jax.random.randint(jax.random.fold_in(own, 4), (count // 2,), 0, 1 << 20) % (margin + 1)
    tallies = tallies.at[source_of].add(-shifted).at[sink].add(shifted)
    members = jnp.searchsorted(jnp.cumsum(tallies), jnp.arange(rows * top), side="right").astype(jnp.int32)
    grid = members.reshape(top, rows).T
    grid = grid[jax.random.permutation(jax.random.fold_in(own, 1), rows)]
    offset_by = jax.random.randint(jax.random.fold_in(own, 2), (rows, 1), 0, top)
    return jnp.take_along_axis(grid, (jnp.arange(top)[None, :] + offset_by) % top, axis=1)


def shares(number_of, total, most, slope, full):
    portions = [(1 << 20) // math.isqrt(grade ** slope) + 1 for grade in range(1, number_of + 1)]
    largest = most if full else min(most, max(-(-total // number_of), total * portions[0] // sum(portions)))
    least = 1 if total - largest >= number_of - 1 else 0
    counts, surplus = [largest] + [least] * (number_of - 1), total - largest - least * (number_of - 1)
    while surplus > 0:
        movable = [i for i in range(1, number_of) if counts[i] < largest] or [i for i in range(1, number_of) if counts[i] < most]
        whole, remaining = sum([portions[i] for i in movable]), surplus
        for i in movable:
            addition = min(most - counts[i], max(1, remaining * portions[i] // whole), surplus)
            counts[i] = counts[i] + addition
            surplus = surplus - addition
    return np.array(counts)


def bell_draw(stream_key, dims, spread, reach, split=(), kind=jnp.bfloat16):
    entries = spread * jax.random.normal(stream_key, dims, jnp.float32)
    if split:
        entries = entries * level_of(stream_key, dims, split, -0.22, 0.18)
    return jnp.clip(entries, -reach, reach).astype(kind)


def setup_inputs(seed: int = 0) -> dict:
    streams_of = jax.random.split(jax.random.key(seed), 8)
    source = bell_draw(streams_of[0], (NPAIR, 2, 3, NX, NY, NZ), 1.0, 6.0, ((0, 4), (3, 8)))
    omega = jnp.clip(jnp.exp(math.log(5.0) - 3.218876 * jax.random.uniform(streams_of[1], (NPAIR,), jnp.float32) ** level_of(streams_of[1], (NPAIR,), ((0, 4),), -0.2, 0.2)), 0.2, 5.0)
    sigma_blocks = jnp.clip(jnp.exp(jax.random.uniform(streams_of[2], (NBLK,), jnp.float32, math.log(0.25), math.log(4.0))), 0.25, 4.0)
    block_ids = draw_block_ids(jax.random.fold_in(streams_of[7], 71), 0)
    rec_owner_keys = jax.random.split(jax.random.fold_in(streams_of[4], 1), NREC // REC_DEV)
    rec_owner_turns = jax.random.permutation(jax.random.fold_in(streams_of[4], 3), NREC // REC_DEV)
    rec_owner = jax.vmap(lambda own, number: deal_out(jax.random.fold_in(streams_of[4], 2), own, number, REC_DEV, N_SLAB, 1, CAP, 2))(rec_owner_keys, rec_owner_turns).reshape((NREC, 1))
    rec_edge = set_ends(jax.random.randint(streams_of[5], (NREC,), 0, EDGES), jax.random.fold_in(streams_of[5], 1), 0, EDGES - 1).astype(jnp.int32)
    observed = bell_draw(streams_of[6], (NPAIR, 2, NREC), 0.3, 4.0, ((0, 4), (2, 8)), jnp.float32)
    return dict(source=source, omega=omega, sigma_blocks=sigma_blocks, block_ids=block_ids, rec_owner=rec_owner, rec_edge=rec_edge, observed=observed)


epsilon = 1e-6


def forward_diff(values, along):
    along = along % values.ndim
    count = values.shape[along]
    ahead_values = jnp.concatenate([lax.slice_in_dim(values, 1, count, axis=along), jnp.zeros_like(lax.slice_in_dim(values, 0, 1, axis=along))], axis=along)
    return ahead_values - values


def adjoint_diff(values, along):
    along = along % values.ndim
    count = values.shape[along]
    behind = jnp.concatenate([jnp.zeros_like(lax.slice_in_dim(values, 0, 1, axis=along)), lax.slice_in_dim(values, 0, count - 1, axis=along)], axis=along)
    return behind - values


def curl_curl(field):
    edge_first = field[..., 0, :, :, :]
    edge_second = field[..., 1, :, :, :]
    edge_third = field[..., 2, :, :, :]
    curl_first = forward_diff(edge_third, -2) - forward_diff(edge_second, -1)
    curl_second = forward_diff(edge_first, -1) - forward_diff(edge_third, -3)
    curl_third = forward_diff(edge_second, -3) - forward_diff(edge_first, -2)
    back_first = adjoint_diff(curl_second, -1) - adjoint_diff(curl_third, -2)
    back_second = adjoint_diff(curl_third, -3) - adjoint_diff(curl_first, -1)
    back_third = adjoint_diff(curl_first, -2) - adjoint_diff(curl_second, -3)
    return jnp.stack([back_first, back_second, back_third], axis=-4)


def residual_sweeps(right_side, damping):
    denominator = 16.0 + damping * damping
    residual = right_side
    solution = jnp.zeros_like(right_side)
    for iteration in range(SWEEPS):
        residual_real = residual[0]
        residual_imag = residual[1]
        precond_real = (4.0 * residual_real + damping * residual_imag) / denominator
        precond_imag = (4.0 * residual_imag - damping * residual_real) / denominator
        stiffness = curl_curl(jnp.stack([precond_real, precond_imag]))
        image_real = stiffness[0] - damping * precond_imag
        image_imag = stiffness[1] + damping * precond_real
        upper_real = jnp.sum(image_real * residual_real + image_imag * residual_imag)
        upper_imag = jnp.sum(image_real * residual_imag - image_imag * residual_real)
        lower_sum = jnp.sum(image_real * image_real + image_imag * image_imag) + epsilon
        step_real = upper_real / lower_sum
        step_imag = upper_imag / lower_sum
        solution = solution + jnp.stack([step_real * precond_real - step_imag * precond_imag, step_real * precond_imag + step_imag * precond_real])
        residual = residual - jnp.stack([step_real * image_real - step_imag * image_imag, step_real * image_imag + step_imag * image_real])
    return solution


def reference(source, omega, sigma_blocks, block_ids, rec_owner, rec_edge, observed):
    conductivity = jnp.take(sigma_blocks, block_ids, axis=0)
    component = rec_edge // (CX * NY * NZ)
    remainder = rec_edge % (CX * NY * NZ)
    plane_index = remainder // (NY * NZ)
    inside = remainder % (NY * NZ)
    global_edge = (component * (NX * NY * NZ) + (rec_owner[:, 0] * CX + plane_index) * (NY * NZ) + inside).astype(jnp.int32)

    def per_pair(inputs):
        right_side, frequency, measured = inputs
        damping = frequency * conductivity
        forward_field = residual_sweeps(right_side.astype(jnp.float32), damping)
        flat_field = forward_field.reshape(2, -1)
        predicted = jnp.take(flat_field, global_edge, axis=1)
        misfit = predicted - measured
        adjoint_flat = jnp.zeros_like(flat_field).at[0, global_edge].add(misfit[0]).at[1, global_edge].add(-misfit[1])
        adjoint_field = residual_sweeps(adjoint_flat.reshape(forward_field.shape), damping)
        cell_term = frequency * jnp.sum(adjoint_field[0] * forward_field[1] + adjoint_field[1] * forward_field[0], axis=0)
        block_term = jax.ops.segment_sum(cell_term.reshape(-1), block_ids.reshape(-1), num_segments=BLK_REG * N_SLAB)
        return forward_field, adjoint_field, block_term

    forward_field, adjoint_field, pair_terms = lax.map(per_pair, (source, omega, observed))
    return forward_field, adjoint_field, jnp.sum(pair_terms, axis=0)
```

```python
import functools

import jax
import jax.numpy as jnp
from jax import lax
from jax.experimental import pallas as pl
from jax.experimental.pallas import tpu as pltpu
from jax.sharding import PartitionSpec as P

SWEEPS = 4
EPSILON = 1e-06
LOW = 16
CAP = 32
MESH = pl.DeviceIdType.MESH
F32 = jnp.float32
BF16 = jnp.bfloat16
PAIRS = [(i, j) for j in range(1, SWEEPS + 1) for i in range(j + 1)]
COUNT = sum(1 if i == j else 2 for i, j in PAIRS)
WIDTH = SWEEPS


def split(values):
    high = values.astype(BF16)
    return high, (values - high.astype(F32)).astype(BF16)


def kernel(
    n, nf, high_blocks,
    omega_ref, source_hbm, sigma_hbm, ids_hbm, owner_hbm, edge_hbm, observed_hbm,
    forward_ref, adjoint_ref, gradient_ref,
    source_ref, sigma_ref, ids_ref, owner_ref, edge_ref, observed_ref,
    damp, real_ref, imag_ref, cond, beside, pack_ref, mis_out, mis_in,
    basis, zb, curl, up_out, down_out, low_in, high_in,
    gram_acc, gram_out, gram_in, pack_in, grad_out, grad_in, grad_out2, grad_in2,
    columns, hot, hot_t, field_hi, field_lo, mis_hi, mis_lo, acc,
    local_s, up_s, up_r, down_s, down_r, gram_s, gram_r, pack_s, pack_r, grad_s, grad_r, grad2_s, grad2_r,
    near_s, near_r, share_s, share_r,
):
    me = lax.axis_index("slab")
    mine = lax.axis_index("freq")
    planes, rows, lanes = ids_ref.shape
    first, last = WIDTH, WIDTH + planes - 1
    wide_planes = planes + 2 * WIDTH
    cells_rows = 3 * planes * rows
    slots = n * CAP
    side_rows = WIDTH * rows
    part = side_rows // nf

    loads = [
        pltpu.make_async_copy(src, dst, local_s.at[k])
        for k, (src, dst) in enumerate([
            (ids_hbm, ids_ref), (sigma_hbm, sigma_ref), (source_hbm, source_ref),
            (owner_hbm, owner_ref), (edge_hbm, edge_ref), (observed_hbm, observed_ref),
        ])
    ]
    for copy in loads:
        copy.start()

    barrier = pltpu.get_barrier_semaphore()
    for d in range(1, n):
        pl.semaphore_signal(barrier, inc=1, device_id={"slab": lax.rem(me + d, n)}, device_id_type=MESH)
    for d in range(1, nf):
        pl.semaphore_signal(barrier, inc=1, device_id={"freq": lax.rem(mine + d, nf)}, device_id_type=MESH)

    def spread(src, dst, send, recv, axis, count, position):
        copies = []
        for d in range(1, count):
            copy = pltpu.make_async_remote_copy(
                src_ref=src, dst_ref=dst.at[d], send_sem=send.at[d], recv_sem=recv.at[d],
                device_id={axis: lax.rem(position + d, count)}, device_id_type=MESH,
            )
            copy.start()
            copies.append(copy)
        return copies

    def total_of(own, buffer, count, position):
        buffer[0] = own
        total = jnp.zeros(own.shape, F32)
        for p in range(count):
            total = total + buffer[lax.rem(position - p + count, count)]
        return total

    lane = lax.broadcasted_iota(jnp.int32, (rows, lanes), 1)
    row = lax.broadcasted_iota(jnp.int32, (rows, lanes), 0)
    inner = slice(0, rows)
    above = slice(1, rows + 1)
    shifted = slice(8, rows + 8)
    under = slice(7, rows + 7)

    def f3(v):
        return jnp.where(lane == lanes - 1, 0.0, pltpu.roll(v, lanes - 1, 1)) - v

    def g3(v):
        return jnp.where(lane == 0, 0.0, pltpu.roll(v, 1, 1)) - v

    valid = jnp.where(me > 0, 1.0, 0.0).astype(F32)
    omega = omega_ref[0]

    def factors(x, at, damping):
        inverse = 1.0 / (16.0 + damping * damping)
        damp[x, at] = damping
        real_ref[x, at] = 4.0 * inverse
        imag_ref[x, at] = damping * inverse

    def pad(x, carry):
        for c in range(2):
            for comp in range(3):
                zb[c, comp, x, rows : rows + 8] = jnp.zeros((8, lanes), F32)
                curl[c, comp, x, 0:8] = jnp.zeros((8, lanes), F32)
        return carry

    lax.fori_loop(0, wide_planes, pad, 0)

    chunks = rows // 16
    loads[0].wait()
    loads[1].wait()
    loads[2].wait()
    tables = [jnp.broadcast_to(sigma_ref[k : k + 1, :], (8, lanes)) for k in range(sigma_ref.shape[0])]

    def begin(x, y):
        for half in range(2):
            at = pl.ds(pl.multiple_of(y + 8 * half, 8), 8)
            ids = ids_ref[x, at, :]
            low, high = ids & (lanes - 1), ids >> 7
            value = jnp.take_along_axis(tables[0], low, axis=1)
            for k in range(1, len(tables)):
                value = jnp.where(high == k, jnp.take_along_axis(tables[k], low, axis=1), value)
            cond[pl.ds(pl.multiple_of(x * rows + y + 8 * half, 8), 8), :] = value
            factors(x + first, at, omega * value)
        at = pl.ds(y, 16)
        for c in range(2):
            for comp in range(3):
                basis[0, c, comp, x + first, at] = source_ref[c, comp, x, at, :].astype(F32)

    def begin_ends(i, carry):
        begin(i // chunks * (planes - 1), pl.multiple_of(i % chunks * 16, 16))
        return carry

    def begin_inner(i, carry):
        begin(i // chunks + 1, pl.multiple_of(i % chunks * 16, 16))
        return carry

    lax.fori_loop(0, 2 * chunks, begin_ends, 0, unroll=4)

    def beside_copy(side):
        start, to = (planes * rows - side_rows, me + 1) if side == 0 else (0, me + n - 1)
        return pltpu.make_async_remote_copy(
            src_ref=cond.at[pl.ds(start + mine * part, part)], dst_ref=beside.at[side, pl.ds(mine * part, part)],
            send_sem=near_s.at[side], recv_sem=near_r.at[side], device_id={"slab": lax.rem(to, n)},
            device_id_type=MESH,
        )

    def share_copies(side):
        at = pl.ds(mine * part, part)
        return [
            pltpu.make_async_remote_copy(
                src_ref=beside.at[side, at], dst_ref=beside.at[side, at], send_sem=share_s.at[side, d],
                recv_sem=share_r.at[side, d], device_id={"freq": lax.rem(mine + d, nf)}, device_id_type=MESH,
            )
            for d in range(1, nf)
        ]

    def misfit_copy(side):
        to = me + 1 if side == 0 else me + n - 1
        return pltpu.make_async_remote_copy(
            src_ref=mis_out, dst_ref=mis_in.at[side], send_sem=near_s.at[2 + side],
            recv_sem=near_r.at[2 + side], device_id={"slab": lax.rem(to, n)}, device_id_type=MESH,
        )

    def up_copy(slot):
        return pltpu.make_async_remote_copy(
            src_ref=up_out.at[slot], dst_ref=low_in.at[slot], send_sem=up_s.at[slot],
            recv_sem=up_r.at[slot], device_id={"slab": lax.rem(me + 1, n)}, device_id_type=MESH,
        )

    def down_copy(slot):
        return pltpu.make_async_remote_copy(
            src_ref=down_out.at[slot], dst_ref=high_in.at[slot], send_sem=down_s.at[slot],
            recv_sem=down_r.at[slot], device_id={"slab": lax.rem(me + n - 1, n)}, device_id_type=MESH,
        )

    def precondition(t, x):
        mr, mi = real_ref[x], imag_ref[x]
        for comp in range(3):
            br, bi = basis[t, 0, comp, x], basis[t, 1, comp, x]
            zb[0, comp, x, inner] = mr * br + mi * bi
            zb[1, comp, x, inner] = mr * bi - mi * br

    def curls(x, ahead=None):
        for c in range(2):
            e1, e2, e3 = zb[c, 0, x, inner], zb[c, 1, x, inner], zb[c, 2, x, inner]
            if ahead is None:
                e2n, e3n = zb[c, 1, x + 1, inner], zb[c, 2, x + 1, inner]
            else:
                e2n, e3n = ahead[c, 0], ahead[c, 1]
            curl[c, 0, x, shifted] = (zb[c, 2, x, above] - e3) - f3(e2)
            curl[c, 1, x, shifted] = f3(e1) - (e3n - e3)
            curl[c, 2, x, shifted] = (e2n - e2) - (zb[c, 0, x, above] - e1)

    def images(t, x, keep=None):
        damping = damp[x]
        for c in range(2):
            b1, b2, b3 = curl[c, 0, x, shifted], curl[c, 1, x, shifted], curl[c, 2, x, shifted]
            b2p, b3p = curl[c, 1, x - 1, shifted], curl[c, 2, x - 1, shifted]
            if keep is not None:
                b2p, b3p = b2p * keep, b3p * keep
            parts = (
                g3(b2) - (curl[c, 2, x, under] - b3),
                (b3p - b3) - g3(b1),
                (curl[c, 0, x, under] - b1) - (b2p - b2),
            )
            for comp in range(3):
                turned = damping * zb[1 - c, comp, x, inner]
                basis[t + 1, c, comp, x] = parts[comp] - turned if c == 0 else parts[comp] + turned

    def sweep(t, lo, hi, masked):
        for k in range(4):
            precondition(t, lo + k)
        curls(lo)
        curls(lo + 1)

        def keep_of(x):
            if not masked:
                return None
            return jnp.where((x == first) & (me == 0), 0.0, 1.0).astype(F32)

        def step(x, carry):
            images(t, x, keep_of(x))
            curls(x + 1)
            precondition(t, x + 3)
            return carry

        lax.fori_loop(lo + 1, hi - 2, step, 0)
        images(t, hi - 2)
        curls(hi - 1)
        images(t, hi - 1)

    def send_down(t):
        precondition(t, first)
        for c in range(2):
            down_out[t, c, 0] = zb[c, 1, first, inner]
            down_out[t, c, 1] = zb[c, 2, first, inner]

        @pl.when(me > 0)
        def _():
            down_copy(t).start()

    def send_up(t):
        precondition(t, last)
        for c in range(2):
            e1 = zb[c, 0, last, inner]
            up_out[t, c, 0] = f3(e1) + zb[c, 2, last, inner]
            up_out[t, c, 1] = (zb[c, 0, last, above] - e1) + zb[c, 1, last, inner]

        @pl.when(me < n - 1)
        def _():
            up_copy(t).start()

    def forward_sweep(t, meanwhile):
        sweep(t, first, last, False)
        meanwhile()

        @pl.when(me > 0)
        def _():
            up_copy(t).wait_recv()
            down_copy(t).wait_send()

        @pl.when(me == 0)
        def _():
            low_in[t] = jnp.zeros(low_in.shape[1:], F32)

        for c in range(2):
            curl[c, 1, first - 1, shifted] = (low_in[t, c, 0] - zb[c, 2, first, inner]) * valid
            curl[c, 2, first - 1, shifted] = (zb[c, 1, first, inner] - low_in[t, c, 1]) * valid
        images(t, first)
        if t < SWEEPS - 1:
            send_down(t + 1)

        @pl.when(me < n - 1)
        def _():
            down_copy(t).wait_recv()
            up_copy(t).wait_send()

        @pl.when(me == n - 1)
        def _():
            high_in[t] = jnp.zeros(high_in.shape[1:], F32)

        curls(last, high_in.at[t])
        images(t, last)
        if t < SWEEPS - 1:
            send_up(t + 1)

    per = rows // 8

    def pair_sums(j_):
        width = 2 * j_ + 1

        def products(i, sums):
            x, y = i // per + first, pl.multiple_of(i % per * 8, 8)
            sums = list(sums)
            for comp in range(3):
                re = [basis[k, 0, comp, x, pl.ds(y, 8), :] for k in range(j_ + 1)]
                im = [basis[k, 1, comp, x, pl.ds(y, 8), :] for k in range(j_ + 1)]
                for i_ in range(j_ + 1):
                    sums[2 * i_] = sums[2 * i_] + (re[i_] * re[j_] + im[i_] * im[j_])
                    if i_ != j_:
                        sums[2 * i_ + 1] = sums[2 * i_ + 1] + (re[i_] * im[j_] - im[i_] * re[j_])
            return tuple(sums)

        zero = jnp.zeros((8, lanes), F32)
        sums = lax.fori_loop(0, planes * per, products, (zero,) * width, unroll=2)
        for k in range(width):
            at = j_ * j_ - 1 + k
            gram_acc[at : at + 1, :] = jnp.sum(sums[k], axis=0, keepdims=True)

    gram_lane = lax.broadcasted_iota(jnp.int32, (COUNT, lanes), 1)
    gram_row = lax.broadcasted_iota(jnp.int32, (COUNT, lanes), 0)
    diagonal_of = gram_lane == gram_row

    def gram_start(which):
        local = jnp.sum(gram_acc[...], axis=1, keepdims=True)
        gram_out[which] = jnp.sum(jnp.where(diagonal_of, local, 0.0), axis=0, keepdims=True)
        return spread(gram_out.at[which], gram_in.at[which], gram_s.at[which], gram_r.at[which], "slab", n, me)

    def coefficients(which):
        total = total_of(gram_out[which], gram_in.at[which], n, me)
        total = jnp.sum(jnp.where(diagonal_of, total, 0.0), axis=1, keepdims=True)
        total = jnp.broadcast_to(total, (COUNT, lanes))
        gram, at = {}, 0
        for i, j in PAIRS:
            re = total[at : at + 1, :]
            at += 1
            im = jnp.zeros_like(re)
            if i != j:
                im = total[at : at + 1, :]
                at += 1
            gram[i, j] = (re, im)
            gram[j, i] = (re, -im)
        one = jnp.ones((1, lanes), F32)
        none = jnp.zeros((1, lanes), F32)

        def times(a, b):
            return a[0] * b[0] - a[1] * b[1], a[0] * b[1] + a[1] * b[0]

        poly = [(one, none)]
        coef = [(none, none) for _ in range(SWEEPS)]
        for k in range(SWEEPS):
            up = (none, none)
            below = none
            for i in range(k + 1):
                conj = (poly[i][0], -poly[i][1])
                for j in range(k + 1):
                    both = times(conj, poly[j])
                    term = times(both, gram[i + 1, j])
                    up = (up[0] + term[0], up[1] + term[1])
                    below = below + times(both, gram[i + 1, j + 1])[0]
            below = below + EPSILON
            step = (up[0] / below, up[1] / below)
            moved = [times(step, p) for p in poly]
            for i in range(k + 1):
                coef[i] = (coef[i][0] + moved[i][0], coef[i][1] + moved[i][1])
            grown = poly + [(none, none)]
            for i in range(k + 1):
                grown[i + 1] = (grown[i + 1][0] - moved[i][0], grown[i + 1][1] - moved[i][1])
            poly = grown

        return [(jnp.broadcast_to(a, (16, lanes)), jnp.broadcast_to(b, (16, lanes))) for a, b in coef]

    def combine(wide, out_ref, keep_parts):
        def step(i, carry):
            x, y = i // chunks, pl.multiple_of(i % chunks * 16, 16)
            at = pl.ds(y, 16)
            mr, mi = real_ref[x + first, at, :], imag_ref[x + first, at, :]
            for comp in range(3):
                sr = jnp.zeros((16, lanes), F32)
                si = jnp.zeros((16, lanes), F32)
                for k in range(SWEEPS):
                    br, bi = basis[k, 0, comp, x + first, at, :], basis[k, 1, comp, x + first, at, :]
                    sr = sr + (wide[k][0] * br - wide[k][1] * bi)
                    si = si + (wide[k][0] * bi + wide[k][1] * br)
                for c, value in enumerate((mr * sr + mi * si, mr * si - mi * sr)):
                    out_ref[c, comp, x, at, :] = value
                    if keep_parts:
                        here = pl.ds(pl.multiple_of((comp * planes + x) * rows + y, 16), 16)
                        hi, lo = split(value)
                        field_hi[here, c * lanes : (c + 1) * lanes] = hi
                        field_lo[here, c * lanes : (c + 1) * lanes] = lo
            return carry

        lax.fori_loop(0, planes * chunks, step, 0, unroll=2)

    packs = [
        pltpu.make_async_remote_copy(
            src_ref=pack_ref, dst_ref=pack_in.at[me], send_sem=pack_s.at[d], recv_sem=pack_r.at[d],
            device_id={"slab": lax.rem(me + d, n)}, device_id_type=MESH,
        )
        for d in range(1, n)
    ]

    cap_row = lax.broadcasted_iota(jnp.int32, (CAP, lanes), 0).astype(F32)
    lane_sq = lax.broadcasted_iota(jnp.int32, (lanes, lanes), 1).astype(F32)
    row_sq = lax.broadcasted_iota(jnp.int32, (lanes, lanes), 0).astype(F32)
    earlier = jnp.where(row_sq < lane_sq, 1.0, 0.0).astype(F32)
    self_id = me.astype(F32)

    def compact(p, carry):
        pack = pack_in[p]
        owner, number, spot = pack[0:1, :], pack[1:2, :], pack[2:3, :]
        third = jnp.where(number >= 2.0 * planes * rows, 2.0, jnp.where(number >= 1.0 * planes * rows, 1.0, 0.0))
        inside = number - third * float(planes * rows)
        upper = inside - float((planes - WIDTH) * rows)
        low_place = jnp.where(upper >= 0.0, third * float(side_rows) + upper, -1.0)
        high_place = jnp.where(inside < float(side_rows), third * float(side_rows) + inside, -1.0)
        owned = [jnp.where(owner == self_id + shift, 1.0, 0.0) for shift in (0.0, -1.0, 1.0)]
        owned = jnp.concatenate(owned + [jnp.zeros((5, lanes), F32)], axis=0)
        rank = jnp.dot(owned, earlier, preferred_element_type=F32)
        at = pl.ds(pl.multiple_of(p * CAP, CAP), CAP)
        wanted = (
            (0, 0, number + 1.0), (1, 0, spot), (2, 0, pack[3:4, :]), (3, 0, pack[4:5, :]),
            (4, 1, low_place + 1.0), (5, 1, spot), (6, 2, high_place + 1.0), (7, 2, spot),
        )
        for k, target, value in wanted:
            hit = (cap_row == rank[target : target + 1, :]) & (owned[target : target + 1, :] > 0.0)
            found = jnp.sum(jnp.where(hit, value, 0.0), axis=1, keepdims=True)
            columns[k, at, :] = jnp.broadcast_to(found, (CAP, lanes))
        return carry

    def picks(p, carry):
        at = pl.ds(pl.multiple_of(p * CAP, CAP), CAP)
        place = columns[0, at, :] - 1.0
        for b in range(cells_rows // lanes):
            hot[at, b * lanes : (b + 1) * lanes] = jnp.where(
                lane_sq[:CAP] == place - float(b * lanes), 1.0, 0.0
            ).astype(BF16)
        return carry

    def placings(start, k, count):
        for q in range(slots // lanes):
            spot = columns[k, q * lanes : (q + 1) * lanes, :].T - 1.0

            def fill(b, carry):
                base = pl.multiple_of(b * lanes, lanes)
                hot_t[pl.ds(start + base, lanes), q * lanes : (q + 1) * lanes] = jnp.where(
                    row_sq + base.astype(F32) == spot, 1.0, 0.0
                ).astype(BF16)
                return carry

            lax.fori_loop(0, count // lanes, fill, 0)

    def spread_values(k, re, im):
        here = lane_of_slot == columns[k]
        for part_, value in enumerate((re, im)):
            hi, lo = split(jnp.where(here, value, 0.0))
            mis_hi[:, part_ * lanes : (part_ + 1) * lanes] = hi
            mis_lo[:, part_ * lanes : (part_ + 1) * lanes] = lo

    def add_source(start, x0, count, group):
        for comp in range(3):
            for x in range(0, count, group):
                begin_ = start + (comp * count + x) * rows
                block = hot_t[begin_ : begin_ + group * rows, :]
                added = jnp.dot(block, mis_hi[...], preferred_element_type=F32)
                added = added + jnp.dot(block, mis_lo[...], preferred_element_type=F32)
                for c in range(2):
                    basis[0, c, comp, x0 + x : x0 + x + group] = added[:, c * lanes : (c + 1) * lanes].reshape(
                        group, rows, lanes
                    )

    lane_of_slot = lax.broadcasted_iota(jnp.int32, (slots, lanes), 1).astype(F32)

    pl.semaphore_wait(barrier, n + nf - 2)
    send_down(0)
    send_up(0)
    loads[3].wait()
    loads[4].wait()
    loads[5].wait()
    edge = edge_ref[...]
    pack_ref[...] = jnp.concatenate(
        [
            owner_ref[...].astype(F32), (edge >> 7).astype(F32), (edge & 127).astype(F32), observed_ref[...],
            jnp.zeros((3, lanes), F32),
        ],
        axis=0,
    )
    for copy in packs:
        copy.start()
    pack_in[me] = pack_ref[...]
    lax.fori_loop(0, (planes - 2) * chunks, begin_inner, 0, unroll=4)

    def while_first():
        pair_sums(1)
        for copy in packs:
            copy.wait()
        lax.fori_loop(0, n, compact, 0)

    def while_second():
        pair_sums(2)
        lax.fori_loop(0, n, picks, 0)

    def while_third():
        pair_sums(3)
        placings(0, 0, cells_rows)
        placings(cells_rows, 4, 3 * side_rows)
        placings(cells_rows + 3 * side_rows, 6, 3 * side_rows)

    forward_sweep(0, lambda: None)
    forward_sweep(1, while_first)
    forward_sweep(2, while_second)
    forward_sweep(3, while_third)
    pair_sums(SWEEPS)
    for copy in gram_start(0):
        copy.wait()

    @pl.when(me > 0)
    def _():
        beside_copy(1).start()

    @pl.when(me < n - 1)
    def _():
        beside_copy(0).start()

    combine(coefficients(0), forward_ref, True)

    picked = jnp.dot(hot[...], field_hi[...], preferred_element_type=F32)
    picked = picked + jnp.dot(hot[...], field_lo[...], preferred_element_type=F32)
    here = lane_of_slot == columns[1]
    re = jnp.sum(jnp.where(here, picked[:, :lanes], 0.0), axis=1, keepdims=True) - columns[2]
    im = columns[3] - jnp.sum(jnp.where(here, picked[:, lanes:], 0.0), axis=1, keepdims=True)
    both = jnp.where(lane_of_slot == 0.0, re, jnp.where(lane_of_slot == 1.0, im, 0.0))
    mis_out[...] = both.T[0:8, :]

    @pl.when(me > 0)
    def _():
        misfit_copy(1).start()
        beside_copy(0).wait_recv()
        for copy in share_copies(0):
            copy.start()

    @pl.when(me < n - 1)
    def _():
        misfit_copy(0).start()
        beside_copy(1).wait_recv()
        for copy in share_copies(1):
            copy.start()

    spread_values(1, re, im)
    add_source(0, first, planes, 4)

    for side, there in enumerate((me > 0, me < n - 1)):
        start = 0 if side == 0 else last + 1

        @pl.when(there)
        def _(side=side, start=start):
            beside_copy(1 - side).wait_send()
            for copy in share_copies(side):
                copy.wait()
            for k in range(WIDTH):
                factors(start + k, inner, omega * beside[side, k * rows : (k + 1) * rows, :])
            misfit_copy(side).wait_recv()
            misfit_copy(1 - side).wait_send()

        @pl.when(jnp.logical_not(there))
        def _(side=side, start=start):
            mis_in[side] = jnp.zeros(mis_in.shape[1:], F32)
            for k in range(WIDTH):
                damp[start + k] = jnp.zeros((rows, lanes), F32)
                real_ref[start + k] = jnp.zeros((rows, lanes), F32)
                imag_ref[start + k] = jnp.zeros((rows, lanes), F32)

        column = jnp.concatenate([mis_in[side]] * (lanes // 8), axis=0).T
        spread_values(5 + 2 * side, column[:, 0:1], column[:, 1:2])
        add_source(cells_rows + side * 3 * side_rows, start, WIDTH, WIDTH)

    for t in range(SWEEPS):
        sweep(t, t, wide_planes - t - 1, True)
        if t:
            pair_sums(t)
    pair_sums(SWEEPS)
    for copy in gram_start(1):
        copy.wait()
    combine(coefficients(1), adjoint_ref, False)

    high_iota = lax.broadcasted_iota(jnp.int32, (high_blocks, lanes), 0)
    low_iota = lax.broadcasted_iota(jnp.int32, (LOW, lanes), 0)
    acc[...] = jnp.zeros(acc.shape, F32)

    def cells(i, carry):
        x, y = i // chunks, pl.multiple_of(i % chunks * 16, 16)
        value = jnp.zeros((16, lanes), F32)
        for comp in range(3):
            fr, fi = forward_ref[0, comp, x, pl.ds(y, 16), :], forward_ref[1, comp, x, pl.ds(y, 16), :]
            ar, ai = adjoint_ref[0, comp, x, pl.ds(y, 16), :], adjoint_ref[1, comp, x, pl.ds(y, 16), :]
            value = value + (ar * fi + ai * fr)
        value = omega * value
        ids = ids_ref[x, pl.ds(y, 16), :]
        high, low = ids >> 4, ids & (LOW - 1)
        hot = jnp.concatenate(
            [jnp.where(high[r : r + 1, :] == high_iota, 1.0, 0.0) for r in range(16)], axis=0
        ).astype(BF16)
        spot = jnp.concatenate(
            [jnp.where(low[r : r + 1, :] == low_iota, value[r : r + 1, :], 0.0) for r in range(16)], axis=0
        )
        acc[...] += lax.dot_general(
            jnp.concatenate([hot, hot], axis=1), jnp.concatenate(split(spot), axis=1),
            (((1,), (1,)), ((), ())), preferred_element_type=F32,
        )
        return carry

    lax.fori_loop(0, planes * chunks, cells, 0, unroll=4)
    wide_lane = lax.broadcasted_iota(jnp.int32, (high_blocks, 16 * LOW), 1)
    diagonal = jnp.zeros((high_blocks, 16 * LOW), F32)
    for r in range(16):
        inside = (wide_lane >= r * LOW) & (wide_lane < (r + 1) * LOW)
        diagonal = diagonal + jnp.where(inside, acc[r * high_blocks : (r + 1) * high_blocks, :], 0.0)
    folded = diagonal[:, :lanes] + diagonal[:, lanes:]
    for shift in (64, 32, 16):
        folded = folded + pltpu.roll(folded, shift, 1)
    fold_lane = lax.broadcasted_iota(jnp.int32, (8, lanes), 1) // LOW
    fold_row = lax.broadcasted_iota(jnp.int32, (8, lanes), 0)
    own = jnp.concatenate(
        [
            jnp.sum(jnp.where(fold_lane == fold_row, folded[8 * k : 8 * k + 8, :], 0.0), axis=0, keepdims=True)
            for k in range(high_blocks // 8)
        ],
        axis=0,
    )
    grad_out[...] = own
    for copy in spread(grad_out, grad_in, grad_s, grad_r, "slab", n, me):
        copy.wait()
    partial = total_of(own, grad_in, n, me)
    grad_out2[...] = partial
    for copy in spread(grad_out2, grad_in2, grad2_s, grad2_r, "freq", nf, mine):
        copy.wait()
    gradient_ref[...] = total_of(partial, grad_in2, nf, mine)


def write_kernel(forward_ref, adjoint_ref, gradient_ref, forward_out, adjoint_out, gradient_out, sems):
    copies = [
        pltpu.make_async_copy(src, dst, sems.at[k])
        for k, (src, dst) in enumerate([
            (forward_ref, forward_out), (adjoint_ref, adjoint_out), (gradient_ref, gradient_out),
        ])
    ]
    for copy in copies:
        copy.start()
    for copy in copies:
        copy.wait()


def body(source, omega, sigma_blocks, block_ids, rec_owner, rec_edge, observed):
    n, nf = lax.axis_size("slab"), lax.axis_size("freq")
    planes, rows, lanes = block_ids.shape
    blocks = sigma_blocks.shape[0]
    high_blocks = blocks // LOW
    vmem = pl.BlockSpec(memory_space=pltpu.VMEM)
    smem = pl.BlockSpec(memory_space=pltpu.SMEM)
    anywhere = pl.BlockSpec(memory_space=pl.ANY)
    cells_rows = 3 * planes * rows
    wide_planes = planes + 2 * WIDTH
    slots = n * CAP
    field = (2, 3, planes, rows, lanes)
    halo = pltpu.VMEM((SWEEPS, 2, 2, rows, lanes), F32)
    dma = pltpu.SemaphoreType.DMA
    grad_shape = (high_blocks // 8, lanes)
    grad = pltpu.VMEM(grad_shape, F32)
    wide = pltpu.VMEM((wide_planes, rows, lanes), F32)
    operands = (
        source[0], sigma_blocks.reshape(-1, lanes), block_ids, rec_owner.reshape(1, -1), rec_edge.reshape(1, -1),
        observed[0],
    )
    operands = [pltpu.with_memory_space_constraint(a, pltpu.HBM) for a in operands]
    results = pl.pallas_call(
        functools.partial(kernel, n, nf, high_blocks),
        out_shape=(pltpu.VMEM(field, F32), pltpu.VMEM(field, F32), pltpu.VMEM(grad_shape, F32)),
        in_specs=[smem] + [anywhere] * 6,
        out_specs=(vmem, vmem, vmem),
        scratch_shapes=[
            pltpu.VMEM(field, BF16),
            pltpu.VMEM((blocks // lanes, lanes), F32),
            pltpu.VMEM((planes, rows, lanes), jnp.int32),
            pltpu.VMEM((1, lanes), jnp.int32),
            pltpu.VMEM((1, lanes), jnp.int32),
            pltpu.VMEM((2, lanes), F32),
            wide, wide, wide,
            pltpu.VMEM((planes * rows, lanes), F32),
            pltpu.VMEM((2, WIDTH * rows, lanes), F32),
            pltpu.VMEM((8, lanes), F32),
            pltpu.VMEM((8, slots), F32),
            pltpu.VMEM((2, 8, slots), F32),
            pltpu.VMEM((SWEEPS + 1, 2, 3, wide_planes, rows, lanes), F32),
            pltpu.VMEM((2, 3, wide_planes, rows + 8, lanes), F32),
            pltpu.VMEM((2, 3, wide_planes, rows + 8, lanes), F32),
            halo, halo, halo, halo,
            pltpu.VMEM((COUNT, lanes), F32),
            pltpu.VMEM((2, 1, lanes), F32),
            pltpu.VMEM((2, n, 1, lanes), F32),
            pltpu.VMEM((n, 8, lanes), F32),
            grad,
            pltpu.VMEM((n,) + grad_shape, F32),
            grad,
            pltpu.VMEM((nf,) + grad_shape, F32),
            pltpu.VMEM((8, slots, lanes), F32),
            pltpu.VMEM((slots, cells_rows), BF16),
            pltpu.VMEM((3 * wide_planes * rows, slots), BF16),
            pltpu.VMEM((cells_rows, 2 * lanes), BF16),
            pltpu.VMEM((cells_rows, 2 * lanes), BF16),
            pltpu.VMEM((slots, 2 * lanes), BF16),
            pltpu.VMEM((slots, 2 * lanes), BF16),
            pltpu.VMEM((16 * high_blocks, 16 * LOW), F32),
            dma((6,)),
            dma((SWEEPS,)), dma((SWEEPS,)), dma((SWEEPS,)), dma((SWEEPS,)),
            dma((2, n)), dma((2, n)),
            dma((n,)), dma((n,)),
            dma((n,)), dma((n,)),
            dma((nf,)), dma((nf,)),
            dma((4,)), dma((4,)),
            dma((2, nf)), dma((2, nf)),
        ],
        compiler_params=pltpu.CompilerParams(
            collective_id=0, has_side_effects=True, vmem_limit_bytes=50 * 1024 * 1024
        ),
        name="solves",
    )(omega, *operands)
    forward, adjoint, gradient = pl.pallas_call(
        write_kernel,
        out_shape=(
            jax.ShapeDtypeStruct(field, F32), jax.ShapeDtypeStruct(field, F32), jax.ShapeDtypeStruct(grad_shape, F32),
        ),
        in_specs=[anywhere] * 3,
        out_specs=(anywhere,) * 3,
        scratch_shapes=[dma((3,))],
        name="write",
    )(*results)
    return forward[None], adjoint[None], gradient.reshape(blocks)


def solution(mesh):
    return jax.shard_map(
        body,
        mesh=mesh,
        in_specs=(
            P("freq", None, None, "slab", None, None),
            P("freq"),
            P(),
            P("slab", None, None),
            P("slab", None),
            P("slab"),
            P("freq", None, "slab"),
        ),
        out_specs=(
            P("freq", None, None, "slab", None, None),
            P("freq", None, None, "slab", None, None),
            P(),
        ),
        check_vma=False,
    )
```

```python
import functools

import jax
import jax.numpy as jnp
from jax import lax
from jax.experimental import pallas as pl
from jax.experimental.pallas import tpu as pltpu
from jax.sharding import PartitionSpec as P

SWEEPS = 4
EPSILON = 1e-06
LOW = 16
CAP = 32
MESH = pl.DeviceIdType.MESH
F32 = jnp.float32
BF16 = jnp.bfloat16
PAIRS = [(i, j) for j in range(1, SWEEPS + 1) for i in range(j + 1)]
COUNT = sum(1 if i == j else 2 for i, j in PAIRS)
WIDTH = SWEEPS


def split(values):
    high = values.astype(BF16)
    return high, (values - high.astype(F32)).astype(BF16)


def kernel(
    n, nf, high_blocks,
    omega_ref, source_hbm, sigma_hbm, ids_hbm, owner_hbm, edge_hbm, observed_hbm,
    forward_ref, adjoint_ref, gradient_ref,
    source_ref, sigma_ref, ids_ref, owner_ref, edge_ref, observed_ref,
    damp, real_ref, imag_ref, cond, beside, pack_ref, mis_out, mis_in,
    basis, zb, curl, up_out, down_out, low_in, high_in,
    gram_acc, gram_out, gram_in, pack_in, grad_out, grad_in, grad_out2, grad_in2,
    columns, hot, hot_t, field_hi, field_lo, mis_hi, mis_lo, acc,
    local_s, up_s, up_r, down_s, down_r, gram_s, gram_r, pack_s, pack_r, grad_s, grad_r, grad2_s, grad2_r,
    near_s, near_r, share_s, share_r,
):
    me = lax.axis_index("slab")
    mine = lax.axis_index("freq")
    planes, rows, lanes = ids_ref.shape
    first, last = WIDTH, WIDTH + planes - 1
    wide_planes = planes + 2 * WIDTH
    cells_rows = 3 * planes * rows
    slots = n * CAP
    side_rows = WIDTH * rows
    part = side_rows // nf

    loads = [
        pltpu.make_async_copy(src, dst, local_s.at[k])
        for k, (src, dst) in enumerate([
            (ids_hbm, ids_ref), (sigma_hbm, sigma_ref), (source_hbm, source_ref),
            (owner_hbm, owner_ref), (edge_hbm, edge_ref), (observed_hbm, observed_ref),
        ])
    ]
    for copy in loads:
        copy.start()

    barrier = pltpu.get_barrier_semaphore()
    for d in range(1, n):
        pl.semaphore_signal(barrier, inc=1, device_id={"slab": lax.rem(me + d, n)}, device_id_type=MESH)
    for d in range(1, nf):
        pl.semaphore_signal(barrier, inc=1, device_id={"freq": lax.rem(mine + d, nf)}, device_id_type=MESH)

    def spread(src, dst, send, recv, axis, count, position):
        copies = []
        for d in range(1, count):
            copy = pltpu.make_async_remote_copy(
                src_ref=src, dst_ref=dst.at[d], send_sem=send.at[d], recv_sem=recv.at[d],
                device_id={axis: lax.rem(position + d, count)}, device_id_type=MESH,
            )
            copy.start()
            copies.append(copy)
        return copies

    def total_of(own, buffer, count, position):
        buffer[0] = own
        total = jnp.zeros(own.shape, F32)
        for p in range(count):
            total = total + buffer[lax.rem(position - p + count, count)]
        return total

    lane = lax.broadcasted_iota(jnp.int32, (rows, lanes), 1)
    row = lax.broadcasted_iota(jnp.int32, (rows, lanes), 0)
    inner = slice(0, rows)
    above = slice(1, rows + 1)
    shifted = slice(8, rows + 8)
    under = slice(7, rows + 7)

    def f3(v):
        return jnp.where(lane == lanes - 1, 0.0, pltpu.roll(v, lanes - 1, 1)) - v

    def g3(v):
        return jnp.where(lane == 0, 0.0, pltpu.roll(v, 1, 1)) - v

    valid = jnp.where(me > 0, 1.0, 0.0).astype(F32)
    omega = omega_ref[0]

    def factors(x, at, damping):
        inverse = 1.0 / (16.0 + damping * damping)
        damp[x, at] = damping
        real_ref[x, at] = 4.0 * inverse
        imag_ref[x, at] = damping * inverse

    def pad(x, carry):
        for c in range(2):
            for comp in range(3):
                zb[c, comp, x, rows : rows + 8] = jnp.zeros((8, lanes), F32)
                curl[c, comp, x, 0:8] = jnp.zeros((8, lanes), F32)
        return carry

    lax.fori_loop(0, wide_planes, pad, 0)

    chunks = rows // 16
    loads[0].wait()
    loads[1].wait()
    loads[2].wait()
    tables = [jnp.broadcast_to(sigma_ref[k : k + 1, :], (8, lanes)) for k in range(sigma_ref.shape[0])]

    def begin(x, y):
        for half in range(2):
            at = pl.ds(pl.multiple_of(y + 8 * half, 8), 8)
            ids = ids_ref[x, at, :]
            low, high = ids & (lanes - 1), ids >> 7
            value = jnp.take_along_axis(tables[0], low, axis=1)
            for k in range(1, len(tables)):
                value = jnp.where(high == k, jnp.take_along_axis(tables[k], low, axis=1), value)
            cond[pl.ds(pl.multiple_of(x * rows + y + 8 * half, 8), 8), :] = value
            factors(x + first, at, omega * value)
        at = pl.ds(y, 16)
        for c in range(2):
            for comp in range(3):
                basis[0, c, comp, x + first, at] = source_ref[c, comp, x, at, :].astype(F32)

    def begin_ends(i, carry):
        begin(i // chunks * (planes - 1), pl.multiple_of(i % chunks * 16, 16))
        return carry

    def begin_inner(i, carry):
        begin(i // chunks + 1, pl.multiple_of(i % chunks * 16, 16))
        return carry

    lax.fori_loop(0, 2 * chunks, begin_ends, 0, unroll=4)

    def beside_copy(side):
        start, to = (planes * rows - side_rows, me + 1) if side == 0 else (0, me + n - 1)
        return pltpu.make_async_remote_copy(
            src_ref=cond.at[pl.ds(start + mine * part, part)], dst_ref=beside.at[side, pl.ds(mine * part, part)],
            send_sem=near_s.at[side], recv_sem=near_r.at[side], device_id={"slab": lax.rem(to, n)},
            device_id_type=MESH,
        )

    def share_copies(side):
        at = pl.ds(mine * part, part)
        return [
            pltpu.make_async_remote_copy(
                src_ref=beside.at[side, at], dst_ref=beside.at[side, at], send_sem=share_s.at[side, d],
                recv_sem=share_r.at[side, d], device_id={"freq": lax.rem(mine + d, nf)}, device_id_type=MESH,
            )
            for d in range(1, nf)
        ]

    def misfit_copy(side):
        to = me + 1 if side == 0 else me + n - 1
        return pltpu.make_async_remote_copy(
            src_ref=mis_out, dst_ref=mis_in.at[side], send_sem=near_s.at[2 + side],
            recv_sem=near_r.at[2 + side], device_id={"slab": lax.rem(to, n)}, device_id_type=MESH,
        )

    def up_copy(slot):
        return pltpu.make_async_remote_copy(
            src_ref=up_out.at[slot], dst_ref=low_in.at[slot], send_sem=up_s.at[slot],
            recv_sem=up_r.at[slot], device_id={"slab": lax.rem(me + 1, n)}, device_id_type=MESH,
        )

    def down_copy(slot):
        return pltpu.make_async_remote_copy(
            src_ref=down_out.at[slot], dst_ref=high_in.at[slot], send_sem=down_s.at[slot],
            recv_sem=down_r.at[slot], device_id={"slab": lax.rem(me + n - 1, n)}, device_id_type=MESH,
        )

    def precondition(t, x):
        mr, mi = real_ref[x], imag_ref[x]
        for comp in range(3):
            br, bi = basis[t, 0, comp, x], basis[t, 1, comp, x]
            zb[0, comp, x, inner] = mr * br + mi * bi
            zb[1, comp, x, inner] = mr * bi - mi * br

    def curls(x, ahead=None):
        for c in range(2):
            e1, e2, e3 = zb[c, 0, x, inner], zb[c, 1, x, inner], zb[c, 2, x, inner]
            if ahead is None:
                e2n, e3n = zb[c, 1, x + 1, inner], zb[c, 2, x + 1, inner]
            else:
                e2n, e3n = ahead[c, 0], ahead[c, 1]
            curl[c, 0, x, shifted] = (zb[c, 2, x, above] - e3) - f3(e2)
            curl[c, 1, x, shifted] = f3(e1) - (e3n - e3)
            curl[c, 2, x, shifted] = (e2n - e2) - (zb[c, 0, x, above] - e1)

    def images(t, x, keep=None):
        damping = damp[x]
        for c in range(2):
            b1, b2, b3 = curl[c, 0, x, shifted], curl[c, 1, x, shifted], curl[c, 2, x, shifted]
            b2p, b3p = curl[c, 1, x - 1, shifted], curl[c, 2, x - 1, shifted]
            if keep is not None:
                b2p, b3p = b2p * keep, b3p * keep
            parts = (
                g3(b2) - (curl[c, 2, x, under] - b3),
                (b3p - b3) - g3(b1),
                (curl[c, 0, x, under] - b1) - (b2p - b2),
            )
            for comp in range(3):
                turned = damping * zb[1 - c, comp, x, inner]
                basis[t + 1, c, comp, x] = parts[comp] - turned if c == 0 else parts[comp] + turned

    def sweep(t, lo, hi, masked):
        for k in range(4):
            precondition(t, lo + k)
        curls(lo)
        curls(lo + 1)

        def keep_of(x):
            if not masked:
                return None
            return jnp.where((x == first) & (me == 0), 0.0, 1.0).astype(F32)

        def step(x, carry):
            images(t, x, keep_of(x))
            curls(x + 1)
            precondition(t, x + 3)
            return carry

        lax.fori_loop(lo + 1, hi - 2, step, 0)
        images(t, hi - 2)
        curls(hi - 1)
        images(t, hi - 1)

    def send_down(t):
        precondition(t, first)
        for c in range(2):
            down_out[t, c, 0] = zb[c, 1, first, inner]
            down_out[t, c, 1] = zb[c, 2, first, inner]

        @pl.when(me > 0)
        def _():
            down_copy(t).start()

    def send_up(t):
        precondition(t, last)
        for c in range(2):
            e1 = zb[c, 0, last, inner]
            up_out[t, c, 0] = f3(e1) + zb[c, 2, last, inner]
            up_out[t, c, 1] = (zb[c, 0, last, above] - e1) + zb[c, 1, last, inner]

        @pl.when(me < n - 1)
        def _():
            up_copy(t).start()

    def forward_sweep(t, meanwhile):
        sweep(t, first, last, False)
        meanwhile()

        @pl.when(me > 0)
        def _():
            up_copy(t).wait_recv()
            down_copy(t).wait_send()

        @pl.when(me == 0)
        def _():
            low_in[t] = jnp.zeros(low_in.shape[1:], F32)

        for c in range(2):
            curl[c, 1, first - 1, shifted] = (low_in[t, c, 0] - zb[c, 2, first, inner]) * valid
            curl[c, 2, first - 1, shifted] = (zb[c, 1, first, inner] - low_in[t, c, 1]) * valid
        images(t, first)
        if t < SWEEPS - 1:
            send_down(t + 1)

        @pl.when(me < n - 1)
        def _():
            down_copy(t).wait_recv()
            up_copy(t).wait_send()

        @pl.when(me == n - 1)
        def _():
            high_in[t] = jnp.zeros(high_in.shape[1:], F32)

        curls(last, high_in.at[t])
        images(t, last)
        if t < SWEEPS - 1:
            send_up(t + 1)

    per = rows // 8

    def pair_sums(j_):
        width = 2 * j_ + 1

        def products(i, sums):
            x, y = i // per + first, pl.multiple_of(i % per * 8, 8)
            sums = list(sums)
            for comp in range(3):
                re = [basis[k, 0, comp, x, pl.ds(y, 8), :] for k in range(j_ + 1)]
                im = [basis[k, 1, comp, x, pl.ds(y, 8), :] for k in range(j_ + 1)]
                for i_ in range(j_ + 1):
                    sums[2 * i_] = sums[2 * i_] + (re[i_] * re[j_] + im[i_] * im[j_])
                    if i_ != j_:
                        sums[2 * i_ + 1] = sums[2 * i_ + 1] + (re[i_] * im[j_] - im[i_] * re[j_])
            return tuple(sums)

        zero = jnp.zeros((8, lanes), F32)
        sums = lax.fori_loop(0, planes * per, products, (zero,) * width, unroll=2)
        for k in range(width):
            at = j_ * j_ - 1 + k
            gram_acc[at : at + 1, :] = jnp.sum(sums[k], axis=0, keepdims=True)

    gram_lane = lax.broadcasted_iota(jnp.int32, (COUNT, lanes), 1)
    gram_row = lax.broadcasted_iota(jnp.int32, (COUNT, lanes), 0)
    diagonal_of = gram_lane == gram_row

    def gram_start(which):
        local = jnp.sum(gram_acc[...], axis=1, keepdims=True)
        gram_out[which] = jnp.sum(jnp.where(diagonal_of, local, 0.0), axis=0, keepdims=True)
        return spread(gram_out.at[which], gram_in.at[which], gram_s.at[which], gram_r.at[which], "slab", n, me)

    def coefficients(which):
        total = total_of(gram_out[which], gram_in.at[which], n, me)
        total = jnp.sum(jnp.where(diagonal_of, total, 0.0), axis=1, keepdims=True)
        total = jnp.broadcast_to(total, (COUNT, lanes))
        gram, at = {}, 0
        for i, j in PAIRS:
            re = total[at : at + 1, :]
            at += 1
            im = jnp.zeros_like(re)
            if i != j:
                im = total[at : at + 1, :]
                at += 1
            gram[i, j] = (re, im)
            gram[j, i] = (re, -im)
        one = jnp.ones((1, lanes), F32)
        none = jnp.zeros((1, lanes), F32)

        def times(a, b):
            return a[0] * b[0] - a[1] * b[1], a[0] * b[1] + a[1] * b[0]

        poly = [(one, none)]
        coef = [(none, none) for _ in range(SWEEPS)]
        for k in range(SWEEPS):
            up = (none, none)
            below = none
            for i in range(k + 1):
                conj = (poly[i][0], -poly[i][1])
                for j in range(k + 1):
                    both = times(conj, poly[j])
                    term = times(both, gram[i + 1, j])
                    up = (up[0] + term[0], up[1] + term[1])
                    below = below + times(both, gram[i + 1, j + 1])[0]
            below = below + EPSILON
            step = (up[0] / below, up[1] / below)
            moved = [times(step, p) for p in poly]
            for i in range(k + 1):
                coef[i] = (coef[i][0] + moved[i][0], coef[i][1] + moved[i][1])
            grown = poly + [(none, none)]
            for i in range(k + 1):
                grown[i + 1] = (grown[i + 1][0] - moved[i][0], grown[i + 1][1] - moved[i][1])
            poly = grown

        return [(jnp.broadcast_to(a, (16, lanes)), jnp.broadcast_to(b, (16, lanes))) for a, b in coef]

    def combine(wide, out_ref, keep_parts):
        def step(i, carry):
            x, y = i // chunks, pl.multiple_of(i % chunks * 16, 16)
            at = pl.ds(y, 16)
            mr, mi = real_ref[x + first, at, :], imag_ref[x + first, at, :]
            for comp in range(3):
                sr = jnp.zeros((16, lanes), F32)
                si = jnp.zeros((16, lanes), F32)
                for k in range(SWEEPS):
                    br, bi = basis[k, 0, comp, x + first, at, :], basis[k, 1, comp, x + first, at, :]
                    sr = sr + (wide[k][0] * br - wide[k][1] * bi)
                    si = si + (wide[k][0] * bi + wide[k][1] * br)
                for c, value in enumerate((mr * sr + mi * si, mr * si - mi * sr)):
                    out_ref[c, comp, x, at, :] = value
                    if keep_parts:
                        here = pl.ds(pl.multiple_of((comp * planes + x) * rows + y, 16), 16)
                        hi, lo = split(value)
                        field_hi[here, c * lanes : (c + 1) * lanes] = hi
                        field_lo[here, c * lanes : (c + 1) * lanes] = lo
            return carry

        lax.fori_loop(0, planes * chunks, step, 0, unroll=2)

    packs = [
        pltpu.make_async_remote_copy(
            src_ref=pack_ref, dst_ref=pack_in.at[me], send_sem=pack_s.at[d], recv_sem=pack_r.at[d],
            device_id={"slab": lax.rem(me + d, n)}, device_id_type=MESH,
        )
        for d in range(1, n)
    ]

    cap_row = lax.broadcasted_iota(jnp.int32, (CAP, lanes), 0).astype(F32)
    lane_sq = lax.broadcasted_iota(jnp.int32, (lanes, lanes), 1).astype(F32)
    row_sq = lax.broadcasted_iota(jnp.int32, (lanes, lanes), 0).astype(F32)
    earlier = jnp.where(row_sq < lane_sq, 1.0, 0.0).astype(F32)
    self_id = me.astype(F32)

    def compact(p, carry):
        pack = pack_in[p]
        owner, number, spot = pack[0:1, :], pack[1:2, :], pack[2:3, :]
        third = jnp.where(number >= 2.0 * planes * rows, 2.0, jnp.where(number >= 1.0 * planes * rows, 1.0, 0.0))
        inside = number - third * float(planes * rows)
        upper = inside - float((planes - WIDTH) * rows)
        low_place = jnp.where(upper >= 0.0, third * float(side_rows) + upper, -1.0)
        high_place = jnp.where(inside < float(side_rows), third * float(side_rows) + inside, -1.0)
        owned = [jnp.where(owner == self_id + shift, 1.0, 0.0) for shift in (0.0, -1.0, 1.0)]
        owned = jnp.concatenate(owned + [jnp.zeros((5, lanes), F32)], axis=0)
        rank = jnp.dot(owned, earlier, preferred_element_type=F32)
        at = pl.ds(pl.multiple_of(p * CAP, CAP), CAP)
        wanted = (
            (0, 0, number + 1.0), (1, 0, spot), (2, 0, pack[3:4, :]), (3, 0, pack[4:5, :]),
            (4, 1, low_place + 1.0), (5, 1, spot), (6, 2, high_place + 1.0), (7, 2, spot),
        )
        for k, target, value in wanted:
            hit = (cap_row == rank[target : target + 1, :]) & (owned[target : target + 1, :] > 0.0)
            found = jnp.sum(jnp.where(hit, value, 0.0), axis=1, keepdims=True)
            columns[k, at, :] = jnp.broadcast_to(found, (CAP, lanes))
        return carry

    def picks(p, carry):
        at = pl.ds(pl.multiple_of(p * CAP, CAP), CAP)
        place = columns[0, at, :] - 1.0
        for b in range(cells_rows // lanes):
            hot[at, b * lanes : (b + 1) * lanes] = jnp.where(
                lane_sq[:CAP] == place - float(b * lanes), 1.0, 0.0
            ).astype(BF16)
        return carry

    def placings(start, k, count):
        for q in range(slots // lanes):
            spot = columns[k, q * lanes : (q + 1) * lanes, :].T - 1.0

            def fill(b, carry):
                base = pl.multiple_of(b * lanes, lanes)
                hot_t[pl.ds(start + base, lanes), q * lanes : (q + 1) * lanes] = jnp.where(
                    row_sq + base.astype(F32) == spot, 1.0, 0.0
                ).astype(BF16)
                return carry

            lax.fori_loop(0, count // lanes, fill, 0)

    def spread_values(k, re, im):
        here = lane_of_slot == columns[k]
        for part_, value in enumerate((re, im)):
            hi, lo = split(jnp.where(here, value, 0.0))
            mis_hi[:, part_ * lanes : (part_ + 1) * lanes] = hi
            mis_lo[:, part_ * lanes : (part_ + 1) * lanes] = lo

    def add_source(start, x0, count, group):
        for comp in range(3):
            for x in range(0, count, group):
                begin_ = start + (comp * count + x) * rows
                block = hot_t[begin_ : begin_ + group * rows, :]
                added = jnp.dot(block, mis_hi[...], preferred_element_type=F32)
                added = added + jnp.dot(block, mis_lo[...], preferred_element_type=F32)
                for c in range(2):
                    basis[0, c, comp, x0 + x : x0 + x + group] = added[:, c * lanes : (c + 1) * lanes].reshape(
                        group, rows, lanes
                    )

    lane_of_slot = lax.broadcasted_iota(jnp.int32, (slots, lanes), 1).astype(F32)

    pl.semaphore_wait(barrier, n + nf - 2)
    send_down(0)
    send_up(0)
    loads[3].wait()
    loads[4].wait()
    loads[5].wait()
    edge = edge_ref[...]
    pack_ref[...] = jnp.concatenate(
        [
            owner_ref[...].astype(F32), (edge >> 7).astype(F32), (edge & 127).astype(F32), observed_ref[...],
            jnp.zeros((3, lanes), F32),
        ],
        axis=0,
    )
    for copy in packs:
        copy.start()
    pack_in[me] = pack_ref[...]
    lax.fori_loop(0, (planes - 2) * chunks, begin_inner, 0, unroll=4)

    def while_first():
        pair_sums(1)
        for copy in packs:
            copy.wait()
        lax.fori_loop(0, n, compact, 0)

    def while_second():
        pair_sums(2)
        lax.fori_loop(0, n, picks, 0)

    def while_third():
        pair_sums(3)
        placings(0, 0, cells_rows)
        placings(cells_rows, 4, 3 * side_rows)
        placings(cells_rows + 3 * side_rows, 6, 3 * side_rows)

    forward_sweep(0, lambda: None)
    forward_sweep(1, while_first)
    forward_sweep(2, while_second)
    forward_sweep(3, while_third)
    pair_sums(SWEEPS)
    for copy in gram_start(0):
        copy.wait()

    @pl.when(me > 0)
    def _():
        beside_copy(1).start()

    @pl.when(me < n - 1)
    def _():
        beside_copy(0).start()

    combine(coefficients(0), forward_ref, True)

    picked = jnp.dot(hot[...], field_hi[...], preferred_element_type=F32)
    picked = picked + jnp.dot(hot[...], field_lo[...], preferred_element_type=F32)
    here = lane_of_slot == columns[1]
    re = jnp.sum(jnp.where(here, picked[:, :lanes], 0.0), axis=1, keepdims=True) - columns[2]
    im = columns[3] - jnp.sum(jnp.where(here, picked[:, lanes:], 0.0), axis=1, keepdims=True)
    both = jnp.where(lane_of_slot == 0.0, re, jnp.where(lane_of_slot == 1.0, im, 0.0))
    mis_out[...] = both.T[0:8, :]

    @pl.when(me > 0)
    def _():
        misfit_copy(1).start()
        beside_copy(0).wait_recv()
        for copy in share_copies(0):
            copy.start()

    @pl.when(me < n - 1)
    def _():
        misfit_copy(0).start()
        beside_copy(1).wait_recv()
        for copy in share_copies(1):
            copy.start()

    spread_values(1, re, im)
    add_source(0, first, planes, 4)

    for side, there in enumerate((me > 0, me < n - 1)):
        start = 0 if side == 0 else last + 1

        @pl.when(there)
        def _(side=side, start=start):
            beside_copy(1 - side).wait_send()
            for copy in share_copies(side):
                copy.wait()
            for k in range(WIDTH):
                factors(start + k, inner, omega * beside[side, k * rows : (k + 1) * rows, :])
            misfit_copy(side).wait_recv()
            misfit_copy(1 - side).wait_send()

        @pl.when(jnp.logical_not(there))
        def _(side=side, start=start):
            mis_in[side] = jnp.zeros(mis_in.shape[1:], F32)
            for k in range(WIDTH):
                damp[start + k] = jnp.zeros((rows, lanes), F32)
                real_ref[start + k] = jnp.zeros((rows, lanes), F32)
                imag_ref[start + k] = jnp.zeros((rows, lanes), F32)

        column = jnp.concatenate([mis_in[side]] * (lanes // 8), axis=0).T
        spread_values(5 + 2 * side, column[:, 0:1], column[:, 1:2])
        add_source(cells_rows + side * 3 * side_rows, start, WIDTH, WIDTH)

    for t in range(SWEEPS):
        sweep(t, t, wide_planes - t - 1, True)
        if t:
            pair_sums(t)
    pair_sums(SWEEPS)
    for copy in gram_start(1):
        copy.wait()
    combine(coefficients(1), adjoint_ref, False)

    high_iota = lax.broadcasted_iota(jnp.int32, (high_blocks, lanes), 0)
    low_iota = lax.broadcasted_iota(jnp.int32, (LOW, lanes), 0)
    acc[...] = jnp.zeros(acc.shape, F32)

    def cells(i, carry):
        x, y = i // chunks, pl.multiple_of(i % chunks * 16, 16)
        value = jnp.zeros((16, lanes), F32)
        for comp in range(3):
            fr, fi = forward_ref[0, comp, x, pl.ds(y, 16), :], forward_ref[1, comp, x, pl.ds(y, 16), :]
            ar, ai = adjoint_ref[0, comp, x, pl.ds(y, 16), :], adjoint_ref[1, comp, x, pl.ds(y, 16), :]
            value = value + (ar * fi + ai * fr)
        value = omega * value
        ids = ids_ref[x, pl.ds(y, 16), :]
        high, low = ids >> 4, ids & (LOW - 1)
        hot = jnp.concatenate(
            [jnp.where(high[r : r + 1, :] == high_iota, 1.0, 0.0) for r in range(16)], axis=0
        ).astype(BF16)
        spot = jnp.concatenate(
            [jnp.where(low[r : r + 1, :] == low_iota, value[r : r + 1, :], 0.0) for r in range(16)], axis=0
        )
        acc[...] += lax.dot_general(
            jnp.concatenate([hot, hot], axis=1), jnp.concatenate(split(spot), axis=1),
            (((1,), (1,)), ((), ())), preferred_element_type=F32,
        )
        return carry

    lax.fori_loop(0, planes * chunks, cells, 0, unroll=4)
    wide_lane = lax.broadcasted_iota(jnp.int32, (high_blocks, 16 * LOW), 1)
    diagonal = jnp.zeros((high_blocks, 16 * LOW), F32)
    for r in range(16):
        inside = (wide_lane >= r * LOW) & (wide_lane < (r + 1) * LOW)
        diagonal = diagonal + jnp.where(inside, acc[r * high_blocks : (r + 1) * high_blocks, :], 0.0)
    folded = diagonal[:, :lanes] + diagonal[:, lanes:]
    for shift in (64, 32, 16):
        folded = folded + pltpu.roll(folded, shift, 1)
    fold_lane = lax.broadcasted_iota(jnp.int32, (8, lanes), 1) // LOW
    fold_row = lax.broadcasted_iota(jnp.int32, (8, lanes), 0)
    own = jnp.concatenate(
        [
            jnp.sum(jnp.where(fold_lane == fold_row, folded[8 * k : 8 * k + 8, :], 0.0), axis=0, keepdims=True)
            for k in range(high_blocks // 8)
        ],
        axis=0,
    )
    grad_out[...] = own
    for copy in spread(grad_out, grad_in, grad_s, grad_r, "slab", n, me):
        copy.wait()
    partial = total_of(own, grad_in, n, me)
    grad_out2[...] = partial
    for copy in spread(grad_out2, grad_in2, grad2_s, grad2_r, "freq", nf, mine):
        copy.wait()
    gradient_ref[...] = total_of(partial, grad_in2, nf, mine)


def write_kernel(forward_ref, adjoint_ref, gradient_ref, forward_out, adjoint_out, gradient_out, sems):
    copies = [
        pltpu.make_async_copy(src, dst, sems.at[k])
        for k, (src, dst) in enumerate([
            (forward_ref, forward_out), (adjoint_ref, adjoint_out), (gradient_ref, gradient_out),
        ])
    ]
    for copy in copies:
        copy.start()
    for copy in copies:
        copy.wait()


def body(source, omega, sigma_blocks, block_ids, rec_owner, rec_edge, observed):
    n, nf = lax.axis_size("slab"), lax.axis_size("freq")
    planes, rows, lanes = block_ids.shape
    blocks = sigma_blocks.shape[0]
    high_blocks = blocks // LOW
    vmem = pl.BlockSpec(memory_space=pltpu.VMEM)
    smem = pl.BlockSpec(memory_space=pltpu.SMEM)
    anywhere = pl.BlockSpec(memory_space=pl.ANY)
    cells_rows = 3 * planes * rows
    wide_planes = planes + 2 * WIDTH
    slots = n * CAP
    field = (2, 3, planes, rows, lanes)
    halo = pltpu.VMEM((SWEEPS, 2, 2, rows, lanes), F32)
    dma = pltpu.SemaphoreType.DMA
    grad_shape = (high_blocks // 8, lanes)
    grad = pltpu.VMEM(grad_shape, F32)
    wide = pltpu.VMEM((wide_planes, rows, lanes), F32)
    operands = (
        source[0], sigma_blocks.reshape(-1, lanes), block_ids, rec_owner.reshape(1, -1), rec_edge.reshape(1, -1),
        observed[0],
    )
    operands = [pltpu.with_memory_space_constraint(a, pltpu.HBM) for a in operands]
    results = pl.pallas_call(
        functools.partial(kernel, n, nf, high_blocks),
        out_shape=(pltpu.VMEM(field, F32), pltpu.VMEM(field, F32), pltpu.VMEM(grad_shape, F32)),
        in_specs=[smem] + [anywhere] * 6,
        out_specs=(vmem, vmem, vmem),
        scratch_shapes=[
            pltpu.VMEM(field, BF16),
            pltpu.VMEM((blocks // lanes, lanes), F32),
            pltpu.VMEM((planes, rows, lanes), jnp.int32),
            pltpu.VMEM((1, lanes), jnp.int32),
            pltpu.VMEM((1, lanes), jnp.int32),
            pltpu.VMEM((2, lanes), F32),
            wide, wide, wide,
            pltpu.VMEM((planes * rows, lanes), F32),
            pltpu.VMEM((2, WIDTH * rows, lanes), F32),
            pltpu.VMEM((8, lanes), F32),
            pltpu.VMEM((8, slots), F32),
            pltpu.VMEM((2, 8, slots), F32),
            pltpu.VMEM((SWEEPS + 1, 2, 3, wide_planes, rows, lanes), F32),
            pltpu.VMEM((2, 3, wide_planes, rows + 8, lanes), F32),
            pltpu.VMEM((2, 3, wide_planes, rows + 8, lanes), F32),
            halo, halo, halo, halo,
            pltpu.VMEM((COUNT, lanes), F32),
            pltpu.VMEM((2, 1, lanes), F32),
            pltpu.VMEM((2, n, 1, lanes), F32),
            pltpu.VMEM((n, 8, lanes), F32),
            grad,
            pltpu.VMEM((n,) + grad_shape, F32),
            grad,
            pltpu.VMEM((nf,) + grad_shape, F32),
            pltpu.VMEM((8, slots, lanes), F32),
            pltpu.VMEM((slots, cells_rows), BF16),
            pltpu.VMEM((3 * wide_planes * rows, slots), BF16),
            pltpu.VMEM((cells_rows, 2 * lanes), BF16),
            pltpu.VMEM((cells_rows, 2 * lanes), BF16),
            pltpu.VMEM((slots, 2 * lanes), BF16),
            pltpu.VMEM((slots, 2 * lanes), BF16),
            pltpu.VMEM((16 * high_blocks, 16 * LOW), F32),
            dma((6,)),
            dma((SWEEPS,)), dma((SWEEPS,)), dma((SWEEPS,)), dma((SWEEPS,)),
            dma((2, n)), dma((2, n)),
            dma((n,)), dma((n,)),
            dma((n,)), dma((n,)),
            dma((nf,)), dma((nf,)),
            dma((4,)), dma((4,)),
            dma((2, nf)), dma((2, nf)),
        ],
        compiler_params=pltpu.CompilerParams(
            collective_id=0, has_side_effects=True, vmem_limit_bytes=50 * 1024 * 1024
        ),
        name="solves",
    )(omega, *operands)
    forward, adjoint, gradient = pl.pallas_call(
        write_kernel,
        out_shape=(
            jax.ShapeDtypeStruct(field, F32), jax.ShapeDtypeStruct(field, F32), jax.ShapeDtypeStruct(grad_shape, F32),
        ),
        in_specs=[vmem] * 3,
        out_specs=(anywhere,) * 3,
        scratch_shapes=[dma((3,))],
        name="write",
    )(*[pltpu.with_memory_space_constraint(a, pltpu.VMEM) for a in results])
    return forward[None], adjoint[None], gradient.reshape(blocks)


def solution(mesh):
    return jax.shard_map(
        body,
        mesh=mesh,
        in_specs=(
            P("freq", None, None, "slab", None, None),
            P("freq"),
            P(),
            P("slab", None, None),
            P("slab", None),
            P("slab"),
            P("freq", None, "slab"),
        ),
        out_specs=(
            P("freq", None, None, "slab", None, None),
            P("freq", None, None, "slab", None, None),
            P(),
        ),
        check_vma=False,
    )
```

```python
import functools

import jax
import jax.numpy as jnp
from jax import lax
from jax.experimental import pallas as pl
from jax.experimental.pallas import tpu as pltpu
from jax.sharding import PartitionSpec as P

SWEEPS = 4
EPSILON = 1e-06
LOW = 16
CAP = 32
MESH = pl.DeviceIdType.MESH
F32 = jnp.float32
BF16 = jnp.bfloat16
PAIRS = [(i, j) for j in range(1, SWEEPS + 1) for i in range(j + 1)]
COUNT = sum(1 if i == j else 2 for i, j in PAIRS)
WIDTH = SWEEPS


def split(values):
    high = values.astype(BF16)
    return high, (values - high.astype(F32)).astype(BF16)


def kernel(
    n, nf, high_blocks,
    omega_ref, source_hbm, sigma_hbm, ids_hbm, owner_hbm, edge_hbm, observed_hbm,
    forward_ref, adjoint_ref, gradient_ref,
    source_ref, sigma_ref, ids_ref, owner_ref, edge_ref, observed_ref,
    damp, real_ref, imag_ref, cond, beside, pack_ref, mis_out, mis_in,
    basis, zb, curl, up_out, down_out, low_in, high_in,
    gram_acc, gram_out, gram_in, pack_in, grad_out, grad_in,
    columns, hot, hot_t, field_hi, field_lo, mis_hi, mis_lo, acc,
    local_s, up_s, up_r, down_s, down_r, gram_s, gram_r, pack_s, pack_r, grad_s, grad_r,
    near_s, near_r, share_s, share_r,
):
    me = lax.axis_index("slab")
    mine = lax.axis_index("freq")
    planes, rows, lanes = ids_ref.shape
    first, last = WIDTH, WIDTH + planes - 1
    wide_planes = planes + 2 * WIDTH
    cells_rows = 3 * planes * rows
    slots = n * CAP
    side_rows = WIDTH * rows
    part = side_rows // nf

    loads = [
        pltpu.make_async_copy(src, dst, local_s.at[k])
        for k, (src, dst) in enumerate([
            (ids_hbm, ids_ref), (sigma_hbm, sigma_ref), (source_hbm, source_ref),
            (owner_hbm, owner_ref), (edge_hbm, edge_ref), (observed_hbm, observed_ref),
        ])
    ]
    for copy in loads:
        copy.start()

    barrier = pltpu.get_barrier_semaphore()
    for k in range(1, n * nf):
        pl.semaphore_signal(
            barrier, inc=1, device_id={"slab": lax.rem(me + k // nf, n), "freq": lax.rem(mine + k % nf, nf)},
            device_id_type=MESH,
        )

    def spread(src, dst, send, recv, axis, count, position):
        copies = []
        for d in range(1, count):
            copy = pltpu.make_async_remote_copy(
                src_ref=src, dst_ref=dst.at[d], send_sem=send.at[d], recv_sem=recv.at[d],
                device_id={axis: lax.rem(position + d, count)}, device_id_type=MESH,
            )
            copy.start()
            copies.append(copy)
        return copies

    def total_of(own, buffer, count, position):
        buffer[0] = own
        total = jnp.zeros(own.shape, F32)
        for p in range(count):
            total = total + buffer[lax.rem(position - p + count, count)]
        return total

    lane = lax.broadcasted_iota(jnp.int32, (rows, lanes), 1)
    inner = slice(0, rows)
    above = slice(1, rows + 1)
    shifted = slice(8, rows + 8)
    under = slice(7, rows + 7)

    def f3(v):
        return jnp.where(lane[: v.shape[0]] == lanes - 1, 0.0, pltpu.roll(v, lanes - 1, 1)) - v

    def g3(v):
        return jnp.where(lane[: v.shape[0]] == 0, 0.0, pltpu.roll(v, 1, 1)) - v

    valid = jnp.where(me > 0, 1.0, 0.0).astype(F32)
    omega = omega_ref[0]

    def factors(x, at, damping):
        inverse = 1.0 / (16.0 + damping * damping)
        damp[x, at] = damping
        real_ref[x, at] = 4.0 * inverse
        imag_ref[x, at] = damping * inverse

    def pad(x, carry):
        for c in range(2):
            for comp in range(3):
                zb[c, comp, x, rows : rows + 8] = jnp.zeros((8, lanes), F32)
                curl[c, comp, x, 0:8] = jnp.zeros((8, lanes), F32)
        return carry

    lax.fori_loop(0, wide_planes, pad, 0)

    chunks = rows // 16
    loads[0].wait()
    loads[1].wait()
    loads[2].wait()
    tables = [jnp.broadcast_to(sigma_ref[k : k + 1, :], (8, lanes)) for k in range(sigma_ref.shape[0])]

    def begin(x, y):
        for half in range(2):
            at = pl.ds(pl.multiple_of(y + 8 * half, 8), 8)
            ids = ids_ref[x, at, :]
            low, high = ids & (lanes - 1), ids >> 7
            value = jnp.take_along_axis(tables[0], low, axis=1)
            for k in range(1, len(tables)):
                value = jnp.where(high == k, jnp.take_along_axis(tables[k], low, axis=1), value)
            cond[pl.ds(pl.multiple_of(x * rows + y + 8 * half, 8), 8), :] = value
            factors(x + first, at, omega * value)
        at = pl.ds(y, 16)
        for c in range(2):
            for comp in range(3):
                basis[0, c, comp, x + first, at] = source_ref[c, comp, x, at, :].astype(F32)

    def begin_ends(i, carry):
        begin(i // chunks * (planes - 1), pl.multiple_of(i % chunks * 16, 16))
        return carry

    def begin_inner(i, carry):
        begin(i // chunks + 1, pl.multiple_of(i % chunks * 16, 16))
        return carry

    lax.fori_loop(0, 2 * chunks, begin_ends, 0, unroll=4)

    def beside_copy(side):
        start, to = (planes * rows - side_rows, me + 1) if side == 0 else (0, me + n - 1)
        return pltpu.make_async_remote_copy(
            src_ref=cond.at[pl.ds(start + mine * part, part)], dst_ref=beside.at[side, pl.ds(mine * part, part)],
            send_sem=near_s.at[side], recv_sem=near_r.at[side], device_id={"slab": lax.rem(to, n)},
            device_id_type=MESH,
        )

    def share_copies(side):
        at = pl.ds(mine * part, part)
        return [
            pltpu.make_async_remote_copy(
                src_ref=beside.at[side, at], dst_ref=beside.at[side, at], send_sem=share_s.at[side, d],
                recv_sem=share_r.at[side, d], device_id={"freq": lax.rem(mine + d, nf)}, device_id_type=MESH,
            )
            for d in range(1, nf)
        ]

    def misfit_copy(side):
        to = me + 1 if side == 0 else me + n - 1
        return pltpu.make_async_remote_copy(
            src_ref=mis_out, dst_ref=mis_in.at[side], send_sem=near_s.at[2 + side],
            recv_sem=near_r.at[2 + side], device_id={"slab": lax.rem(to, n)}, device_id_type=MESH,
        )

    def cut_of(t):
        return rows // 8 // 2 * 8 + 8 * (1 - t)

    def rows_of(t, half):
        return (0, cut_of(t)) if half == 0 else (cut_of(t), rows)

    def span(t, half):
        lo, hi = rows_of(t, half)
        return pl.ds(4 * lo, 4 * (hi - lo))

    def place_of(t, half, c, k):
        lo, hi = rows_of(t, half)
        start = 4 * lo + (2 * c + k) * (hi - lo)
        return slice(start, start + hi - lo)

    def up_copy(t, half):
        at = span(t, half)
        return pltpu.make_async_remote_copy(
            src_ref=up_out.at[t, at], dst_ref=low_in.at[t, at], send_sem=up_s.at[t, half],
            recv_sem=up_r.at[t, half], device_id={"slab": lax.rem(me + 1, n)}, device_id_type=MESH,
        )

    def down_copy(t, half):
        at = span(t, half)
        return pltpu.make_async_remote_copy(
            src_ref=down_out.at[t, at], dst_ref=high_in.at[t, at], send_sem=down_s.at[t, half],
            recv_sem=down_r.at[t, half], device_id={"slab": lax.rem(me + n - 1, n)}, device_id_type=MESH,
        )

    def precondition(t, x, at=inner):
        mr, mi = real_ref[x, at], imag_ref[x, at]
        for comp in range(3):
            br, bi = basis[t, 0, comp, x, at], basis[t, 1, comp, x, at]
            zb[0, comp, x, at] = mr * br + mi * bi
            zb[1, comp, x, at] = mr * bi - mi * br

    def curls(x):
        for c in range(2):
            e1, e2, e3 = zb[c, 0, x, inner], zb[c, 1, x, inner], zb[c, 2, x, inner]
            curl[c, 0, x, shifted] = (zb[c, 2, x, above] - e3) - f3(e2)
            curl[c, 1, x, shifted] = f3(e1) - (zb[c, 2, x + 1, inner] - e3)
            curl[c, 2, x, shifted] = (zb[c, 1, x + 1, inner] - e2) - (zb[c, 0, x, above] - e1)

    def images(t, x, keep=None):
        damping = damp[x]
        for c in range(2):
            b1, b2, b3 = curl[c, 0, x, shifted], curl[c, 1, x, shifted], curl[c, 2, x, shifted]
            b2p, b3p = curl[c, 1, x - 1, shifted], curl[c, 2, x - 1, shifted]
            if keep is not None:
                b2p, b3p = b2p * keep, b3p * keep
            parts = (
                g3(b2) - (curl[c, 2, x, under] - b3),
                (b3p - b3) - g3(b1),
                (curl[c, 0, x, under] - b1) - (b2p - b2),
            )
            for comp in range(3):
                turned = damping * zb[1 - c, comp, x, inner]
                basis[t + 1, c, comp, x] = parts[comp] - turned if c == 0 else parts[comp] + turned

    def sweep_inner(t):
        for k in range(1, 4):
            precondition(t, first + k)
        curls(first)
        curls(first + 1)

        def step(x, carry):
            images(t, x)
            curls(x + 1)
            precondition(t, x + 3)
            return carry

        lax.fori_loop(first + 1, last - 3, step, 0)
        images(t, last - 3)
        curls(last - 2)
        images(t, last - 2)
        curls(last - 1)
        images(t, last - 1)
        for c in range(2):
            def turn(x, comp):
                turned = damp[x] * zb[1 - c, comp, x, inner]
                return turned if c else -turned

            b1, b2, b3 = (curl[c, k, first, shifted] for k in range(3))
            basis[t + 1, c, 0, first] = g3(b2) - (curl[c, 2, first, under] - b3) + turn(first, 0)
            basis[t + 1, c, 1, first] = turn(first, 1) - b3 - g3(b1)
            basis[t + 1, c, 2, first] = (curl[c, 0, first, under] - b1) + b2 + turn(first, 2)
            e2, e3 = zb[c, 1, last, inner], zb[c, 2, last, inner]
            b1 = (zb[c, 2, last, above] - e3) - f3(e2)
            curl[c, 0, last, shifted] = b1
            basis[t + 1, c, 0, last] = turn(last, 0)
            basis[t + 1, c, 1, last] = turn(last, 1) + curl[c, 2, last - 1, shifted] - g3(b1)
            basis[t + 1, c, 2, last] = turn(last, 2) - curl[c, 1, last - 1, shifted]
            basis[t + 1, c, 2, last] += curl[c, 0, last, under] - b1

    def send_down(t, half):
        lo, hi = rows_of(t, half)
        for c in range(2):
            for k in range(2):
                down_out[t, place_of(t, half, c, k)] = zb[c, 1 + k, first, lo:hi]

        @pl.when(me > 0)
        def _():
            down_copy(t, half).start()

    def send_up(t, half):
        lo, hi = rows_of(t, half)
        for c in range(2):
            e1 = zb[c, 0, last, lo:hi]
            up_out[t, place_of(t, half, c, 0)] = f3(e1) + zb[c, 2, last, lo:hi]
            up_out[t, place_of(t, half, c, 1)] = (zb[c, 0, last, lo + 1 : hi + 1] - e1) + zb[c, 1, last, lo:hi]

        @pl.when(me < n - 1)
        def _():
            up_copy(t, half).start()

    def receive(t, half):
        lo, hi = rows_of(t, half)
        at = slice(lo, hi)

        @pl.when(me > 0)
        def _():
            up_copy(t, half).wait_recv()

        for c in range(2):
            b2p = (low_in[t, place_of(t, half, c, 0)] - zb[c, 2, first, at]) * valid
            b3p = (zb[c, 1, first, at] - low_in[t, place_of(t, half, c, 1)]) * valid
            basis[t + 1, c, 1, first, at] += b3p
            basis[t + 1, c, 2, first, at] -= b2p
        if t < SWEEPS - 1:
            precondition(t + 1, first, at)
            send_down(t + 1, half)

        @pl.when(me < n - 1)
        def _():
            down_copy(t, half).wait_recv()

        for c in range(2):
            b2 = up_out[t, place_of(t, half, c, 0)] - high_in[t, place_of(t, half, c, 1)]
            b3 = high_in[t, place_of(t, half, c, 0)] - up_out[t, place_of(t, half, c, 1)]
            curl[c, 2, last, lo + 8 : hi + 8] = b3
            basis[t + 1, c, 0, last, at] += g3(b2) - (curl[c, 2, last, lo + 7 : hi + 7] - b3)
            basis[t + 1, c, 1, last, at] -= b3
            basis[t + 1, c, 2, last, at] += b2
        if t < SWEEPS - 1:
            precondition(t + 1, last, at)
            send_up(t + 1, half)

    def forward_sweep(t, before, between):
        sweep_inner(t)
        before()
        receive(t, 0)
        between()
        receive(t, 1)

    def forward_sent():
        for t in range(SWEEPS):
            for half in range(2):
                @pl.when(me > 0)
                def _(t=t, half=half):
                    down_copy(t, half).wait_send()

                @pl.when(me < n - 1)
                def _(t=t, half=half):
                    up_copy(t, half).wait_send()

    per = rows // 8

    def products(j_, x, at, sums):
        sums = list(sums)
        for comp in range(3):
            re = [basis[k, 0, comp, x, at, :] for k in range(j_ + 1)]
            im = [basis[k, 1, comp, x, at, :] for k in range(j_ + 1)]
            for i_ in range(j_ + 1):
                sums[2 * i_] = sums[2 * i_] + (re[i_] * re[j_] + im[i_] * im[j_])
                if i_ != j_:
                    sums[2 * i_ + 1] = sums[2 * i_ + 1] + (re[i_] * im[j_] - im[i_] * re[j_])
        return tuple(sums)

    def blank_sums(j_):
        return (jnp.zeros((8, lanes), F32),) * (2 * j_ + 1)

    def keep_sums(j_, sums):
        for k in range(2 * j_ + 1):
            at = j_ * j_ - 1 + k
            gram_acc[at : at + 1, :] = jnp.sum(sums[k], axis=0, keepdims=True)

    def pair_sums(j_, start, step, count, sums):
        def body_(i, sums):
            return products(j_, i // per * step + start, pl.ds(pl.multiple_of(i % per * 8, 8), 8), sums)

        return lax.fori_loop(0, count * per, body_, sums, unroll=2)

    def all_sums(j_):
        keep_sums(j_, pair_sums(j_, first, 1, planes, blank_sums(j_)))

    def sweep(t):
        lo, hi = t, wide_planes - t - 1
        wanted = [t] if 0 < t < SWEEPS - 1 else [t, t + 1] if t else []
        for k in range(4):
            precondition(t, lo + k)
        curls(lo)
        curls(lo + 1)

        def gather(x, sums):
            return tuple(
                functools.reduce(lambda held, y: products(j, x, slice(y, y + 8), held), range(0, rows, 8), own)
                for j, own in zip(wanted, sums)
            )

        def step(x, carry, inside):
            keep = jnp.where((x == first) & (me == 0), 0.0, 1.0).astype(F32) if inside else None
            images(t, x, keep)
            curls(x + 1)
            precondition(t, x + 3)
            return gather(x, carry) if inside else carry

        sums = tuple(blank_sums(j) for j in wanted)
        top = min(hi - 2, last + 1)
        lax.fori_loop(lo + 1, first, lambda x, carry: step(x, carry, False), 0)
        sums = lax.fori_loop(first, top, lambda x, carry: step(x, carry, True), sums)
        lax.fori_loop(top, hi - 2, lambda x, carry: step(x, carry, False), 0)
        images(t, hi - 2)
        curls(hi - 1)
        images(t, hi - 1)
        for x in range(top, last + 1):
            sums = gather(x, sums)
        for j, own in zip(wanted, sums):
            keep_sums(j, own)

    gram_lane = lax.broadcasted_iota(jnp.int32, (COUNT, lanes), 1)
    gram_row = lax.broadcasted_iota(jnp.int32, (COUNT, lanes), 0)
    diagonal_of = gram_lane == gram_row

    def gram_start(which):
        local = jnp.sum(gram_acc[...], axis=1, keepdims=True)
        gram_out[which] = jnp.sum(jnp.where(diagonal_of, local, 0.0), axis=0, keepdims=True)
        return spread(gram_out.at[which], gram_in.at[which], gram_s.at[which], gram_r.at[which], "slab", n, me)

    def coefficients(which):
        total = total_of(gram_out[which], gram_in.at[which], n, me)
        total = jnp.sum(jnp.where(diagonal_of, total, 0.0), axis=1, keepdims=True)
        total = jnp.broadcast_to(total, (COUNT, lanes))
        gram, at = {}, 0
        for i, j in PAIRS:
            re = total[at : at + 1, :]
            at += 1
            im = jnp.zeros_like(re)
            if i != j:
                im = total[at : at + 1, :]
                at += 1
            gram[i, j] = (re, im)
            gram[j, i] = (re, -im)
        one = jnp.ones((1, lanes), F32)
        none = jnp.zeros((1, lanes), F32)

        def times(a, b):
            return a[0] * b[0] - a[1] * b[1], a[0] * b[1] + a[1] * b[0]

        poly = [(one, none)]
        coef = [(none, none) for _ in range(SWEEPS)]
        for k in range(SWEEPS):
            up = (none, none)
            below = none
            for i in range(k + 1):
                conj = (poly[i][0], -poly[i][1])
                for j in range(k + 1):
                    both = times(conj, poly[j])
                    term = times(both, gram[i + 1, j])
                    up = (up[0] + term[0], up[1] + term[1])
                    below = below + times(both, gram[i + 1, j + 1])[0]
            below = below + EPSILON
            step = (up[0] / below, up[1] / below)
            moved = [times(step, p) for p in poly]
            for i in range(k + 1):
                coef[i] = (coef[i][0] + moved[i][0], coef[i][1] + moved[i][1])
            grown = poly + [(none, none)]
            for i in range(k + 1):
                grown[i + 1] = (grown[i + 1][0] - moved[i][0], grown[i + 1][1] - moved[i][1])
            poly = grown

        return [(jnp.broadcast_to(a, (16, lanes)), jnp.broadcast_to(b, (16, lanes))) for a, b in coef]

    def combine(wide, out_ref, keep_parts):
        def step(i, carry):
            x, y = i // chunks, pl.multiple_of(i % chunks * 16, 16)
            at = pl.ds(y, 16)
            mr, mi = real_ref[x + first, at, :], imag_ref[x + first, at, :]
            for comp in range(3):
                sr = jnp.zeros((16, lanes), F32)
                si = jnp.zeros((16, lanes), F32)
                for k in range(SWEEPS):
                    br, bi = basis[k, 0, comp, x + first, at, :], basis[k, 1, comp, x + first, at, :]
                    sr = sr + (wide[k][0] * br - wide[k][1] * bi)
                    si = si + (wide[k][0] * bi + wide[k][1] * br)
                for c, value in enumerate((mr * sr + mi * si, mr * si - mi * sr)):
                    out_ref[c, comp, x, at, :] = value
                    if keep_parts:
                        here = pl.ds(pl.multiple_of((comp * planes + x) * rows + y, 16), 16)
                        hi, lo = split(value)
                        field_hi[here, c * lanes : (c + 1) * lanes] = hi
                        field_lo[here, c * lanes : (c + 1) * lanes] = lo
            return carry

        lax.fori_loop(0, planes * chunks, step, 0, unroll=2)

    packs = [
        pltpu.make_async_remote_copy(
            src_ref=pack_ref, dst_ref=pack_in.at[me], send_sem=pack_s.at[d], recv_sem=pack_r.at[d],
            device_id={"slab": lax.rem(me + d, n)}, device_id_type=MESH,
        )
        for d in range(1, n)
    ]

    cap_row = lax.broadcasted_iota(jnp.int32, (CAP, lanes), 0).astype(F32)
    lane_sq = lax.broadcasted_iota(jnp.int32, (lanes, lanes), 1).astype(F32)
    row_sq = lax.broadcasted_iota(jnp.int32, (lanes, lanes), 0).astype(F32)
    earlier = jnp.where(row_sq < lane_sq, 1.0, 0.0).astype(F32)
    self_id = me.astype(F32)

    def compact(p, carry):
        pack = pack_in[p]
        owner, number, spot = pack[0:1, :], pack[1:2, :], pack[2:3, :]
        third = jnp.where(number >= 2.0 * planes * rows, 2.0, jnp.where(number >= 1.0 * planes * rows, 1.0, 0.0))
        inside = number - third * float(planes * rows)
        upper = inside - float((planes - WIDTH) * rows)
        low_place = jnp.where(upper >= 0.0, third * float(side_rows) + upper, -1.0)
        high_place = jnp.where(inside < float(side_rows), third * float(side_rows) + inside, -1.0)
        owned = [jnp.where(owner == self_id + shift, 1.0, 0.0) for shift in (0.0, -1.0, 1.0)]
        owned = jnp.concatenate(owned + [jnp.zeros((5, lanes), F32)], axis=0)
        rank = jnp.dot(owned, earlier, preferred_element_type=F32)
        at = pl.ds(pl.multiple_of(p * CAP, CAP), CAP)
        wanted = (
            (0, 0, number + 1.0), (1, 0, spot), (2, 0, pack[3:4, :]), (3, 0, pack[4:5, :]),
            (4, 1, low_place + 1.0), (5, 1, spot), (6, 2, high_place + 1.0), (7, 2, spot),
        )
        for k, target, value in wanted:
            hit = (cap_row == rank[target : target + 1, :]) & (owned[target : target + 1, :] > 0.0)
            found = jnp.sum(jnp.where(hit, value, 0.0), axis=1, keepdims=True)
            columns[k, at, :] = jnp.broadcast_to(found, (CAP, lanes))
        return carry

    def picks(p, carry):
        at = pl.ds(pl.multiple_of(p * CAP, CAP), CAP)
        place = columns[0, at, :] - 1.0
        for b in range(cells_rows // lanes):
            hot[at, b * lanes : (b + 1) * lanes] = jnp.where(
                lane_sq[:CAP] == place - float(b * lanes), 1.0, 0.0
            ).astype(BF16)
        return carry

    def placings(start, k, count):
        for q in range(slots // lanes):
            spot = columns[k, q * lanes : (q + 1) * lanes, :].T - 1.0

            def fill(b, carry):
                base = pl.multiple_of(b * lanes, lanes)
                hot_t[pl.ds(start + base, lanes), q * lanes : (q + 1) * lanes] = jnp.where(
                    row_sq + base.astype(F32) == spot, 1.0, 0.0
                ).astype(BF16)
                return carry

            lax.fori_loop(0, count // lanes, fill, 0)

    def spread_values(k, re, im):
        here = lane_of_slot == columns[k]
        for part_, value in enumerate((re, im)):
            hi, lo = split(jnp.where(here, value, 0.0))
            mis_hi[:, part_ * lanes : (part_ + 1) * lanes] = hi
            mis_lo[:, part_ * lanes : (part_ + 1) * lanes] = lo

    def add_source(start, x0, count, group):
        for comp in range(3):
            for x in range(0, count, group):
                begin_ = start + (comp * count + x) * rows
                block = hot_t[begin_ : begin_ + group * rows, :]
                added = jnp.dot(block, mis_hi[...], preferred_element_type=F32)
                added = added + jnp.dot(block, mis_lo[...], preferred_element_type=F32)
                for c in range(2):
                    basis[0, c, comp, x0 + x : x0 + x + group] = added[:, c * lanes : (c + 1) * lanes].reshape(
                        group, rows, lanes
                    )

    lane_of_slot = lax.broadcasted_iota(jnp.int32, (slots, lanes), 1).astype(F32)

    precondition(0, first)
    precondition(0, last)

    @pl.when(me == 0)
    def _():
        low_in[...] = jnp.zeros(low_in.shape, F32)

    @pl.when(me == n - 1)
    def _():
        high_in[...] = jnp.zeros(high_in.shape, F32)

    pl.semaphore_wait(barrier, n * nf - 1)
    for half in range(2):
        send_down(0, half)
        send_up(0, half)
    loads[3].wait()
    loads[4].wait()
    loads[5].wait()
    edge = edge_ref[...]
    pack_ref[...] = jnp.concatenate(
        [
            owner_ref[...].astype(F32), (edge >> 7).astype(F32), (edge & 127).astype(F32), observed_ref[...],
            jnp.zeros((3, lanes), F32),
        ],
        axis=0,
    )
    for copy in packs:
        copy.start()
    pack_in[me] = pack_ref[...]
    lax.fori_loop(0, (planes - 2) * chunks, begin_inner, 0, unroll=4)

    def nothing():
        pass

    def receive_packs():
        all_sums(2)
        for copy in packs:
            copy.wait()
        lax.fori_loop(0, n, compact, 0)

    last_sums = []

    def near_last():
        all_sums(3)
        last_sums.append(pair_sums(SWEEPS, first + 1, 1, planes - 2, blank_sums(SWEEPS)))

    forward_sweep(0, nothing, nothing)
    forward_sweep(1, nothing, functools.partial(all_sums, 1))
    forward_sweep(2, nothing, receive_packs)
    forward_sweep(3, nothing, near_last)
    keep_sums(SWEEPS, pair_sums(SWEEPS, first, planes - 1, 2, last_sums[0]))
    sums_sent = gram_start(0)
    forward_sent()
    lax.fori_loop(0, n, picks, 0)
    placings(0, 0, cells_rows)
    placings(cells_rows, 4, 3 * side_rows)
    placings(cells_rows + 3 * side_rows, 6, 3 * side_rows)
    for copy in sums_sent:
        copy.wait()

    @pl.when(me > 0)
    def _():
        beside_copy(1).start()

    @pl.when(me < n - 1)
    def _():
        beside_copy(0).start()

    combine(coefficients(0), forward_ref, True)

    picked = jnp.dot(hot[...], field_hi[...], preferred_element_type=F32)
    picked = picked + jnp.dot(hot[...], field_lo[...], preferred_element_type=F32)
    here = lane_of_slot == columns[1]
    re = jnp.sum(jnp.where(here, picked[:, :lanes], 0.0), axis=1, keepdims=True) - columns[2]
    im = columns[3] - jnp.sum(jnp.where(here, picked[:, lanes:], 0.0), axis=1, keepdims=True)
    both = jnp.where(lane_of_slot == 0.0, re, jnp.where(lane_of_slot == 1.0, im, 0.0))
    mis_out[...] = both.T[0:8, :]

    @pl.when(me > 0)
    def _():
        misfit_copy(1).start()
        beside_copy(0).wait_recv()
        for copy in share_copies(0):
            copy.start()

    @pl.when(me < n - 1)
    def _():
        misfit_copy(0).start()
        beside_copy(1).wait_recv()
        for copy in share_copies(1):
            copy.start()

    spread_values(1, re, im)
    add_source(0, first, planes, 4)

    for side, there in enumerate((me > 0, me < n - 1)):
        start = 0 if side == 0 else last + 1

        @pl.when(there)
        def _(side=side, start=start):
            beside_copy(1 - side).wait_send()
            for copy in share_copies(side):
                copy.wait()
            for k in range(WIDTH):
                factors(start + k, inner, omega * beside[side, k * rows : (k + 1) * rows, :])
            misfit_copy(side).wait_recv()
            misfit_copy(1 - side).wait_send()

        @pl.when(jnp.logical_not(there))
        def _(side=side, start=start):
            mis_in[side] = jnp.zeros(mis_in.shape[1:], F32)
            for k in range(WIDTH):
                damp[start + k] = jnp.zeros((rows, lanes), F32)
                real_ref[start + k] = jnp.zeros((rows, lanes), F32)
                imag_ref[start + k] = jnp.zeros((rows, lanes), F32)

        column = jnp.concatenate([mis_in[side]] * (lanes // 8), axis=0).T
        spread_values(5 + 2 * side, column[:, 0:1], column[:, 1:2])
        add_source(cells_rows + side * 3 * side_rows, start, WIDTH, WIDTH)

    for t in range(SWEEPS):
        sweep(t)
    for copy in gram_start(1):
        copy.wait()
    combine(coefficients(1), adjoint_ref, False)

    high_iota = lax.broadcasted_iota(jnp.int32, (high_blocks, lanes), 0)
    low_iota = lax.broadcasted_iota(jnp.int32, (LOW, lanes), 0)
    acc[...] = jnp.zeros(acc.shape, F32)

    def cells(i, carry):
        x, y = i // chunks, pl.multiple_of(i % chunks * 16, 16)
        value = jnp.zeros((16, lanes), F32)
        for comp in range(3):
            fr, fi = forward_ref[0, comp, x, pl.ds(y, 16), :], forward_ref[1, comp, x, pl.ds(y, 16), :]
            ar, ai = adjoint_ref[0, comp, x, pl.ds(y, 16), :], adjoint_ref[1, comp, x, pl.ds(y, 16), :]
            value = value + (ar * fi + ai * fr)
        value = omega * value
        ids = ids_ref[x, pl.ds(y, 16), :]
        high, low = ids >> 4, ids & (LOW - 1)
        hot = jnp.concatenate(
            [jnp.where(high[r : r + 1, :] == high_iota, 1.0, 0.0) for r in range(16)], axis=0
        ).astype(BF16)
        spot = jnp.concatenate(
            [jnp.where(low[r : r + 1, :] == low_iota, value[r : r + 1, :], 0.0) for r in range(16)], axis=0
        )
        acc[...] += lax.dot_general(
            jnp.concatenate([hot, hot], axis=1), jnp.concatenate(split(spot), axis=1),
            (((1,), (1,)), ((), ())), preferred_element_type=F32,
        )
        return carry

    lax.fori_loop(0, planes * chunks, cells, 0, unroll=4)
    wide_lane = lax.broadcasted_iota(jnp.int32, (high_blocks, 16 * LOW), 1)
    diagonal = jnp.zeros((high_blocks, 16 * LOW), F32)
    for r in range(16):
        inside = (wide_lane >= r * LOW) & (wide_lane < (r + 1) * LOW)
        diagonal = diagonal + jnp.where(inside, acc[r * high_blocks : (r + 1) * high_blocks, :], 0.0)
    folded = diagonal[:, :lanes] + diagonal[:, lanes:]
    for shift in (64, 32, 16):
        folded = folded + pltpu.roll(folded, shift, 1)
    fold_lane = lax.broadcasted_iota(jnp.int32, (8, lanes), 1) // LOW
    fold_row = lax.broadcasted_iota(jnp.int32, (8, lanes), 0)
    own = jnp.concatenate(
        [
            jnp.sum(jnp.where(fold_lane == fold_row, folded[8 * k : 8 * k + 8, :], 0.0), axis=0, keepdims=True)
            for k in range(high_blocks // 8)
        ],
        axis=0,
    )
    grad_out[...] = own
    copies = []
    for k in range(1, n * nf):
        copy = pltpu.make_async_remote_copy(
            src_ref=grad_out, dst_ref=grad_in.at[k], send_sem=grad_s.at[k], recv_sem=grad_r.at[k],
            device_id={"slab": lax.rem(me + k // nf, n), "freq": lax.rem(mine + k % nf, nf)}, device_id_type=MESH,
        )
        copy.start()
        copies.append(copy)
    grad_in[0] = own
    for copy in copies:
        copy.wait()

    def add_one(k, total):
        a, f = k // nf, k % nf
        return total + grad_in[lax.rem(me - a + n, n) * nf + lax.rem(mine - f + nf, nf)]

    gradient_ref[...] = lax.fori_loop(0, n * nf, add_one, jnp.zeros(own.shape, F32), unroll=4)


def write_kernel(forward_ref, adjoint_ref, gradient_ref, forward_out, adjoint_out, gradient_out, sems):
    copies = [
        pltpu.make_async_copy(src, dst, sems.at[k])
        for k, (src, dst) in enumerate([
            (forward_ref, forward_out), (adjoint_ref, adjoint_out), (gradient_ref, gradient_out),
        ])
    ]
    for copy in copies:
        copy.start()
    for copy in copies:
        copy.wait()


def body(source, omega, sigma_blocks, block_ids, rec_owner, rec_edge, observed):
    n, nf = lax.axis_size("slab"), lax.axis_size("freq")
    planes, rows, lanes = block_ids.shape
    blocks = sigma_blocks.shape[0]
    high_blocks = blocks // LOW
    vmem = pl.BlockSpec(memory_space=pltpu.VMEM)
    smem = pl.BlockSpec(memory_space=pltpu.SMEM)
    anywhere = pl.BlockSpec(memory_space=pl.ANY)
    cells_rows = 3 * planes * rows
    wide_planes = planes + 2 * WIDTH
    slots = n * CAP
    field = (2, 3, planes, rows, lanes)
    halo = pltpu.VMEM((SWEEPS, 4 * rows, lanes), F32)
    dma = pltpu.SemaphoreType.DMA
    grad_shape = (high_blocks // 8, lanes)
    grad = pltpu.VMEM(grad_shape, F32)
    wide = pltpu.VMEM((wide_planes, rows, lanes), F32)
    operands = (
        source[0], sigma_blocks.reshape(-1, lanes), block_ids, rec_owner.reshape(1, -1), rec_edge.reshape(1, -1),
        observed[0],
    )
    operands = [pltpu.with_memory_space_constraint(a, pltpu.HBM) for a in operands]
    results = pl.pallas_call(
        functools.partial(kernel, n, nf, high_blocks),
        out_shape=(pltpu.VMEM(field, F32), pltpu.VMEM(field, F32), pltpu.VMEM(grad_shape, F32)),
        in_specs=[smem] + [anywhere] * 6,
        out_specs=(vmem, vmem, vmem),
        scratch_shapes=[
            pltpu.VMEM(field, BF16),
            pltpu.VMEM((blocks // lanes, lanes), F32),
            pltpu.VMEM((planes, rows, lanes), jnp.int32),
            pltpu.VMEM((1, lanes), jnp.int32),
            pltpu.VMEM((1, lanes), jnp.int32),
            pltpu.VMEM((2, lanes), F32),
            wide, wide, wide,
            pltpu.VMEM((planes * rows, lanes), F32),
            pltpu.VMEM((2, WIDTH * rows, lanes), F32),
            pltpu.VMEM((8, lanes), F32),
            pltpu.VMEM((8, slots), F32),
            pltpu.VMEM((2, 8, slots), F32),
            pltpu.VMEM((SWEEPS + 1, 2, 3, wide_planes, rows, lanes), F32),
            pltpu.VMEM((2, 3, wide_planes, rows + 8, lanes), F32),
            pltpu.VMEM((2, 3, wide_planes, rows + 8, lanes), F32),
            halo, halo, halo, halo,
            pltpu.VMEM((COUNT, lanes), F32),
            pltpu.VMEM((2, 1, lanes), F32),
            pltpu.VMEM((2, n, 1, lanes), F32),
            pltpu.VMEM((n, 8, lanes), F32),
            grad,
            pltpu.VMEM((n * nf,) + grad_shape, F32),
            pltpu.VMEM((8, slots, lanes), F32),
            pltpu.VMEM((slots, cells_rows), BF16),
            pltpu.VMEM((3 * wide_planes * rows, slots), BF16),
            pltpu.VMEM((cells_rows, 2 * lanes), BF16),
            pltpu.VMEM((cells_rows, 2 * lanes), BF16),
            pltpu.VMEM((slots, 2 * lanes), BF16),
            pltpu.VMEM((slots, 2 * lanes), BF16),
            pltpu.VMEM((16 * high_blocks, 16 * LOW), F32),
            dma((6,)),
            dma((SWEEPS, 2)), dma((SWEEPS, 2)), dma((SWEEPS, 2)), dma((SWEEPS, 2)),
            dma((2, n)), dma((2, n)),
            dma((n,)), dma((n,)),
            dma((n * nf,)), dma((n * nf,)),
            dma((4,)), dma((4,)),
            dma((2, nf)), dma((2, nf)),
        ],
        compiler_params=pltpu.CompilerParams(
            collective_id=0, has_side_effects=True, vmem_limit_bytes=50 * 1024 * 1024
        ),
        name="solves",
    )(omega, *operands)
    forward, adjoint, gradient = pl.pallas_call(
        write_kernel,
        out_shape=(
            jax.ShapeDtypeStruct(field, F32), jax.ShapeDtypeStruct(field, F32), jax.ShapeDtypeStruct(grad_shape, F32),
        ),
        in_specs=[vmem] * 3,
        out_specs=(anywhere,) * 3,
        scratch_shapes=[dma((3,))],
        name="write",
    )(*[pltpu.with_memory_space_constraint(a, pltpu.VMEM) for a in results])
    return forward[None], adjoint[None], gradient.reshape(blocks)


def solution(mesh):
    return jax.shard_map(
        body,
        mesh=mesh,
        in_specs=(
            P("freq", None, None, "slab", None, None),
            P("freq"),
            P(),
            P("slab", None, None),
            P("slab", None),
            P("slab"),
            P("freq", None, "slab"),
        ),
        out_specs=(
            P("freq", None, None, "slab", None, None),
            P("freq", None, None, "slab", None, None),
            P(),
        ),
        check_vma=False,
    )
```

```python
import functools

import jax
import jax.numpy as jnp
from jax import lax
from jax.experimental import pallas as pl
from jax.experimental.pallas import tpu as pltpu
from jax.sharding import PartitionSpec as P

SWEEPS = 4
EPSILON = 1e-06
LOW = 16
CAP = 32
MESH = pl.DeviceIdType.MESH
F32 = jnp.float32
BF16 = jnp.bfloat16
PAIRS = [(i, j) for j in range(1, SWEEPS + 1) for i in range(j + 1)]
COUNT = sum(1 if i == j else 2 for i, j in PAIRS)
WIDTH = SWEEPS


def split(values):
    high = values.astype(BF16)
    return high, (values - high.astype(F32)).astype(BF16)


def kernel(
    n, nf, high_blocks,
    omega_ref, source_hbm, sigma_hbm, ids_hbm, owner_hbm, edge_hbm, observed_hbm,
    forward_ref, adjoint_ref, gradient_ref,
    source_ref, sigma_ref, ids_ref, owner_ref, edge_ref, observed_ref,
    damp, real_ref, imag_ref, cond, beside, pack_ref, mis_out, mis_in,
    basis, zb, curl, up_out, down_out, low_in, high_in,
    gram_acc, gram_out, gram_in, pack_in, grad_out, grad_in,
    columns, hot, hot_t, field_hi, field_lo, mis_hi, mis_lo, acc, hot_block, overlap,
    local_s, up_s, up_r, down_s, down_r, gram_s, gram_r, pack_s, pack_r, grad_s, grad_r,
    near_s, near_r, share_s, share_r,
):
    me = lax.axis_index("slab")
    mine = lax.axis_index("freq")
    planes, rows, lanes = ids_ref.shape
    first, last = WIDTH, WIDTH + planes - 1
    wide_planes = planes + 2 * WIDTH
    cells_rows = 3 * planes * rows
    slots = n * CAP
    side_rows = WIDTH * rows
    part = side_rows // nf

    loads = [
        pltpu.make_async_copy(src, dst, local_s.at[k])
        for k, (src, dst) in enumerate([
            (ids_hbm, ids_ref), (sigma_hbm, sigma_ref), (source_hbm, source_ref),
            (owner_hbm, owner_ref), (edge_hbm, edge_ref), (observed_hbm, observed_ref),
        ])
    ]
    for copy in loads:
        copy.start()

    barrier = pltpu.get_barrier_semaphore()
    for k in range(1, n * nf):
        pl.semaphore_signal(
            barrier, inc=1, device_id={"slab": lax.rem(me + k // nf, n), "freq": lax.rem(mine + k % nf, nf)},
            device_id_type=MESH,
        )

    def spread(src, dst, send, recv, axis, count, position):
        copies = []
        for d in range(1, count):
            copy = pltpu.make_async_remote_copy(
                src_ref=src, dst_ref=dst.at[d], send_sem=send.at[d], recv_sem=recv.at[d],
                device_id={axis: lax.rem(position + d, count)}, device_id_type=MESH,
            )
            copy.start()
            copies.append(copy)
        return copies

    def total_of(own, buffer, count, position):
        buffer[0] = own
        total = jnp.zeros(own.shape, F32)
        for p in range(count):
            total = total + buffer[lax.rem(position - p + count, count)]
        return total

    lane = lax.broadcasted_iota(jnp.int32, (rows, lanes), 1)
    inner = slice(0, rows)
    above = slice(1, rows + 1)
    shifted = slice(8, rows + 8)
    under = slice(7, rows + 7)

    def f3(v):
        return jnp.where(lane[: v.shape[0]] == lanes - 1, 0.0, pltpu.roll(v, lanes - 1, 1)) - v

    def g3(v):
        return jnp.where(lane[: v.shape[0]] == 0, 0.0, pltpu.roll(v, 1, 1)) - v

    valid = jnp.where(me > 0, 1.0, 0.0).astype(F32)
    omega = omega_ref[0]

    def factors(x, at, damping):
        inverse = 1.0 / (16.0 + damping * damping)
        damp[x, at] = damping
        real_ref[x, at] = 4.0 * inverse
        imag_ref[x, at] = damping * inverse

    def pad(x, carry):
        for c in range(2):
            for comp in range(3):
                zb[c, comp, x, rows : rows + 8] = jnp.zeros((8, lanes), F32)
                curl[c, comp, x, 0:8] = jnp.zeros((8, lanes), F32)
        return carry

    lax.fori_loop(0, wide_planes, pad, 0)

    chunks = rows // 16
    loads[0].wait()
    loads[1].wait()
    loads[2].wait()
    tables = [jnp.broadcast_to(sigma_ref[k : k + 1, :], (8, lanes)) for k in range(sigma_ref.shape[0])]

    def begin(x, y):
        for half in range(2):
            at = pl.ds(pl.multiple_of(y + 8 * half, 8), 8)
            ids = ids_ref[x, at, :]
            low, high = ids & (lanes - 1), ids >> 7
            value = jnp.take_along_axis(tables[0], low, axis=1)
            for k in range(1, len(tables)):
                value = jnp.where(high == k, jnp.take_along_axis(tables[k], low, axis=1), value)
            cond[pl.ds(pl.multiple_of(x * rows + y + 8 * half, 8), 8), :] = value
            factors(x + first, at, omega * value)
        at = pl.ds(y, 16)
        for c in range(2):
            for comp in range(3):
                basis[0, c, comp, x + first, at] = source_ref[c, comp, x, at, :].astype(F32)

    def begin_ends(i, carry):
        begin(i // chunks * (planes - 1), pl.multiple_of(i % chunks * 16, 16))
        return carry

    def begin_inner(i, carry):
        begin(i // chunks + 1, pl.multiple_of(i % chunks * 16, 16))
        return carry

    lax.fori_loop(0, 2 * chunks, begin_ends, 0, unroll=4)

    def beside_copy(side):
        start, to = (planes * rows - side_rows, me + 1) if side == 0 else (0, me + n - 1)
        return pltpu.make_async_remote_copy(
            src_ref=cond.at[pl.ds(start + mine * part, part)], dst_ref=beside.at[side, pl.ds(mine * part, part)],
            send_sem=near_s.at[side], recv_sem=near_r.at[side], device_id={"slab": lax.rem(to, n)},
            device_id_type=MESH,
        )

    def share_copies(side):
        at = pl.ds(mine * part, part)
        return [
            pltpu.make_async_remote_copy(
                src_ref=beside.at[side, at], dst_ref=beside.at[side, at], send_sem=share_s.at[side, d],
                recv_sem=share_r.at[side, d], device_id={"freq": lax.rem(mine + d, nf)}, device_id_type=MESH,
            )
            for d in range(1, nf)
        ]

    def misfit_copy(side):
        to = me + 1 if side == 0 else me + n - 1
        return pltpu.make_async_remote_copy(
            src_ref=mis_out, dst_ref=mis_in.at[side], send_sem=near_s.at[2 + side],
            recv_sem=near_r.at[2 + side], device_id={"slab": lax.rem(to, n)}, device_id_type=MESH,
        )

    def cut_of(t):
        return rows // 8 // 2 * 8 + 8 * (1 - t)

    def rows_of(t, half):
        return (0, cut_of(t)) if half == 0 else (cut_of(t), rows)

    def span(t, half):
        lo, hi = rows_of(t, half)
        return pl.ds(4 * lo, 4 * (hi - lo))

    def place_of(t, half, c, k):
        lo, hi = rows_of(t, half)
        start = 4 * lo + (2 * c + k) * (hi - lo)
        return slice(start, start + hi - lo)

    def up_copy(t, half):
        at = span(t, half)
        return pltpu.make_async_remote_copy(
            src_ref=up_out.at[t, at], dst_ref=low_in.at[t, at], send_sem=up_s.at[t, half],
            recv_sem=up_r.at[t, half], device_id={"slab": lax.rem(me + 1, n)}, device_id_type=MESH,
        )

    def down_copy(t, half):
        at = span(t, half)
        return pltpu.make_async_remote_copy(
            src_ref=down_out.at[t, at], dst_ref=high_in.at[t, at], send_sem=down_s.at[t, half],
            recv_sem=down_r.at[t, half], device_id={"slab": lax.rem(me + n - 1, n)}, device_id_type=MESH,
        )

    def precondition(t, x, at=inner):
        mr, mi = real_ref[x, at], imag_ref[x, at]
        for comp in range(3):
            br, bi = basis[t, 0, comp, x, at], basis[t, 1, comp, x, at]
            zb[0, comp, x, at] = mr * br + mi * bi
            zb[1, comp, x, at] = mr * bi - mi * br

    def curls(x):
        for c in range(2):
            e1, e2, e3 = zb[c, 0, x, inner], zb[c, 1, x, inner], zb[c, 2, x, inner]
            curl[c, 0, x, shifted] = (zb[c, 2, x, above] - e3) - f3(e2)
            curl[c, 1, x, shifted] = f3(e1) - (zb[c, 2, x + 1, inner] - e3)
            curl[c, 2, x, shifted] = (zb[c, 1, x + 1, inner] - e2) - (zb[c, 0, x, above] - e1)

    def images(t, x):
        damping = damp[x]
        for c in range(2):
            b1, b2, b3 = curl[c, 0, x, shifted], curl[c, 1, x, shifted], curl[c, 2, x, shifted]
            b2p, b3p = curl[c, 1, x - 1, shifted], curl[c, 2, x - 1, shifted]
            parts = (
                g3(b2) - (curl[c, 2, x, under] - b3),
                (b3p - b3) - g3(b1),
                (curl[c, 0, x, under] - b1) - (b2p - b2),
            )
            for comp in range(3):
                turned = damping * zb[1 - c, comp, x, inner]
                basis[t + 1, c, comp, x] = parts[comp] - turned if c == 0 else parts[comp] + turned

    def sweep_inner(t):
        for k in range(1, 4):
            precondition(t, first + k)
        curls(first)
        curls(first + 1)

        def step(x, carry):
            images(t, x)
            curls(x + 1)
            precondition(t, x + 3)
            return carry

        lax.fori_loop(first + 1, last - 3, step, 0)
        images(t, last - 3)
        curls(last - 2)
        images(t, last - 2)
        curls(last - 1)
        images(t, last - 1)
        for c in range(2):
            def turn(x, comp):
                turned = damp[x] * zb[1 - c, comp, x, inner]
                return turned if c else -turned

            b1, b2, b3 = (curl[c, k, first, shifted] for k in range(3))
            basis[t + 1, c, 0, first] = g3(b2) - (curl[c, 2, first, under] - b3) + turn(first, 0)
            basis[t + 1, c, 1, first] = turn(first, 1) - b3 - g3(b1)
            basis[t + 1, c, 2, first] = (curl[c, 0, first, under] - b1) + b2 + turn(first, 2)
            e2, e3 = zb[c, 1, last, inner], zb[c, 2, last, inner]
            b1 = (zb[c, 2, last, above] - e3) - f3(e2)
            curl[c, 0, last, shifted] = b1
            basis[t + 1, c, 0, last] = turn(last, 0)
            basis[t + 1, c, 1, last] = turn(last, 1) + curl[c, 2, last - 1, shifted] - g3(b1)
            basis[t + 1, c, 2, last] = turn(last, 2) - curl[c, 1, last - 1, shifted]
            basis[t + 1, c, 2, last] += curl[c, 0, last, under] - b1

    def send_down(t, half):
        lo, hi = rows_of(t, half)
        for c in range(2):
            for k in range(2):
                down_out[t, place_of(t, half, c, k)] = zb[c, 1 + k, first, lo:hi]

        @pl.when(me > 0)
        def _():
            down_copy(t, half).start()

    def send_up(t, half):
        lo, hi = rows_of(t, half)
        for c in range(2):
            e1 = zb[c, 0, last, lo:hi]
            up_out[t, place_of(t, half, c, 0)] = f3(e1) + zb[c, 2, last, lo:hi]
            up_out[t, place_of(t, half, c, 1)] = (zb[c, 0, last, lo + 1 : hi + 1] - e1) + zb[c, 1, last, lo:hi]

        @pl.when(me < n - 1)
        def _():
            up_copy(t, half).start()

    def receive(t, half):
        lo, hi = rows_of(t, half)
        at = slice(lo, hi)

        @pl.when(me > 0)
        def _():
            up_copy(t, half).wait_recv()

        for c in range(2):
            b2p = (low_in[t, place_of(t, half, c, 0)] - zb[c, 2, first, at]) * valid
            b3p = (zb[c, 1, first, at] - low_in[t, place_of(t, half, c, 1)]) * valid
            basis[t + 1, c, 1, first, at] += b3p
            basis[t + 1, c, 2, first, at] -= b2p
        if t < SWEEPS - 1:
            precondition(t + 1, first, at)
            send_down(t + 1, half)

        @pl.when(me < n - 1)
        def _():
            down_copy(t, half).wait_recv()

        for c in range(2):
            b2 = up_out[t, place_of(t, half, c, 0)] - high_in[t, place_of(t, half, c, 1)]
            b3 = high_in[t, place_of(t, half, c, 0)] - up_out[t, place_of(t, half, c, 1)]
            curl[c, 2, last, lo + 8 : hi + 8] = b3
            basis[t + 1, c, 0, last, at] += g3(b2) - (curl[c, 2, last, lo + 7 : hi + 7] - b3)
            basis[t + 1, c, 1, last, at] -= b3
            basis[t + 1, c, 2, last, at] += b2
        if t < SWEEPS - 1:
            precondition(t + 1, last, at)
            send_up(t + 1, half)

    def forward_sweep(t, before, between):
        sweep_inner(t)
        before()
        receive(t, 0)
        between()
        receive(t, 1)

    def forward_sent():
        for t in range(SWEEPS):
            for half in range(2):
                @pl.when(me > 0)
                def _(t=t, half=half):
                    down_copy(t, half).wait_send()

                @pl.when(me < n - 1)
                def _(t=t, half=half):
                    up_copy(t, half).wait_send()

    per = rows // 8

    def products(j_, x, at, sums):
        sums = list(sums)
        for comp in range(3):
            re = [basis[k, 0, comp, x, at, :] for k in range(j_ + 1)]
            im = [basis[k, 1, comp, x, at, :] for k in range(j_ + 1)]
            for i_ in range(j_ + 1):
                sums[2 * i_] = sums[2 * i_] + (re[i_] * re[j_] + im[i_] * im[j_])
                if i_ != j_:
                    sums[2 * i_ + 1] = sums[2 * i_ + 1] + (re[i_] * im[j_] - im[i_] * re[j_])
        return tuple(sums)

    def blank_sums(j_):
        return (jnp.zeros((8, lanes), F32),) * (2 * j_ + 1)

    def keep_sums(j_, sums):
        for k in range(2 * j_ + 1):
            at = j_ * j_ - 1 + k
            gram_acc[at : at + 1, :] = jnp.sum(sums[k], axis=0, keepdims=True)

    def pair_sums(j_, start, step, count, sums):
        def body_(i, sums):
            return products(j_, i // per * step + start, pl.ds(pl.multiple_of(i % per * 8, 8), 8), sums)

        return lax.fori_loop(0, count * per, body_, sums, unroll=2)

    def all_sums(j_):
        keep_sums(j_, pair_sums(j_, first, 1, planes, blank_sums(j_)))

    def sweep(t):
        lo, hi = t, wide_planes - t - 1
        wanted = [t] if 0 < t < SWEEPS - 1 else [t, t + 1] if t else []
        for k in range(4):
            precondition(t, lo + k)
        curls(lo)
        curls(lo + 1)

        def gather(x, sums):
            return tuple(
                functools.reduce(lambda held, y: products(j, x, slice(y, y + 8), held), range(0, rows, 8), own)
                for j, own in zip(wanted, sums)
            )

        def step(x, carry, inside):
            images(t, x)
            curls(x + 1)
            precondition(t, x + 3)
            return gather(x, carry) if inside else carry

        sums = tuple(blank_sums(j) for j in wanted)
        top = min(hi - 2, last + 1)
        lax.fori_loop(lo + 1, first, lambda x, carry: step(x, carry, False), 0)
        for c in range(2):
            for k in range(1, 3):
                curl[c, k, first - 1, shifted] = curl[c, k, first - 1, shifted] * valid
        sums = lax.fori_loop(first, top, lambda x, carry: step(x, carry, True), sums)
        lax.fori_loop(top, hi - 2, lambda x, carry: step(x, carry, False), 0)
        images(t, hi - 2)
        curls(hi - 1)
        images(t, hi - 1)
        for x in range(top, last + 1):
            sums = gather(x, sums)
        for j, own in zip(wanted, sums):
            keep_sums(j, own)

    gram_lane = lax.broadcasted_iota(jnp.int32, (COUNT, lanes), 1)
    gram_row = lax.broadcasted_iota(jnp.int32, (COUNT, lanes), 0)
    diagonal_of = gram_lane == gram_row

    def gram_start(which):
        local = jnp.sum(gram_acc[...], axis=1, keepdims=True)
        gram_out[which] = jnp.sum(jnp.where(diagonal_of, local, 0.0), axis=0, keepdims=True)
        return spread(gram_out.at[which], gram_in.at[which], gram_s.at[which], gram_r.at[which], "slab", n, me)

    def coefficients(which):
        total = total_of(gram_out[which], gram_in.at[which], n, me)
        total = jnp.sum(jnp.where(diagonal_of, total, 0.0), axis=1, keepdims=True)
        total = jnp.broadcast_to(total, (COUNT, lanes))
        gram, at = {}, 0
        for i, j in PAIRS:
            re = total[at : at + 1, :]
            at += 1
            im = jnp.zeros_like(re)
            if i != j:
                im = total[at : at + 1, :]
                at += 1
            gram[i, j] = (re, im)
            gram[j, i] = (re, -im)
        one = jnp.ones((1, lanes), F32)
        none = jnp.zeros((1, lanes), F32)

        def times(a, b):
            return a[0] * b[0] - a[1] * b[1], a[0] * b[1] + a[1] * b[0]

        poly = [(one, none)]
        coef = [(none, none) for _ in range(SWEEPS)]
        for k in range(SWEEPS):
            up = (none, none)
            below = none
            for i in range(k + 1):
                conj = (poly[i][0], -poly[i][1])
                for j in range(k + 1):
                    both = times(conj, poly[j])
                    term = times(both, gram[i + 1, j])
                    up = (up[0] + term[0], up[1] + term[1])
                    below = below + times(both, gram[i + 1, j + 1])[0]
            below = below + EPSILON
            step = (up[0] / below, up[1] / below)
            moved = [times(step, p) for p in poly]
            for i in range(k + 1):
                coef[i] = (coef[i][0] + moved[i][0], coef[i][1] + moved[i][1])
            grown = poly + [(none, none)]
            for i in range(k + 1):
                grown[i + 1] = (grown[i + 1][0] - moved[i][0], grown[i + 1][1] - moved[i][1])
            poly = grown

        return [(jnp.broadcast_to(a, (16, lanes)), jnp.broadcast_to(b, (16, lanes))) for a, b in coef]

    def combine(wide, out_ref, keep_parts):
        def step(i, carry):
            x, y = i // chunks, pl.multiple_of(i % chunks * 16, 16)
            at = pl.ds(y, 16)
            mr, mi = real_ref[x + first, at, :], imag_ref[x + first, at, :]
            for comp in range(3):
                sr = jnp.zeros((16, lanes), F32)
                si = jnp.zeros((16, lanes), F32)
                for k in range(SWEEPS):
                    br, bi = basis[k, 0, comp, x + first, at, :], basis[k, 1, comp, x + first, at, :]
                    sr = sr + (wide[k][0] * br - wide[k][1] * bi)
                    si = si + (wide[k][0] * bi + wide[k][1] * br)
                for c, value in enumerate((mr * sr + mi * si, mr * si - mi * sr)):
                    out_ref[c, comp, x, at, :] = value
                    if keep_parts:
                        here = pl.ds(pl.multiple_of((comp * planes + x) * rows + y, 16), 16)
                        hi, lo = split(value)
                        field_hi[here, c * lanes : (c + 1) * lanes] = hi
                        field_lo[here, c * lanes : (c + 1) * lanes] = lo
            return carry

        lax.fori_loop(0, planes * chunks, step, 0, unroll=2)

    packs = [
        pltpu.make_async_remote_copy(
            src_ref=pack_ref, dst_ref=pack_in.at[me], send_sem=pack_s.at[d], recv_sem=pack_r.at[d],
            device_id={"slab": lax.rem(me + d, n)}, device_id_type=MESH,
        )
        for d in range(1, n)
    ]

    cap_row = lax.broadcasted_iota(jnp.int32, (CAP, lanes), 0).astype(F32)
    lane_sq = lax.broadcasted_iota(jnp.int32, (lanes, lanes), 1).astype(F32)
    row_sq = lax.broadcasted_iota(jnp.int32, (lanes, lanes), 0).astype(F32)
    earlier = jnp.where(row_sq < lane_sq, 1.0, 0.0).astype(F32)
    self_id = me.astype(F32)

    def compact(p, carry):
        pack = pack_in[p]
        owner, number, spot = pack[0:1, :], pack[1:2, :], pack[2:3, :]
        third = jnp.where(number >= 2.0 * planes * rows, 2.0, jnp.where(number >= 1.0 * planes * rows, 1.0, 0.0))
        inside = number - third * float(planes * rows)
        upper = inside - float((planes - WIDTH) * rows)
        low_place = jnp.where(upper >= 0.0, third * float(side_rows) + upper, -1.0)
        high_place = jnp.where(inside < float(side_rows), third * float(side_rows) + inside, -1.0)
        owned = [jnp.where(owner == self_id + shift, 1.0, 0.0) for shift in (0.0, -1.0, 1.0)]
        owned = jnp.concatenate(owned + [jnp.zeros((5, lanes), F32)], axis=0)
        rank = jnp.dot(owned, earlier, preferred_element_type=F32)
        at = pl.ds(pl.multiple_of(p * CAP, CAP), CAP)
        wanted = (
            (0, 0, number + 1.0), (1, 0, spot), (2, 0, pack[3:4, :]), (3, 0, pack[4:5, :]),
            (4, 1, low_place + 1.0), (5, 1, spot), (6, 2, high_place + 1.0), (7, 2, spot),
        )
        for k, target, value in wanted:
            hit = (cap_row == rank[target : target + 1, :]) & (owned[target : target + 1, :] > 0.0)
            found = jnp.sum(jnp.where(hit, value, 0.0), axis=1, keepdims=True)
            columns[k, at, :] = jnp.broadcast_to(found, (CAP, lanes))
        return carry

    def picks(p, carry):
        at = pl.ds(pl.multiple_of(p * CAP, CAP), CAP)
        place = columns[0, at, :] - 1.0
        for b in range(cells_rows // lanes):
            hot[at, b * lanes : (b + 1) * lanes] = jnp.where(
                lane_sq[:CAP] == place - float(b * lanes), 1.0, 0.0
            ).astype(BF16)
        return carry

    def placings(start, k, count):
        for q in range(slots // lanes):
            spot = columns[k, q * lanes : (q + 1) * lanes, :].T - 1.0

            def fill(b, carry):
                base = pl.multiple_of(b * lanes, lanes)
                hot_t[pl.ds(start + base, lanes), q * lanes : (q + 1) * lanes] = jnp.where(
                    row_sq + base.astype(F32) == spot, 1.0, 0.0
                ).astype(BF16)
                return carry

            lax.fori_loop(0, count // lanes, fill, 0)

    def spread_values(k, re, im):
        here = lane_of_slot == columns[k]
        for part_, value in enumerate((re, im)):
            hi, lo = split(jnp.where(here, value, 0.0))
            mis_hi[:, part_ * lanes : (part_ + 1) * lanes] = hi
            mis_lo[:, part_ * lanes : (part_ + 1) * lanes] = lo

    def add_source(start, x0, count, group):
        for comp in range(3):
            for x in range(0, count, group):
                begin_ = start + (comp * count + x) * rows
                block = hot_t[begin_ : begin_ + group * rows, :]
                added = jnp.dot(block, mis_hi[...], preferred_element_type=F32)
                added = added + jnp.dot(block, mis_lo[...], preferred_element_type=F32)
                for c in range(2):
                    basis[0, c, comp, x0 + x : x0 + x + group] = added[:, c * lanes : (c + 1) * lanes].reshape(
                        group, rows, lanes
                    )

    lane_of_slot = lax.broadcasted_iota(jnp.int32, (slots, lanes), 1).astype(F32)

    precondition(0, first)
    precondition(0, last)

    @pl.when(me == 0)
    def _():
        low_in[...] = jnp.zeros(low_in.shape, F32)

    @pl.when(me == n - 1)
    def _():
        high_in[...] = jnp.zeros(high_in.shape, F32)

    pl.semaphore_wait(barrier, n * nf - 1)
    send_down(0, 0)
    send_up(0, 0)
    loads[3].wait()
    loads[4].wait()
    loads[5].wait()
    edge = edge_ref[...]
    pack_ref[...] = jnp.concatenate(
        [
            owner_ref[...].astype(F32), (edge >> 7).astype(F32), (edge & 127).astype(F32), observed_ref[...],
            jnp.zeros((3, lanes), F32),
        ],
        axis=0,
    )
    pack_in[me] = pack_ref[...]
    lax.fori_loop(0, (planes - 2) * chunks, begin_inner, 0, unroll=4)
    send_down(0, 1)
    send_up(0, 1)
    for copy in packs:
        copy.start()

    def nothing():
        pass

    def receive_packs():
        all_sums(2)
        for copy in packs:
            copy.wait()
        lax.fori_loop(0, n, compact, 0)

    last_sums = []

    def near_last():
        all_sums(3)
        last_sums.append(pair_sums(SWEEPS, first + 1, 1, planes - 2, blank_sums(SWEEPS)))

    forward_sweep(0, nothing, nothing)
    forward_sweep(1, nothing, functools.partial(all_sums, 1))
    forward_sweep(2, nothing, receive_packs)
    forward_sweep(3, nothing, near_last)
    keep_sums(SWEEPS, pair_sums(SWEEPS, first, planes - 1, 2, last_sums[0]))
    sums_sent = gram_start(0)
    forward_sent()
    lax.fori_loop(0, n, picks, 0)
    placings(0, 0, cells_rows)
    placings(cells_rows, 4, 3 * side_rows)
    placings(cells_rows + 3 * side_rows, 6, 3 * side_rows)
    for copy in sums_sent:
        copy.wait()

    @pl.when(me > 0)
    def _():
        beside_copy(1).start()

    @pl.when(me < n - 1)
    def _():
        beside_copy(0).start()

    combine(coefficients(0), forward_ref, True)

    picked = jnp.dot(hot[...], field_hi[...], preferred_element_type=F32)
    picked = picked + jnp.dot(hot[...], field_lo[...], preferred_element_type=F32)
    here = lane_of_slot == columns[1]
    re = jnp.sum(jnp.where(here, picked[:, :lanes], 0.0), axis=1, keepdims=True) - columns[2]
    im = columns[3] - jnp.sum(jnp.where(here, picked[:, lanes:], 0.0), axis=1, keepdims=True)
    both = jnp.where(lane_of_slot == 0.0, re, jnp.where(lane_of_slot == 1.0, im, 0.0))
    mis_out[...] = both.T[0:8, :]

    @pl.when(me > 0)
    def _():
        misfit_copy(1).start()
        beside_copy(0).wait_recv()
        for copy in share_copies(0):
            copy.start()

    @pl.when(me < n - 1)
    def _():
        misfit_copy(0).start()
        beside_copy(1).wait_recv()
        for copy in share_copies(1):
            copy.start()

    spread_values(1, re, im)
    add_source(0, first, planes, 4)

    for side, there in enumerate((me > 0, me < n - 1)):
        start = 0 if side == 0 else last + 1

        @pl.when(there)
        def _(side=side, start=start):
            beside_copy(1 - side).wait_send()
            for copy in share_copies(side):
                copy.wait()
            for k in range(WIDTH):
                factors(start + k, inner, omega * beside[side, k * rows : (k + 1) * rows, :])
            misfit_copy(side).wait_recv()
            misfit_copy(1 - side).wait_send()

        @pl.when(jnp.logical_not(there))
        def _(side=side, start=start):
            mis_in[side] = jnp.zeros(mis_in.shape[1:], F32)
            for k in range(WIDTH):
                damp[start + k] = jnp.zeros((rows, lanes), F32)
                real_ref[start + k] = jnp.zeros((rows, lanes), F32)
                imag_ref[start + k] = jnp.zeros((rows, lanes), F32)

        column = jnp.concatenate([mis_in[side]] * (lanes // 8), axis=0).T
        spread_values(5 + 2 * side, column[:, 0:1], column[:, 1:2])
        add_source(cells_rows + side * 3 * side_rows, start, WIDTH, WIDTH)

    for t in range(SWEEPS):
        sweep(t)
    sums_sent = gram_start(1)

    high_iota = lax.broadcasted_iota(jnp.int32, (high_blocks, lanes), 0)
    low_iota = lax.broadcasted_iota(jnp.int32, (LOW, lanes), 0)

    def block_rows(i, carry):
        x, y = i // chunks, pl.multiple_of(i % chunks * 16, 16)
        high = ids_ref[x, pl.ds(y, 16), :] >> 4
        hot_block[i] = jnp.concatenate(
            [jnp.where(high[r : r + 1, :] == high_iota, 1.0, 0.0) for r in range(16)], axis=0
        ).astype(BF16)
        return carry

    def overlaps(i, carry):
        x, y = i // chunks, pl.multiple_of(i % chunks * 16, 16)
        at = pl.ds(y, 16)
        field = [[forward_ref[c, comp, x, at, :] for comp in range(3)] for c in range(2)]
        mr, mi = real_ref[x + first, at, :], imag_ref[x + first, at, :]
        for k in range(SWEEPS):
            qr = jnp.zeros((16, lanes), F32)
            qi = jnp.zeros((16, lanes), F32)
            for comp in range(3):
                br, bi = basis[k, 0, comp, x + first, at, :], basis[k, 1, comp, x + first, at, :]
                qr = qr + (br * field[0][comp] - bi * field[1][comp])
                qi = qi + (br * field[1][comp] + bi * field[0][comp])
            overlap[k, 0, x, at] = mr * qr + mi * qi
            overlap[k, 1, x, at] = mr * qi - mi * qr
        return carry

    lax.fori_loop(0, planes * chunks, block_rows, 0, unroll=2)
    lax.fori_loop(0, planes * chunks, overlaps, 0, unroll=2)
    for copy in sums_sent:
        copy.wait()
    adjoint_steps = coefficients(1)

    acc[...] = jnp.zeros(acc.shape, F32)

    def cells(i, carry):
        x, y = i // chunks, pl.multiple_of(i % chunks * 16, 16)
        at = pl.ds(y, 16)
        value = jnp.zeros((16, lanes), F32)
        for k in range(SWEEPS):
            value = value + (adjoint_steps[k][0] * overlap[k, 1, x, at, :] + adjoint_steps[k][1] * overlap[k, 0, x, at, :])
        value = omega * value
        low = ids_ref[x, at, :] & (LOW - 1)
        spot = jnp.concatenate(
            [jnp.where(low[r : r + 1, :] == low_iota, value[r : r + 1, :], 0.0) for r in range(16)], axis=0
        )
        here = hot_block[i]
        acc[...] += lax.dot_general(
            jnp.concatenate([here, here], axis=1), jnp.concatenate(split(spot), axis=1),
            (((1,), (1,)), ((), ())), preferred_element_type=F32,
        )
        return carry

    lax.fori_loop(0, planes * chunks, cells, 0, unroll=4)
    wide_lane = lax.broadcasted_iota(jnp.int32, (high_blocks, 16 * LOW), 1)
    diagonal = jnp.zeros((high_blocks, 16 * LOW), F32)
    for r in range(16):
        inside = (wide_lane >= r * LOW) & (wide_lane < (r + 1) * LOW)
        diagonal = diagonal + jnp.where(inside, acc[r * high_blocks : (r + 1) * high_blocks, :], 0.0)
    folded = diagonal[:, :lanes] + diagonal[:, lanes:]
    for shift in (64, 32, 16):
        folded = folded + pltpu.roll(folded, shift, 1)
    fold_lane = lax.broadcasted_iota(jnp.int32, (8, lanes), 1) // LOW
    fold_row = lax.broadcasted_iota(jnp.int32, (8, lanes), 0)
    own = jnp.concatenate(
        [
            jnp.sum(jnp.where(fold_lane == fold_row, folded[8 * k : 8 * k + 8, :], 0.0), axis=0, keepdims=True)
            for k in range(high_blocks // 8)
        ],
        axis=0,
    )
    grad_out[...] = own
    copies = []
    for k in range(1, n * nf):
        copy = pltpu.make_async_remote_copy(
            src_ref=grad_out, dst_ref=grad_in.at[k], send_sem=grad_s.at[k], recv_sem=grad_r.at[k],
            device_id={"slab": lax.rem(me + k // nf, n), "freq": lax.rem(mine + k % nf, nf)}, device_id_type=MESH,
        )
        copy.start()
        copies.append(copy)
    grad_in[0] = own
    combine(adjoint_steps, adjoint_ref, False)
    for copy in copies:
        copy.wait()

    def add_one(k, total):
        a, f = k // nf, k % nf
        return total + grad_in[lax.rem(me - a + n, n) * nf + lax.rem(mine - f + nf, nf)]

    gradient_ref[...] = lax.fori_loop(0, n * nf, add_one, jnp.zeros(own.shape, F32), unroll=4)


def write_kernel(forward_ref, adjoint_ref, gradient_ref, forward_out, adjoint_out, gradient_out, sems):
    copies = [
        pltpu.make_async_copy(src, dst, sems.at[k])
        for k, (src, dst) in enumerate([
            (forward_ref, forward_out), (adjoint_ref, adjoint_out), (gradient_ref, gradient_out),
        ])
    ]
    for copy in copies:
        copy.start()
    for copy in copies:
        copy.wait()


def body(source, omega, sigma_blocks, block_ids, rec_owner, rec_edge, observed):
    n, nf = lax.axis_size("slab"), lax.axis_size("freq")
    planes, rows, lanes = block_ids.shape
    blocks = sigma_blocks.shape[0]
    high_blocks = blocks // LOW
    vmem = pl.BlockSpec(memory_space=pltpu.VMEM)
    smem = pl.BlockSpec(memory_space=pltpu.SMEM)
    anywhere = pl.BlockSpec(memory_space=pl.ANY)
    cells_rows = 3 * planes * rows
    wide_planes = planes + 2 * WIDTH
    slots = n * CAP
    field = (2, 3, planes, rows, lanes)
    halo = pltpu.VMEM((SWEEPS, 4 * rows, lanes), F32)
    dma = pltpu.SemaphoreType.DMA
    grad_shape = (high_blocks // 8, lanes)
    grad = pltpu.VMEM(grad_shape, F32)
    wide = pltpu.VMEM((wide_planes, rows, lanes), F32)
    operands = (
        source[0], sigma_blocks.reshape(-1, lanes), block_ids, rec_owner.reshape(1, -1), rec_edge.reshape(1, -1),
        observed[0],
    )
    operands = [pltpu.with_memory_space_constraint(a, pltpu.HBM) for a in operands]
    results = pl.pallas_call(
        functools.partial(kernel, n, nf, high_blocks),
        out_shape=(pltpu.VMEM(field, F32), pltpu.VMEM(field, F32), pltpu.VMEM(grad_shape, F32)),
        in_specs=[smem] + [anywhere] * 6,
        out_specs=(vmem, vmem, vmem),
        scratch_shapes=[
            pltpu.VMEM(field, BF16),
            pltpu.VMEM((blocks // lanes, lanes), F32),
            pltpu.VMEM((planes, rows, lanes), jnp.int32),
            pltpu.VMEM((1, lanes), jnp.int32),
            pltpu.VMEM((1, lanes), jnp.int32),
            pltpu.VMEM((2, lanes), F32),
            wide, wide, wide,
            pltpu.VMEM((planes * rows, lanes), F32),
            pltpu.VMEM((2, WIDTH * rows, lanes), F32),
            pltpu.VMEM((8, lanes), F32),
            pltpu.VMEM((8, slots), F32),
            pltpu.VMEM((2, 8, slots), F32),
            pltpu.VMEM((SWEEPS + 1, 2, 3, wide_planes, rows, lanes), F32),
            pltpu.VMEM((2, 3, wide_planes, rows + 8, lanes), F32),
            pltpu.VMEM((2, 3, wide_planes, rows + 8, lanes), F32),
            halo, halo, halo, halo,
            pltpu.VMEM((COUNT, lanes), F32),
            pltpu.VMEM((2, 1, lanes), F32),
            pltpu.VMEM((2, n, 1, lanes), F32),
            pltpu.VMEM((n, 8, lanes), F32),
            grad,
            pltpu.VMEM((n * nf,) + grad_shape, F32),
            pltpu.VMEM((8, slots, lanes), F32),
            pltpu.VMEM((slots, cells_rows), BF16),
            pltpu.VMEM((3 * wide_planes * rows, slots), BF16),
            pltpu.VMEM((cells_rows, 2 * lanes), BF16),
            pltpu.VMEM((cells_rows, 2 * lanes), BF16),
            pltpu.VMEM((slots, 2 * lanes), BF16),
            pltpu.VMEM((slots, 2 * lanes), BF16),
            pltpu.VMEM((16 * high_blocks, 16 * LOW), F32),
            pltpu.VMEM((planes * rows // 16, 16 * high_blocks, lanes), BF16),
            pltpu.VMEM((SWEEPS, 2, planes, rows, lanes), F32),
            dma((6,)),
            dma((SWEEPS, 2)), dma((SWEEPS, 2)), dma((SWEEPS, 2)), dma((SWEEPS, 2)),
            dma((2, n)), dma((2, n)),
            dma((n,)), dma((n,)),
            dma((n * nf,)), dma((n * nf,)),
            dma((4,)), dma((4,)),
            dma((2, nf)), dma((2, nf)),
        ],
        compiler_params=pltpu.CompilerParams(
            collective_id=0, has_side_effects=True, vmem_limit_bytes=50 * 1024 * 1024
        ),
        name="solves",
    )(omega, *operands)
    forward, adjoint, gradient = pl.pallas_call(
        write_kernel,
        out_shape=(
            jax.ShapeDtypeStruct(field, F32), jax.ShapeDtypeStruct(field, F32), jax.ShapeDtypeStruct(grad_shape, F32),
        ),
        in_specs=[vmem] * 3,
        out_specs=(anywhere,) * 3,
        scratch_shapes=[dma((3,))],
        name="write",
    )(*[pltpu.with_memory_space_constraint(a, pltpu.VMEM) for a in results])
    return forward[None], adjoint[None], gradient.reshape(blocks)


def solution(mesh):
    return jax.shard_map(
        body,
        mesh=mesh,
        in_specs=(
            P("freq", None, None, "slab", None, None),
            P("freq"),
            P(),
            P("slab", None, None),
            P("slab", None),
            P("slab"),
            P("freq", None, "slab"),
        ),
        out_specs=(
            P("freq", None, None, "slab", None, None),
            P("freq", None, None, "slab", None, None),
            P(),
        ),
        check_vma=False,
    )
```

```python
import functools

import jax
import jax.numpy as jnp
from jax import lax
from jax.experimental import pallas as pl
from jax.experimental.pallas import tpu as pltpu
from jax.sharding import PartitionSpec as P

SWEEPS = 4
EPSILON = 1e-06
LOW = 16
CAP = 32
MESH = pl.DeviceIdType.MESH
F32 = jnp.float32
BF16 = jnp.bfloat16
PAIRS = [(i, j) for j in range(1, SWEEPS + 1) for i in range(j + 1)]
COUNT = sum(1 if i == j else 2 for i, j in PAIRS)
WIDTH = SWEEPS


def split(values):
    high = values.astype(BF16)
    return high, (values - high.astype(F32)).astype(BF16)


def kernel(
    n, nf, high_blocks,
    omega_ref, source_hbm, sigma_hbm, ids_hbm, owner_hbm, edge_hbm, observed_hbm,
    forward_ref, adjoint_ref, gradient_ref,
    source_ref, sigma_ref, ids_ref, owner_ref, edge_ref, observed_ref,
    damp, real_ref, imag_ref, cond, beside, pack_ref, mis_out, mis_in,
    basis, zb, curl, up_out, down_out, low_in, high_in,
    gram_acc, gram_out, gram_in, pack_in, grad_out, grad_in,
    columns, hot, hot_t, field_hi, field_lo, mis_hi, mis_lo, acc, hot_block, low_block, overlap,
    local_s, up_s, up_r, down_s, down_r, gram_s, gram_r, pack_s, pack_r, grad_s, grad_r,
    near_s, near_r, share_s, share_r,
):
    me = lax.axis_index("slab")
    mine = lax.axis_index("freq")
    planes, rows, lanes = ids_ref.shape
    first, last = WIDTH, WIDTH + planes - 1
    wide_planes = planes + 2 * WIDTH
    cells_rows = 3 * planes * rows
    slots = n * CAP
    side_rows = WIDTH * rows
    part = side_rows // nf

    loads = [
        pltpu.make_async_copy(src, dst, local_s.at[k])
        for k, (src, dst) in enumerate([
            (ids_hbm, ids_ref), (sigma_hbm, sigma_ref), (source_hbm, source_ref),
            (owner_hbm, owner_ref), (edge_hbm, edge_ref), (observed_hbm, observed_ref),
        ])
    ]
    for copy in loads:
        copy.start()

    barrier = pltpu.get_barrier_semaphore()
    for k in range(1, n * nf):
        pl.semaphore_signal(
            barrier, inc=1, device_id={"slab": lax.rem(me + k // nf, n), "freq": lax.rem(mine + k % nf, nf)},
            device_id_type=MESH,
        )

    def spread(src, dst, send, recv, axis, count, position):
        copies = []
        for d in range(1, count):
            copy = pltpu.make_async_remote_copy(
                src_ref=src, dst_ref=dst.at[d], send_sem=send.at[d], recv_sem=recv.at[d],
                device_id={axis: lax.rem(position + d, count)}, device_id_type=MESH,
            )
            copy.start()
            copies.append(copy)
        return copies

    def total_of(own, buffer, count, position):
        buffer[0] = own
        total = jnp.zeros(own.shape, F32)
        for p in range(count):
            total = total + buffer[lax.rem(position - p + count, count)]
        return total

    lane = lax.broadcasted_iota(jnp.int32, (rows, lanes), 1)
    inner = slice(0, rows)
    above = slice(1, rows + 1)
    shifted = slice(8, rows + 8)
    under = slice(7, rows + 7)

    def f3(v):
        return jnp.where(lane[: v.shape[0]] == lanes - 1, 0.0, pltpu.roll(v, lanes - 1, 1)) - v

    def g3(v):
        return jnp.where(lane[: v.shape[0]] == 0, 0.0, pltpu.roll(v, 1, 1)) - v

    valid = jnp.where(me > 0, 1.0, 0.0).astype(F32)
    omega = omega_ref[0]

    def factors(x, at, damping):
        inverse = 1.0 / (16.0 + damping * damping)
        damp[x, at] = damping
        real_ref[x, at] = 4.0 * inverse
        imag_ref[x, at] = damping * inverse

    def pad(x, carry):
        for c in range(2):
            for comp in range(3):
                zb[c, comp, x, rows : rows + 8] = jnp.zeros((8, lanes), F32)
                curl[c, comp, x, 0:8] = jnp.zeros((8, lanes), F32)
        return carry

    lax.fori_loop(0, wide_planes, pad, 0)

    chunks = rows // 16
    loads[0].wait()
    loads[1].wait()
    loads[2].wait()
    tables = [jnp.broadcast_to(sigma_ref[k : k + 1, :], (8, lanes)) for k in range(sigma_ref.shape[0])]

    def begin(x, y):
        for half in range(2):
            at = pl.ds(pl.multiple_of(y + 8 * half, 8), 8)
            ids = ids_ref[x, at, :]
            low, high = ids & (lanes - 1), ids >> 7
            value = jnp.take_along_axis(tables[0], low, axis=1)
            for k in range(1, len(tables)):
                value = jnp.where(high == k, jnp.take_along_axis(tables[k], low, axis=1), value)
            cond[pl.ds(pl.multiple_of(x * rows + y + 8 * half, 8), 8), :] = value
            factors(x + first, at, omega * value)
        at = pl.ds(y, 16)
        for c in range(2):
            for comp in range(3):
                basis[0, c, comp, x + first, at] = source_ref[c, comp, x, at, :].astype(F32)

    def begin_ends(i, carry):
        begin(i // chunks * (planes - 1), pl.multiple_of(i % chunks * 16, 16))
        return carry

    def begin_inner(i, carry):
        begin(i // chunks + 1, pl.multiple_of(i % chunks * 16, 16))
        return carry

    lax.fori_loop(0, 2 * chunks, begin_ends, 0, unroll=4)

    def beside_copy(side):
        start, to = (planes * rows - side_rows, me + 1) if side == 0 else (0, me + n - 1)
        return pltpu.make_async_remote_copy(
            src_ref=cond.at[pl.ds(start + mine * part, part)], dst_ref=beside.at[side, pl.ds(mine * part, part)],
            send_sem=near_s.at[side], recv_sem=near_r.at[side], device_id={"slab": lax.rem(to, n)},
            device_id_type=MESH,
        )

    def share_copies(side):
        at = pl.ds(mine * part, part)
        return [
            pltpu.make_async_remote_copy(
                src_ref=beside.at[side, at], dst_ref=beside.at[side, at], send_sem=share_s.at[side, d],
                recv_sem=share_r.at[side, d], device_id={"freq": lax.rem(mine + d, nf)}, device_id_type=MESH,
            )
            for d in range(1, nf)
        ]

    def misfit_copy(side):
        to = me + 1 if side == 0 else me + n - 1
        return pltpu.make_async_remote_copy(
            src_ref=mis_out, dst_ref=mis_in.at[side], send_sem=near_s.at[2 + side],
            recv_sem=near_r.at[2 + side], device_id={"slab": lax.rem(to, n)}, device_id_type=MESH,
        )

    def cut_of(t):
        return rows // 8 // 2 * 8 + 8 * (1 - t)

    def rows_of(t, half):
        return (0, cut_of(t)) if half == 0 else (cut_of(t), rows)

    def span(t, half):
        lo, hi = rows_of(t, half)
        return pl.ds(4 * lo, 4 * (hi - lo))

    def place_of(t, half, c, k):
        lo, hi = rows_of(t, half)
        start = 4 * lo + (2 * c + k) * (hi - lo)
        return slice(start, start + hi - lo)

    def up_copy(t, half):
        at = span(t, half)
        return pltpu.make_async_remote_copy(
            src_ref=up_out.at[t, at], dst_ref=low_in.at[t, at], send_sem=up_s.at[t, half],
            recv_sem=up_r.at[t, half], device_id={"slab": lax.rem(me + 1, n)}, device_id_type=MESH,
        )

    def down_copy(t, half):
        at = span(t, half)
        return pltpu.make_async_remote_copy(
            src_ref=down_out.at[t, at], dst_ref=high_in.at[t, at], send_sem=down_s.at[t, half],
            recv_sem=down_r.at[t, half], device_id={"slab": lax.rem(me + n - 1, n)}, device_id_type=MESH,
        )

    def precondition(t, x, at=inner):
        mr, mi = real_ref[x, at], imag_ref[x, at]
        for comp in range(3):
            br, bi = basis[t, 0, comp, x, at], basis[t, 1, comp, x, at]
            zb[0, comp, x, at] = mr * br + mi * bi
            zb[1, comp, x, at] = mr * bi - mi * br

    def curls(x):
        for c in range(2):
            e1, e2, e3 = zb[c, 0, x, inner], zb[c, 1, x, inner], zb[c, 2, x, inner]
            curl[c, 0, x, shifted] = (zb[c, 2, x, above] - e3) - f3(e2)
            curl[c, 1, x, shifted] = f3(e1) - (zb[c, 2, x + 1, inner] - e3)
            curl[c, 2, x, shifted] = (zb[c, 1, x + 1, inner] - e2) - (zb[c, 0, x, above] - e1)

    def images(t, x):
        damping = damp[x]
        for c in range(2):
            b1, b2, b3 = curl[c, 0, x, shifted], curl[c, 1, x, shifted], curl[c, 2, x, shifted]
            b2p, b3p = curl[c, 1, x - 1, shifted], curl[c, 2, x - 1, shifted]
            parts = (
                g3(b2) - (curl[c, 2, x, under] - b3),
                (b3p - b3) - g3(b1),
                (curl[c, 0, x, under] - b1) - (b2p - b2),
            )
            for comp in range(3):
                turned = damping * zb[1 - c, comp, x, inner]
                basis[t + 1, c, comp, x] = parts[comp] - turned if c == 0 else parts[comp] + turned

    def sweep_inner(t):
        for k in range(1, 4):
            precondition(t, first + k)
        curls(first)
        curls(first + 1)

        def step(x, carry):
            images(t, x)
            curls(x + 1)
            precondition(t, x + 3)
            return carry

        lax.fori_loop(first + 1, last - 3, step, 0)
        images(t, last - 3)
        curls(last - 2)
        images(t, last - 2)
        curls(last - 1)
        images(t, last - 1)
        for c in range(2):
            def turn(x, comp):
                turned = damp[x] * zb[1 - c, comp, x, inner]
                return turned if c else -turned

            b1, b2, b3 = (curl[c, k, first, shifted] for k in range(3))
            basis[t + 1, c, 0, first] = g3(b2) - (curl[c, 2, first, under] - b3) + turn(first, 0)
            basis[t + 1, c, 1, first] = turn(first, 1) - b3 - g3(b1)
            basis[t + 1, c, 2, first] = (curl[c, 0, first, under] - b1) + b2 + turn(first, 2)
            e2, e3 = zb[c, 1, last, inner], zb[c, 2, last, inner]
            b1 = (zb[c, 2, last, above] - e3) - f3(e2)
            curl[c, 0, last, shifted] = b1
            basis[t + 1, c, 0, last] = turn(last, 0)
            basis[t + 1, c, 1, last] = turn(last, 1) + curl[c, 2, last - 1, shifted] - g3(b1)
            basis[t + 1, c, 2, last] = turn(last, 2) - curl[c, 1, last - 1, shifted]
            basis[t + 1, c, 2, last] += curl[c, 0, last, under] - b1

    def send_down(t, half):
        lo, hi = rows_of(t, half)
        for c in range(2):
            for k in range(2):
                down_out[t, place_of(t, half, c, k)] = zb[c, 1 + k, first, lo:hi]

        @pl.when(me > 0)
        def _():
            down_copy(t, half).start()

    def send_up(t, half):
        lo, hi = rows_of(t, half)
        for c in range(2):
            e1 = zb[c, 0, last, lo:hi]
            up_out[t, place_of(t, half, c, 0)] = f3(e1) + zb[c, 2, last, lo:hi]
            up_out[t, place_of(t, half, c, 1)] = (zb[c, 0, last, lo + 1 : hi + 1] - e1) + zb[c, 1, last, lo:hi]

        @pl.when(me < n - 1)
        def _():
            up_copy(t, half).start()

    def receive(t, half):
        lo, hi = rows_of(t, half)
        at = slice(lo, hi)

        @pl.when(me > 0)
        def _():
            up_copy(t, half).wait_recv()

        for c in range(2):
            b2p = (low_in[t, place_of(t, half, c, 0)] - zb[c, 2, first, at]) * valid
            b3p = (zb[c, 1, first, at] - low_in[t, place_of(t, half, c, 1)]) * valid
            basis[t + 1, c, 1, first, at] += b3p
            basis[t + 1, c, 2, first, at] -= b2p
        if t < SWEEPS - 1:
            precondition(t + 1, first, at)
            send_down(t + 1, half)

        @pl.when(me < n - 1)
        def _():
            down_copy(t, half).wait_recv()

        for c in range(2):
            b2 = up_out[t, place_of(t, half, c, 0)] - high_in[t, place_of(t, half, c, 1)]
            b3 = high_in[t, place_of(t, half, c, 0)] - up_out[t, place_of(t, half, c, 1)]
            curl[c, 2, last, lo + 8 : hi + 8] = b3
            basis[t + 1, c, 0, last, at] += g3(b2) - (curl[c, 2, last, lo + 7 : hi + 7] - b3)
            basis[t + 1, c, 1, last, at] -= b3
            basis[t + 1, c, 2, last, at] += b2
        if t < SWEEPS - 1:
            precondition(t + 1, last, at)
            send_up(t + 1, half)

    def forward_sweep(t, before, between):
        sweep_inner(t)
        before()
        receive(t, 0)
        between()
        receive(t, 1)

    def forward_sent():
        for t in range(SWEEPS):
            for half in range(2):
                @pl.when(me > 0)
                def _(t=t, half=half):
                    down_copy(t, half).wait_send()

                @pl.when(me < n - 1)
                def _(t=t, half=half):
                    up_copy(t, half).wait_send()

    per = rows // 8

    def products(j_, x, at, sums):
        sums = list(sums)
        for comp in range(3):
            re = [basis[k, 0, comp, x, at, :] for k in range(j_ + 1)]
            im = [basis[k, 1, comp, x, at, :] for k in range(j_ + 1)]
            for i_ in range(j_ + 1):
                sums[2 * i_] = sums[2 * i_] + (re[i_] * re[j_] + im[i_] * im[j_])
                if i_ != j_:
                    sums[2 * i_ + 1] = sums[2 * i_ + 1] + (re[i_] * im[j_] - im[i_] * re[j_])
        return tuple(sums)

    def blank_sums(j_):
        return (jnp.zeros((8, lanes), F32),) * (2 * j_ + 1)

    def keep_sums(j_, sums):
        for k in range(2 * j_ + 1):
            at = j_ * j_ - 1 + k
            gram_acc[at : at + 1, :] = jnp.sum(sums[k], axis=0, keepdims=True)

    def pair_sums(j_, start, step, count, sums):
        def body_(i, sums):
            return products(j_, i // per * step + start, pl.ds(pl.multiple_of(i % per * 8, 8), 8), sums)

        return lax.fori_loop(0, count * per, body_, sums, unroll=2)

    def all_sums(j_):
        keep_sums(j_, pair_sums(j_, first, 1, planes, blank_sums(j_)))

    def sweep(t):
        lo, hi = t, wide_planes - t - 1
        wanted = [t] if 0 < t < SWEEPS - 1 else [t, t + 1] if t else []
        for k in range(4):
            precondition(t, lo + k)
        curls(lo)
        curls(lo + 1)

        def gather(x, sums):
            return tuple(
                functools.reduce(lambda held, y: products(j, x, slice(y, y + 8), held), range(0, rows, 8), own)
                for j, own in zip(wanted, sums)
            )

        def step(x, carry, inside):
            images(t, x)
            curls(x + 1)
            precondition(t, x + 3)
            return gather(x, carry) if inside else carry

        sums = tuple(blank_sums(j) for j in wanted)
        top = min(hi - 2, last + 1)
        lax.fori_loop(lo + 1, first, lambda x, carry: step(x, carry, False), 0)
        for c in range(2):
            for k in range(1, 3):
                curl[c, k, first - 1, shifted] = curl[c, k, first - 1, shifted] * valid
        sums = lax.fori_loop(first, top, lambda x, carry: step(x, carry, True), sums)
        lax.fori_loop(top, hi - 2, lambda x, carry: step(x, carry, False), 0)
        images(t, hi - 2)
        curls(hi - 1)
        images(t, hi - 1)
        for x in range(top, last + 1):
            sums = gather(x, sums)
        for j, own in zip(wanted, sums):
            keep_sums(j, own)

    gram_lane = lax.broadcasted_iota(jnp.int32, (COUNT, lanes), 1)
    gram_row = lax.broadcasted_iota(jnp.int32, (COUNT, lanes), 0)
    diagonal_of = gram_lane == gram_row

    def gram_start(which):
        local = jnp.sum(gram_acc[...], axis=1, keepdims=True)
        gram_out[which] = jnp.sum(jnp.where(diagonal_of, local, 0.0), axis=0, keepdims=True)
        return spread(gram_out.at[which], gram_in.at[which], gram_s.at[which], gram_r.at[which], "slab", n, me)

    def coefficients(which):
        total = total_of(gram_out[which], gram_in.at[which], n, me)
        total = jnp.sum(jnp.where(diagonal_of, total, 0.0), axis=1, keepdims=True)
        total = jnp.broadcast_to(total, (COUNT, lanes))
        gram, at = {}, 0
        for i, j in PAIRS:
            re = total[at : at + 1, :]
            at += 1
            im = jnp.zeros_like(re)
            if i != j:
                im = total[at : at + 1, :]
                at += 1
            gram[i, j] = (re, im)
            gram[j, i] = (re, -im)
        one = jnp.ones((1, lanes), F32)
        none = jnp.zeros((1, lanes), F32)

        def times(a, b):
            return a[0] * b[0] - a[1] * b[1], a[0] * b[1] + a[1] * b[0]

        poly = [(one, none)]
        coef = [(none, none) for _ in range(SWEEPS)]
        for k in range(SWEEPS):
            up = (none, none)
            below = none
            for i in range(k + 1):
                conj = (poly[i][0], -poly[i][1])
                for j in range(k + 1):
                    both = times(conj, poly[j])
                    term = times(both, gram[i + 1, j])
                    up = (up[0] + term[0], up[1] + term[1])
                    below = below + times(both, gram[i + 1, j + 1])[0]
            below = below + EPSILON
            step = (up[0] / below, up[1] / below)
            moved = [times(step, p) for p in poly]
            for i in range(k + 1):
                coef[i] = (coef[i][0] + moved[i][0], coef[i][1] + moved[i][1])
            grown = poly + [(none, none)]
            for i in range(k + 1):
                grown[i + 1] = (grown[i + 1][0] - moved[i][0], grown[i + 1][1] - moved[i][1])
            poly = grown

        return [(jnp.broadcast_to(a, (16, lanes)), jnp.broadcast_to(b, (16, lanes))) for a, b in coef]

    def combine(wide, out_ref, keep_parts):
        def step(i, carry):
            x, y = i // chunks, pl.multiple_of(i % chunks * 16, 16)
            at = pl.ds(y, 16)
            mr, mi = real_ref[x + first, at, :], imag_ref[x + first, at, :]
            for comp in range(3):
                sr = jnp.zeros((16, lanes), F32)
                si = jnp.zeros((16, lanes), F32)
                for k in range(SWEEPS):
                    br, bi = basis[k, 0, comp, x + first, at, :], basis[k, 1, comp, x + first, at, :]
                    sr = sr + (wide[k][0] * br - wide[k][1] * bi)
                    si = si + (wide[k][0] * bi + wide[k][1] * br)
                for c, value in enumerate((mr * sr + mi * si, mr * si - mi * sr)):
                    out_ref[c, comp, x, at, :] = value
                    if keep_parts:
                        here = pl.ds(pl.multiple_of((comp * planes + x) * rows + y, 16), 16)
                        hi, lo = split(value)
                        field_hi[here, c * lanes : (c + 1) * lanes] = hi
                        field_lo[here, c * lanes : (c + 1) * lanes] = lo
            return carry

        lax.fori_loop(0, planes * chunks, step, 0, unroll=2)

    packs = [
        pltpu.make_async_remote_copy(
            src_ref=pack_ref, dst_ref=pack_in.at[me], send_sem=pack_s.at[d], recv_sem=pack_r.at[d],
            device_id={"slab": lax.rem(me + d, n)}, device_id_type=MESH,
        )
        for d in range(1, n)
    ]

    cap_row = lax.broadcasted_iota(jnp.int32, (CAP, lanes), 0).astype(F32)
    lane_sq = lax.broadcasted_iota(jnp.int32, (lanes, lanes), 1).astype(F32)
    row_sq = lax.broadcasted_iota(jnp.int32, (lanes, lanes), 0).astype(F32)
    earlier = jnp.where(row_sq < lane_sq, 1.0, 0.0).astype(F32)
    self_id = me.astype(F32)

    def compact(p, carry):
        pack = pack_in[p]
        owner, number, spot = pack[0:1, :], pack[1:2, :], pack[2:3, :]
        third = jnp.where(number >= 2.0 * planes * rows, 2.0, jnp.where(number >= 1.0 * planes * rows, 1.0, 0.0))
        inside = number - third * float(planes * rows)
        upper = inside - float((planes - WIDTH) * rows)
        low_place = jnp.where(upper >= 0.0, third * float(side_rows) + upper, -1.0)
        high_place = jnp.where(inside < float(side_rows), third * float(side_rows) + inside, -1.0)
        owned = [jnp.where(owner == self_id + shift, 1.0, 0.0) for shift in (0.0, -1.0, 1.0)]
        owned = jnp.concatenate(owned + [jnp.zeros((5, lanes), F32)], axis=0)
        rank = jnp.dot(owned, earlier, preferred_element_type=F32)
        at = pl.ds(pl.multiple_of(p * CAP, CAP), CAP)
        wanted = (
            (0, 0, number + 1.0), (1, 0, spot), (2, 0, pack[3:4, :]), (3, 0, pack[4:5, :]),
            (4, 1, low_place + 1.0), (5, 1, spot), (6, 2, high_place + 1.0), (7, 2, spot),
        )
        for k, target, value in wanted:
            hit = (cap_row == rank[target : target + 1, :]) & (owned[target : target + 1, :] > 0.0)
            found = jnp.sum(jnp.where(hit, value, 0.0), axis=1, keepdims=True)
            columns[k, at, :] = jnp.broadcast_to(found, (CAP, lanes))
        return carry

    def picks(p, carry):
        at = pl.ds(pl.multiple_of(p * CAP, CAP), CAP)
        place = columns[0, at, :] - 1.0
        for b in range(cells_rows // lanes):
            hot[at, b * lanes : (b + 1) * lanes] = jnp.where(
                lane_sq[:CAP] == place - float(b * lanes), 1.0, 0.0
            ).astype(BF16)
        return carry

    def placings(start, k, count):
        for q in range(slots // lanes):
            spot = columns[k, q * lanes : (q + 1) * lanes, :].T - 1.0

            def fill(b, carry):
                base = pl.multiple_of(b * lanes, lanes)
                hot_t[pl.ds(start + base, lanes), q * lanes : (q + 1) * lanes] = jnp.where(
                    row_sq + base.astype(F32) == spot, 1.0, 0.0
                ).astype(BF16)
                return carry

            lax.fori_loop(0, count // lanes, fill, 0)

    def spread_values(k, re, im):
        here = lane_of_slot == columns[k]
        for part_, value in enumerate((re, im)):
            hi, lo = split(jnp.where(here, value, 0.0))
            mis_hi[:, part_ * lanes : (part_ + 1) * lanes] = hi
            mis_lo[:, part_ * lanes : (part_ + 1) * lanes] = lo

    def add_source(start, x0, count, group):
        for comp in range(3):
            for x in range(0, count, group):
                begin_ = start + (comp * count + x) * rows
                block = hot_t[begin_ : begin_ + group * rows, :]
                added = jnp.dot(block, mis_hi[...], preferred_element_type=F32)
                added = added + jnp.dot(block, mis_lo[...], preferred_element_type=F32)
                for c in range(2):
                    basis[0, c, comp, x0 + x : x0 + x + group] = added[:, c * lanes : (c + 1) * lanes].reshape(
                        group, rows, lanes
                    )

    lane_of_slot = lax.broadcasted_iota(jnp.int32, (slots, lanes), 1).astype(F32)

    precondition(0, first)
    precondition(0, last)

    @pl.when(me == 0)
    def _():
        low_in[...] = jnp.zeros(low_in.shape, F32)

    @pl.when(me == n - 1)
    def _():
        high_in[...] = jnp.zeros(high_in.shape, F32)

    pl.semaphore_wait(barrier, n * nf - 1)
    send_down(0, 0)
    send_up(0, 0)
    loads[3].wait()
    loads[4].wait()
    loads[5].wait()
    edge = edge_ref[...]
    pack_ref[...] = jnp.concatenate(
        [
            owner_ref[...].astype(F32), (edge >> 7).astype(F32), (edge & 127).astype(F32), observed_ref[...],
            jnp.zeros((3, lanes), F32),
        ],
        axis=0,
    )
    pack_in[me] = pack_ref[...]
    lax.fori_loop(0, (planes - 2) * chunks, begin_inner, 0, unroll=4)
    send_down(0, 1)
    send_up(0, 1)
    for copy in packs:
        copy.start()

    def nothing():
        pass

    def receive_packs():
        all_sums(2)
        for copy in packs:
            copy.wait()
        lax.fori_loop(0, n, compact, 0)

    last_sums = []

    def near_last():
        all_sums(3)
        last_sums.append(pair_sums(SWEEPS, first + 1, 1, planes - 2, blank_sums(SWEEPS)))

    forward_sweep(0, nothing, nothing)
    forward_sweep(1, nothing, functools.partial(all_sums, 1))
    forward_sweep(2, nothing, receive_packs)
    forward_sweep(3, nothing, near_last)
    keep_sums(SWEEPS, pair_sums(SWEEPS, first, planes - 1, 2, last_sums[0]))
    sums_sent = gram_start(0)
    forward_sent()
    lax.fori_loop(0, n, picks, 0)
    placings(0, 0, cells_rows)
    placings(cells_rows, 4, 3 * side_rows)
    placings(cells_rows + 3 * side_rows, 6, 3 * side_rows)
    for copy in sums_sent:
        copy.wait()

    @pl.when(me > 0)
    def _():
        beside_copy(1).start()

    @pl.when(me < n - 1)
    def _():
        beside_copy(0).start()

    combine(coefficients(0), forward_ref, True)

    picked = jnp.dot(hot[...], field_hi[...], preferred_element_type=F32)
    picked = picked + jnp.dot(hot[...], field_lo[...], preferred_element_type=F32)
    here = lane_of_slot == columns[1]
    re = jnp.sum(jnp.where(here, picked[:, :lanes], 0.0), axis=1, keepdims=True) - columns[2]
    im = columns[3] - jnp.sum(jnp.where(here, picked[:, lanes:], 0.0), axis=1, keepdims=True)
    both = jnp.where(lane_of_slot == 0.0, re, jnp.where(lane_of_slot == 1.0, im, 0.0))
    mis_out[...] = both.T[0:8, :]

    @pl.when(me > 0)
    def _():
        misfit_copy(1).start()
        beside_copy(0).wait_recv()
        for copy in share_copies(0):
            copy.start()

    @pl.when(me < n - 1)
    def _():
        misfit_copy(0).start()
        beside_copy(1).wait_recv()
        for copy in share_copies(1):
            copy.start()

    spread_values(1, re, im)
    add_source(0, first, planes, 4)

    for side, there in enumerate((me > 0, me < n - 1)):
        start = 0 if side == 0 else last + 1

        @pl.when(there)
        def _(side=side, start=start):
            beside_copy(1 - side).wait_send()
            for copy in share_copies(side):
                copy.wait()
            for k in range(WIDTH):
                factors(start + k, inner, omega * beside[side, k * rows : (k + 1) * rows, :])
            misfit_copy(side).wait_recv()
            misfit_copy(1 - side).wait_send()

        @pl.when(jnp.logical_not(there))
        def _(side=side, start=start):
            mis_in[side] = jnp.zeros(mis_in.shape[1:], F32)
            for k in range(WIDTH):
                damp[start + k] = jnp.zeros((rows, lanes), F32)
                real_ref[start + k] = jnp.zeros((rows, lanes), F32)
                imag_ref[start + k] = jnp.zeros((rows, lanes), F32)

        column = jnp.concatenate([mis_in[side]] * (lanes // 8), axis=0).T
        spread_values(5 + 2 * side, column[:, 0:1], column[:, 1:2])
        add_source(cells_rows + side * 3 * side_rows, start, WIDTH, WIDTH)

    for t in range(SWEEPS):
        sweep(t)
    sums_sent = gram_start(1)

    high_iota = lax.broadcasted_iota(jnp.int32, (high_blocks, lanes), 0)
    low_iota = lax.broadcasted_iota(jnp.int32, (LOW, lanes), 0)

    def block_rows(i, carry):
        x, y = i // per, pl.multiple_of(i % per * 8, 8)
        ids = ids_ref[x, pl.ds(y, 8), :]
        high, low = ids >> 4, ids & (LOW - 1)
        hot_block[i] = jnp.concatenate(
            [jnp.where(high[r : r + 1, :] == high_iota, 1.0, 0.0) for r in range(8)], axis=0
        ).astype(BF16)
        for r in range(8):
            low_block[i, r * LOW : (r + 1) * LOW, :] = jnp.where(low[r : r + 1, :] == low_iota, 1.0, 0.0)
        return carry

    def overlaps(i, carry):
        x, y = i // chunks, pl.multiple_of(i % chunks * 16, 16)
        at = pl.ds(y, 16)
        field = [[forward_ref[c, comp, x, at, :] for comp in range(3)] for c in range(2)]
        mr, mi = real_ref[x + first, at, :], imag_ref[x + first, at, :]
        for k in range(SWEEPS):
            qr = jnp.zeros((16, lanes), F32)
            qi = jnp.zeros((16, lanes), F32)
            for comp in range(3):
                br, bi = basis[k, 0, comp, x + first, at, :], basis[k, 1, comp, x + first, at, :]
                qr = qr + (br * field[0][comp] - bi * field[1][comp])
                qi = qi + (br * field[1][comp] + bi * field[0][comp])
            overlap[k, 0, x, at] = mr * qr + mi * qi
            overlap[k, 1, x, at] = mr * qi - mi * qr
        return carry

    lax.fori_loop(0, planes * per, block_rows, 0, unroll=4)
    lax.fori_loop(0, planes * chunks, overlaps, 0, unroll=2)
    for copy in sums_sent:
        copy.wait()
    adjoint_steps = coefficients(1)

    acc[...] = jnp.zeros(acc.shape, F32)

    def cells(i, carry):
        x, y = i // per, pl.multiple_of(i % per * 8, 8)
        at = pl.ds(y, 8)
        value = jnp.zeros((8, lanes), F32)
        for k in range(SWEEPS):
            cr, ci = adjoint_steps[k][0][:8], adjoint_steps[k][1][:8]
            value = value + (cr * overlap[k, 1, x, at, :] + ci * overlap[k, 0, x, at, :])
        value = omega * value
        spot = jnp.concatenate(
            [low_block[i, r * LOW : (r + 1) * LOW, :] * value[r : r + 1, :] for r in range(8)], axis=0
        )
        here = hot_block[i]
        acc[...] += lax.dot_general(
            jnp.concatenate([here, here], axis=1), jnp.concatenate(split(spot), axis=1),
            (((1,), (1,)), ((), ())), preferred_element_type=F32,
        )
        return carry

    lax.fori_loop(0, planes * per, cells, 0, unroll=8)
    wide_lane = lax.broadcasted_iota(jnp.int32, (high_blocks, 8 * LOW), 1)
    folded = jnp.zeros((high_blocks, 8 * LOW), F32)
    for r in range(8):
        inside = (wide_lane >= r * LOW) & (wide_lane < (r + 1) * LOW)
        folded = folded + jnp.where(inside, acc[r * high_blocks : (r + 1) * high_blocks, :], 0.0)
    for shift in (64, 32, 16):
        folded = folded + pltpu.roll(folded, shift, 1)
    fold_lane = lax.broadcasted_iota(jnp.int32, (8, lanes), 1) // LOW
    fold_row = lax.broadcasted_iota(jnp.int32, (8, lanes), 0)
    own = jnp.concatenate(
        [
            jnp.sum(jnp.where(fold_lane == fold_row, folded[8 * k : 8 * k + 8, :], 0.0), axis=0, keepdims=True)
            for k in range(high_blocks // 8)
        ],
        axis=0,
    )
    grad_out[...] = own
    copies = []
    for k in range(1, n * nf):
        copy = pltpu.make_async_remote_copy(
            src_ref=grad_out, dst_ref=grad_in.at[k], send_sem=grad_s.at[k], recv_sem=grad_r.at[k],
            device_id={"slab": lax.rem(me + k // nf, n), "freq": lax.rem(mine + k % nf, nf)}, device_id_type=MESH,
        )
        copy.start()
        copies.append(copy)
    grad_in[0] = own
    combine(adjoint_steps, adjoint_ref, False)
    for copy in copies:
        copy.wait()

    def add_one(k, total):
        a, f = k // nf, k % nf
        return total + grad_in[lax.rem(me - a + n, n) * nf + lax.rem(mine - f + nf, nf)]

    gradient_ref[...] = lax.fori_loop(0, n * nf, add_one, jnp.zeros(own.shape, F32), unroll=4)


def write_kernel(forward_ref, adjoint_ref, gradient_ref, forward_out, adjoint_out, gradient_out, sems):
    copies = [
        pltpu.make_async_copy(src, dst, sems.at[k])
        for k, (src, dst) in enumerate([
            (forward_ref, forward_out), (adjoint_ref, adjoint_out), (gradient_ref, gradient_out),
        ])
    ]
    for copy in copies:
        copy.start()
    for copy in copies:
        copy.wait()


def body(source, omega, sigma_blocks, block_ids, rec_owner, rec_edge, observed):
    n, nf = lax.axis_size("slab"), lax.axis_size("freq")
    planes, rows, lanes = block_ids.shape
    blocks = sigma_blocks.shape[0]
    high_blocks = blocks // LOW
    vmem = pl.BlockSpec(memory_space=pltpu.VMEM)
    smem = pl.BlockSpec(memory_space=pltpu.SMEM)
    anywhere = pl.BlockSpec(memory_space=pl.ANY)
    cells_rows = 3 * planes * rows
    wide_planes = planes + 2 * WIDTH
    slots = n * CAP
    field = (2, 3, planes, rows, lanes)
    halo = pltpu.VMEM((SWEEPS, 4 * rows, lanes), F32)
    dma = pltpu.SemaphoreType.DMA
    grad_shape = (high_blocks // 8, lanes)
    grad = pltpu.VMEM(grad_shape, F32)
    wide = pltpu.VMEM((wide_planes, rows, lanes), F32)
    operands = (
        source[0], sigma_blocks.reshape(-1, lanes), block_ids, rec_owner.reshape(1, -1), rec_edge.reshape(1, -1),
        observed[0],
    )
    operands = [pltpu.with_memory_space_constraint(a, pltpu.HBM) for a in operands]
    results = pl.pallas_call(
        functools.partial(kernel, n, nf, high_blocks),
        out_shape=(pltpu.VMEM(field, F32), pltpu.VMEM(field, F32), pltpu.VMEM(grad_shape, F32)),
        in_specs=[smem] + [anywhere] * 6,
        out_specs=(vmem, vmem, vmem),
        scratch_shapes=[
            pltpu.VMEM(field, BF16),
            pltpu.VMEM((blocks // lanes, lanes), F32),
            pltpu.VMEM((planes, rows, lanes), jnp.int32),
            pltpu.VMEM((1, lanes), jnp.int32),
            pltpu.VMEM((1, lanes), jnp.int32),
            pltpu.VMEM((2, lanes), F32),
            wide, wide, wide,
            pltpu.VMEM((planes * rows, lanes), F32),
            pltpu.VMEM((2, WIDTH * rows, lanes), F32),
            pltpu.VMEM((8, lanes), F32),
            pltpu.VMEM((8, slots), F32),
            pltpu.VMEM((2, 8, slots), F32),
            pltpu.VMEM((SWEEPS + 1, 2, 3, wide_planes, rows, lanes), F32),
            pltpu.VMEM((2, 3, wide_planes, rows + 8, lanes), F32),
            pltpu.VMEM((2, 3, wide_planes, rows + 8, lanes), F32),
            halo, halo, halo, halo,
            pltpu.VMEM((COUNT, lanes), F32),
            pltpu.VMEM((2, 1, lanes), F32),
            pltpu.VMEM((2, n, 1, lanes), F32),
            pltpu.VMEM((n, 8, lanes), F32),
            grad,
            pltpu.VMEM((n * nf,) + grad_shape, F32),
            pltpu.VMEM((8, slots, lanes), F32),
            pltpu.VMEM((slots, cells_rows), BF16),
            pltpu.VMEM((3 * wide_planes * rows, slots), BF16),
            pltpu.VMEM((cells_rows, 2 * lanes), BF16),
            pltpu.VMEM((cells_rows, 2 * lanes), BF16),
            pltpu.VMEM((slots, 2 * lanes), BF16),
            pltpu.VMEM((slots, 2 * lanes), BF16),
            pltpu.VMEM((8 * high_blocks, 8 * LOW), F32),
            pltpu.VMEM((planes * rows // 8, 8 * high_blocks, lanes), BF16),
            pltpu.VMEM((planes * rows // 8, 8 * LOW, lanes), F32),
            pltpu.VMEM((SWEEPS, 2, planes, rows, lanes), F32),
            dma((6,)),
            dma((SWEEPS, 2)), dma((SWEEPS, 2)), dma((SWEEPS, 2)), dma((SWEEPS, 2)),
            dma((2, n)), dma((2, n)),
            dma((n,)), dma((n,)),
            dma((n * nf,)), dma((n * nf,)),
            dma((4,)), dma((4,)),
            dma((2, nf)), dma((2, nf)),
        ],
        compiler_params=pltpu.CompilerParams(
            collective_id=0, has_side_effects=True, vmem_limit_bytes=50 * 1024 * 1024
        ),
        name="solves",
    )(omega, *operands)
    forward, adjoint, gradient = pl.pallas_call(
        write_kernel,
        out_shape=(
            jax.ShapeDtypeStruct(field, F32), jax.ShapeDtypeStruct(field, F32), jax.ShapeDtypeStruct(grad_shape, F32),
        ),
        in_specs=[vmem] * 3,
        out_specs=(anywhere,) * 3,
        scratch_shapes=[dma((3,))],
        name="write",
    )(*[pltpu.with_memory_space_constraint(a, pltpu.VMEM) for a in results])
    return forward[None], adjoint[None], gradient.reshape(blocks)


def solution(mesh):
    return jax.shard_map(
        body,
        mesh=mesh,
        in_specs=(
            P("freq", None, None, "slab", None, None),
            P("freq"),
            P(),
            P("slab", None, None),
            P("slab", None),
            P("slab"),
            P("freq", None, "slab"),
        ),
        out_specs=(
            P("freq", None, None, "slab", None, None),
            P("freq", None, None, "slab", None, None),
            P(),
        ),
        check_vma=False,
    )
```

```python
import functools

import jax
import jax.numpy as jnp
from jax import lax
from jax.experimental import pallas as pl
from jax.experimental.pallas import tpu as pltpu
from jax.sharding import PartitionSpec as P

SWEEPS = 4
EPSILON = 1e-06
LOW = 16
CAP = 32
MESH = pl.DeviceIdType.MESH
F32 = jnp.float32
BF16 = jnp.bfloat16
PAIRS = [(i, j) for j in range(1, SWEEPS + 1) for i in range(j + 1)]
COUNT = sum(1 if i == j else 2 for i, j in PAIRS)
WIDTH = SWEEPS


def split(values):
    high = values.astype(BF16)
    return high, (values - high.astype(F32)).astype(BF16)


def kernel(
    n, nf, high_blocks,
    omega_ref, source_hbm, sigma_hbm, ids_hbm, owner_hbm, edge_hbm, observed_hbm,
    forward_ref, adjoint_ref, gradient_ref,
    source_ref, sigma_ref, ids_ref, owner_ref, edge_ref, observed_ref,
    damp, real_ref, imag_ref, cond, beside, pack_ref, mis_out, mis_in,
    basis, zb, curl, up_out, down_out, low_in, high_in,
    gram_acc, gram_out, gram_in, pack_in, grad_out, grad_in,
    columns, hot, hot_t, field_hi, field_lo, mis_hi, mis_lo, acc, hot_block, low_block, overlap,
    local_s, up_s, up_r, down_s, down_r, gram_s, gram_r, pack_s, pack_r, grad_s, grad_r,
    near_s, near_r, share_s, share_r,
):
    me = lax.axis_index("slab")
    mine = lax.axis_index("freq")
    planes, rows, lanes = ids_ref.shape
    first, last = WIDTH, WIDTH + planes - 1
    wide_planes = planes + 2 * WIDTH
    cells_rows = 3 * planes * rows
    slots = n * CAP
    side_rows = WIDTH * rows
    part = side_rows // nf

    loads = [
        pltpu.make_async_copy(src, dst, local_s.at[k])
        for k, (src, dst) in enumerate([
            (ids_hbm, ids_ref), (sigma_hbm, sigma_ref), (source_hbm, source_ref),
            (owner_hbm, owner_ref), (edge_hbm, edge_ref), (observed_hbm, observed_ref),
        ])
    ]
    for copy in loads:
        copy.start()

    barrier = pltpu.get_barrier_semaphore()
    for k in range(1, n * nf):
        pl.semaphore_signal(
            barrier, inc=1, device_id={"slab": lax.rem(me + k // nf, n), "freq": lax.rem(mine + k % nf, nf)},
            device_id_type=MESH,
        )

    def spread(src, dst, send, recv, axis, count, position):
        copies = []
        for d in range(1, count):
            copy = pltpu.make_async_remote_copy(
                src_ref=src, dst_ref=dst.at[d], send_sem=send.at[d], recv_sem=recv.at[d],
                device_id={axis: lax.rem(position + d, count)}, device_id_type=MESH,
            )
            copy.start()
            copies.append(copy)
        return copies

    def total_of(own, buffer, count, position):
        buffer[0] = own
        total = jnp.zeros(own.shape, F32)
        for p in range(count):
            total = total + buffer[lax.rem(position - p + count, count)]
        return total

    lane = lax.broadcasted_iota(jnp.int32, (rows, lanes), 1)
    inner = slice(0, rows)
    above = slice(1, rows + 1)
    shifted = slice(8, rows + 8)
    under = slice(7, rows + 7)

    def f3(v):
        return jnp.where(lane[: v.shape[0]] == lanes - 1, 0.0, pltpu.roll(v, lanes - 1, 1)) - v

    def g3(v):
        return jnp.where(lane[: v.shape[0]] == 0, 0.0, pltpu.roll(v, 1, 1)) - v

    valid = jnp.where(me > 0, 1.0, 0.0).astype(F32)
    omega = omega_ref[0]

    def factors(x, at, damping):
        inverse = 1.0 / (16.0 + damping * damping)
        damp[x, at] = damping
        real_ref[x, at] = 4.0 * inverse
        imag_ref[x, at] = damping * inverse

    def pad(x, carry):
        for c in range(2):
            for comp in range(3):
                zb[c, comp, x, rows : rows + 8] = jnp.zeros((8, lanes), F32)
                curl[c, comp, x, 0:8] = jnp.zeros((8, lanes), F32)
        return carry

    lax.fori_loop(0, wide_planes, pad, 0)

    chunks = rows // 16
    loads[0].wait()
    loads[1].wait()
    loads[2].wait()
    tables = [jnp.broadcast_to(sigma_ref[k : k + 1, :], (8, lanes)) for k in range(sigma_ref.shape[0])]

    def begin(x, y):
        for half in range(2):
            at = pl.ds(pl.multiple_of(y + 8 * half, 8), 8)
            ids = ids_ref[x, at, :]
            low, high = ids & (lanes - 1), ids >> 7
            value = jnp.take_along_axis(tables[0], low, axis=1)
            for k in range(1, len(tables)):
                value = jnp.where(high == k, jnp.take_along_axis(tables[k], low, axis=1), value)
            cond[pl.ds(pl.multiple_of(x * rows + y + 8 * half, 8), 8), :] = value
            factors(x + first, at, omega * value)
        at = pl.ds(y, 16)
        for c in range(2):
            for comp in range(3):
                basis[0, c, comp, x + first, at] = source_ref[c, comp, x, at, :].astype(F32)

    def begin_ends(i, carry):
        begin(i // chunks * (planes - 1), pl.multiple_of(i % chunks * 16, 16))
        return carry

    def begin_inner(i, carry):
        begin(i // chunks + 1, pl.multiple_of(i % chunks * 16, 16))
        return carry

    lax.fori_loop(0, 2 * chunks, begin_ends, 0, unroll=4)

    def beside_copy(side):
        start, to = (planes * rows - side_rows, me + 1) if side == 0 else (0, me + n - 1)
        return pltpu.make_async_remote_copy(
            src_ref=cond.at[pl.ds(start + mine * part, part)], dst_ref=beside.at[side, pl.ds(mine * part, part)],
            send_sem=near_s.at[side], recv_sem=near_r.at[side], device_id={"slab": lax.rem(to, n)},
            device_id_type=MESH,
        )

    def share_copies(side):
        at = pl.ds(mine * part, part)
        return [
            pltpu.make_async_remote_copy(
                src_ref=beside.at[side, at], dst_ref=beside.at[side, at], send_sem=share_s.at[side, d],
                recv_sem=share_r.at[side, d], device_id={"freq": lax.rem(mine + d, nf)}, device_id_type=MESH,
            )
            for d in range(1, nf)
        ]

    def misfit_copy(side):
        to = me + 1 if side == 0 else me + n - 1
        return pltpu.make_async_remote_copy(
            src_ref=mis_out, dst_ref=mis_in.at[side], send_sem=near_s.at[2 + side],
            recv_sem=near_r.at[2 + side], device_id={"slab": lax.rem(to, n)}, device_id_type=MESH,
        )

    def cut_of(t):
        return rows // 8 // 2 * 8 + 8 * (1 - t)

    def rows_of(t, half):
        return (0, cut_of(t)) if half == 0 else (cut_of(t), rows)

    def span(t, half):
        lo, hi = rows_of(t, half)
        return pl.ds(4 * lo, 4 * (hi - lo))

    def place_of(t, half, c, k):
        lo, hi = rows_of(t, half)
        start = 4 * lo + (2 * c + k) * (hi - lo)
        return slice(start, start + hi - lo)

    def up_copy(t, half):
        at = span(t, half)
        return pltpu.make_async_remote_copy(
            src_ref=up_out.at[t, at], dst_ref=low_in.at[t, at], send_sem=up_s.at[t, half],
            recv_sem=up_r.at[t, half], device_id={"slab": lax.rem(me + 1, n)}, device_id_type=MESH,
        )

    def down_copy(t, half):
        at = span(t, half)
        return pltpu.make_async_remote_copy(
            src_ref=down_out.at[t, at], dst_ref=high_in.at[t, at], send_sem=down_s.at[t, half],
            recv_sem=down_r.at[t, half], device_id={"slab": lax.rem(me + n - 1, n)}, device_id_type=MESH,
        )

    def precondition(t, x, at=inner):
        mr, mi = real_ref[x, at], imag_ref[x, at]
        for comp in range(3):
            br, bi = basis[t, 0, comp, x, at], basis[t, 1, comp, x, at]
            zb[0, comp, x, at] = mr * br + mi * bi
            zb[1, comp, x, at] = mr * bi - mi * br

    def curls(x):
        for c in range(2):
            e1, e2, e3 = zb[c, 0, x, inner], zb[c, 1, x, inner], zb[c, 2, x, inner]
            curl[c, 0, x, shifted] = (zb[c, 2, x, above] - e3) - f3(e2)
            curl[c, 1, x, shifted] = f3(e1) - (zb[c, 2, x + 1, inner] - e3)
            curl[c, 2, x, shifted] = (zb[c, 1, x + 1, inner] - e2) - (zb[c, 0, x, above] - e1)

    def images(t, x):
        damping = damp[x]
        for c in range(2):
            b1, b2, b3 = curl[c, 0, x, shifted], curl[c, 1, x, shifted], curl[c, 2, x, shifted]
            b2p, b3p = curl[c, 1, x - 1, shifted], curl[c, 2, x - 1, shifted]
            parts = (
                g3(b2) - (curl[c, 2, x, under] - b3),
                (b3p - b3) - g3(b1),
                (curl[c, 0, x, under] - b1) - (b2p - b2),
            )
            for comp in range(3):
                turned = damping * zb[1 - c, comp, x, inner]
                basis[t + 1, c, comp, x] = parts[comp] - turned if c == 0 else parts[comp] + turned

    def sweep_inner(t):
        for k in range(1, 4):
            precondition(t, first + k)
        curls(first)
        curls(first + 1)

        def step(x, carry):
            images(t, x)
            curls(x + 1)
            precondition(t, x + 3)
            return carry

        lax.fori_loop(first + 1, last - 3, step, 0)
        images(t, last - 3)
        curls(last - 2)
        images(t, last - 2)
        curls(last - 1)
        images(t, last - 1)
        for c in range(2):
            def turn(x, comp):
                turned = damp[x] * zb[1 - c, comp, x, inner]
                return turned if c else -turned

            b1, b2, b3 = (curl[c, k, first, shifted] for k in range(3))
            basis[t + 1, c, 0, first] = g3(b2) - (curl[c, 2, first, under] - b3) + turn(first, 0)
            basis[t + 1, c, 1, first] = turn(first, 1) - b3 - g3(b1)
            basis[t + 1, c, 2, first] = (curl[c, 0, first, under] - b1) + b2 + turn(first, 2)
            e2, e3 = zb[c, 1, last, inner], zb[c, 2, last, inner]
            b1 = (zb[c, 2, last, above] - e3) - f3(e2)
            curl[c, 0, last, shifted] = b1
            basis[t + 1, c, 0, last] = turn(last, 0)
            basis[t + 1, c, 1, last] = turn(last, 1) + curl[c, 2, last - 1, shifted] - g3(b1)
            basis[t + 1, c, 2, last] = turn(last, 2) - curl[c, 1, last - 1, shifted]
            basis[t + 1, c, 2, last] += curl[c, 0, last, under] - b1

    def send_down(t, half):
        lo, hi = rows_of(t, half)
        for c in range(2):
            for k in range(2):
                down_out[t, place_of(t, half, c, k)] = zb[c, 1 + k, first, lo:hi]

        @pl.when(me > 0)
        def _():
            down_copy(t, half).start()

    def send_up(t, half):
        lo, hi = rows_of(t, half)
        for c in range(2):
            e1 = zb[c, 0, last, lo:hi]
            up_out[t, place_of(t, half, c, 0)] = f3(e1) + zb[c, 2, last, lo:hi]
            up_out[t, place_of(t, half, c, 1)] = (zb[c, 0, last, lo + 1 : hi + 1] - e1) + zb[c, 1, last, lo:hi]

        @pl.when(me < n - 1)
        def _():
            up_copy(t, half).start()

    def receive(t, half):
        lo, hi = rows_of(t, half)
        at = slice(lo, hi)

        @pl.when(me < n - 1)
        def _():
            down_copy(t, half).wait_recv()

        for c in range(2):
            b2 = up_out[t, place_of(t, half, c, 0)] - high_in[t, place_of(t, half, c, 1)]
            b3 = high_in[t, place_of(t, half, c, 0)] - up_out[t, place_of(t, half, c, 1)]
            curl[c, 2, last, lo + 8 : hi + 8] = b3
            basis[t + 1, c, 0, last, at] += g3(b2) - (curl[c, 2, last, lo + 7 : hi + 7] - b3)
            basis[t + 1, c, 1, last, at] -= b3
            basis[t + 1, c, 2, last, at] += b2
        if t < SWEEPS - 1:
            precondition(t + 1, last, at)
            send_up(t + 1, half)

        @pl.when(me > 0)
        def _():
            up_copy(t, half).wait_recv()

        for c in range(2):
            b2p = (low_in[t, place_of(t, half, c, 0)] - zb[c, 2, first, at]) * valid
            b3p = (zb[c, 1, first, at] - low_in[t, place_of(t, half, c, 1)]) * valid
            basis[t + 1, c, 1, first, at] += b3p
            basis[t + 1, c, 2, first, at] -= b2p
        if t < SWEEPS - 1:
            precondition(t + 1, first, at)
            send_down(t + 1, half)

    def forward_sweep(t, before, between):
        sweep_inner(t)
        before()
        receive(t, 0)
        between()
        receive(t, 1)

    def forward_sent():
        for t in range(SWEEPS):
            for half in range(2):
                @pl.when(me > 0)
                def _(t=t, half=half):
                    down_copy(t, half).wait_send()

                @pl.when(me < n - 1)
                def _(t=t, half=half):
                    up_copy(t, half).wait_send()

    per = rows // 8

    def products(j_, x, at, sums):
        sums = list(sums)
        for comp in range(3):
            re = [basis[k, 0, comp, x, at, :] for k in range(j_ + 1)]
            im = [basis[k, 1, comp, x, at, :] for k in range(j_ + 1)]
            for i_ in range(j_ + 1):
                sums[2 * i_] = sums[2 * i_] + (re[i_] * re[j_] + im[i_] * im[j_])
                if i_ != j_:
                    sums[2 * i_ + 1] = sums[2 * i_ + 1] + (re[i_] * im[j_] - im[i_] * re[j_])
        return tuple(sums)

    def blank_sums(j_):
        return (jnp.zeros((8, lanes), F32),) * (2 * j_ + 1)

    def keep_sums(j_, sums):
        for k in range(2 * j_ + 1):
            at = j_ * j_ - 1 + k
            gram_acc[at : at + 1, :] = jnp.sum(sums[k], axis=0, keepdims=True)

    def pair_sums(j_, start, step, count, sums):
        def body_(i, sums):
            return products(j_, i // per * step + start, pl.ds(pl.multiple_of(i % per * 8, 8), 8), sums)

        return lax.fori_loop(0, count * per, body_, sums, unroll=2)

    def all_sums(j_):
        keep_sums(j_, pair_sums(j_, first, 1, planes, blank_sums(j_)))

    def sweep(t):
        lo, hi = t, wide_planes - t - 1
        wanted = [t] if 0 < t < SWEEPS - 1 else [t, t + 1] if t else []
        for k in range(4):
            precondition(t, lo + k)
        curls(lo)
        curls(lo + 1)

        def gather(x, sums):
            return tuple(
                functools.reduce(lambda held, y: products(j, x, slice(y, y + 8), held), range(0, rows, 8), own)
                for j, own in zip(wanted, sums)
            )

        def step(x, carry, inside):
            images(t, x)
            curls(x + 1)
            precondition(t, x + 3)
            return gather(x, carry) if inside else carry

        sums = tuple(blank_sums(j) for j in wanted)
        top = min(hi - 2, last + 1)
        lax.fori_loop(lo + 1, first, lambda x, carry: step(x, carry, False), 0)
        for c in range(2):
            for k in range(1, 3):
                curl[c, k, first - 1, shifted] = curl[c, k, first - 1, shifted] * valid
        sums = lax.fori_loop(first, top, lambda x, carry: step(x, carry, True), sums)
        lax.fori_loop(top, hi - 2, lambda x, carry: step(x, carry, False), 0)
        images(t, hi - 2)
        curls(hi - 1)
        images(t, hi - 1)
        for x in range(top, last + 1):
            sums = gather(x, sums)
        for j, own in zip(wanted, sums):
            keep_sums(j, own)

    gram_lane = lax.broadcasted_iota(jnp.int32, (COUNT, lanes), 1)
    gram_row = lax.broadcasted_iota(jnp.int32, (COUNT, lanes), 0)
    diagonal_of = gram_lane == gram_row

    def gram_start(which):
        local = jnp.sum(gram_acc[...], axis=1, keepdims=True)
        gram_out[which] = jnp.sum(jnp.where(diagonal_of, local, 0.0), axis=0, keepdims=True)
        return spread(gram_out.at[which], gram_in.at[which], gram_s.at[which], gram_r.at[which], "slab", n, me)

    def coefficients(which):
        total = total_of(gram_out[which], gram_in.at[which], n, me)
        total = jnp.sum(jnp.where(diagonal_of, total, 0.0), axis=1, keepdims=True)
        total = jnp.broadcast_to(total, (COUNT, lanes))
        gram, at = {}, 0
        for i, j in PAIRS:
            re = total[at : at + 1, :]
            at += 1
            im = jnp.zeros_like(re)
            if i != j:
                im = total[at : at + 1, :]
                at += 1
            gram[i, j] = (re, im)
            gram[j, i] = (re, -im)
        one = jnp.ones((1, lanes), F32)
        none = jnp.zeros((1, lanes), F32)

        def times(a, b):
            return a[0] * b[0] - a[1] * b[1], a[0] * b[1] + a[1] * b[0]

        poly = [(one, none)]
        coef = [(none, none) for _ in range(SWEEPS)]
        for k in range(SWEEPS):
            up = (none, none)
            below = none
            for i in range(k + 1):
                conj = (poly[i][0], -poly[i][1])
                for j in range(k + 1):
                    both = times(conj, poly[j])
                    term = times(both, gram[i + 1, j])
                    up = (up[0] + term[0], up[1] + term[1])
                    below = below + times(both, gram[i + 1, j + 1])[0]
            below = below + EPSILON
            step = (up[0] / below, up[1] / below)
            moved = [times(step, p) for p in poly]
            for i in range(k + 1):
                coef[i] = (coef[i][0] + moved[i][0], coef[i][1] + moved[i][1])
            grown = poly + [(none, none)]
            for i in range(k + 1):
                grown[i + 1] = (grown[i + 1][0] - moved[i][0], grown[i + 1][1] - moved[i][1])
            poly = grown

        return [(jnp.broadcast_to(a, (16, lanes)), jnp.broadcast_to(b, (16, lanes))) for a, b in coef]

    def combine(wide, out_ref, keep_parts):
        def step(i, carry):
            x, y = i // chunks, pl.multiple_of(i % chunks * 16, 16)
            at = pl.ds(y, 16)
            mr, mi = real_ref[x + first, at, :], imag_ref[x + first, at, :]
            for comp in range(3):
                sr = jnp.zeros((16, lanes), F32)
                si = jnp.zeros((16, lanes), F32)
                for k in range(SWEEPS):
                    br, bi = basis[k, 0, comp, x + first, at, :], basis[k, 1, comp, x + first, at, :]
                    sr = sr + (wide[k][0] * br - wide[k][1] * bi)
                    si = si + (wide[k][0] * bi + wide[k][1] * br)
                for c, value in enumerate((mr * sr + mi * si, mr * si - mi * sr)):
                    out_ref[c, comp, x, at, :] = value
                    if keep_parts:
                        here = pl.ds(pl.multiple_of((comp * planes + x) * rows + y, 16), 16)
                        hi, lo = split(value)
                        field_hi[here, c * lanes : (c + 1) * lanes] = hi
                        field_lo[here, c * lanes : (c + 1) * lanes] = lo
            return carry

        lax.fori_loop(0, planes * chunks, step, 0, unroll=2)

    packs = [
        pltpu.make_async_remote_copy(
            src_ref=pack_ref, dst_ref=pack_in.at[me], send_sem=pack_s.at[d], recv_sem=pack_r.at[d],
            device_id={"slab": lax.rem(me + d, n)}, device_id_type=MESH,
        )
        for d in range(1, n)
    ]

    cap_row = lax.broadcasted_iota(jnp.int32, (CAP, lanes), 0).astype(F32)
    lane_sq = lax.broadcasted_iota(jnp.int32, (lanes, lanes), 1).astype(F32)
    row_sq = lax.broadcasted_iota(jnp.int32, (lanes, lanes), 0).astype(F32)
    earlier = jnp.where(row_sq < lane_sq, 1.0, 0.0).astype(F32)
    self_id = me.astype(F32)

    def compact(p, carry):
        pack = pack_in[p]
        owner, number, spot = pack[0:1, :], pack[1:2, :], pack[2:3, :]
        third = jnp.where(number >= 2.0 * planes * rows, 2.0, jnp.where(number >= 1.0 * planes * rows, 1.0, 0.0))
        inside = number - third * float(planes * rows)
        upper = inside - float((planes - WIDTH) * rows)
        low_place = jnp.where(upper >= 0.0, third * float(side_rows) + upper, -1.0)
        high_place = jnp.where(inside < float(side_rows), third * float(side_rows) + inside, -1.0)
        owned = [jnp.where(owner == self_id + shift, 1.0, 0.0) for shift in (0.0, -1.0, 1.0)]
        owned = jnp.concatenate(owned + [jnp.zeros((5, lanes), F32)], axis=0)
        rank = jnp.dot(owned, earlier, preferred_element_type=F32)
        at = pl.ds(pl.multiple_of(p * CAP, CAP), CAP)
        wanted = (
            (0, 0, number + 1.0), (1, 0, spot), (2, 0, pack[3:4, :]), (3, 0, pack[4:5, :]),
            (4, 1, low_place + 1.0), (5, 1, spot), (6, 2, high_place + 1.0), (7, 2, spot),
        )
        for k, target, value in wanted:
            hit = (cap_row == rank[target : target + 1, :]) & (owned[target : target + 1, :] > 0.0)
            found = jnp.sum(jnp.where(hit, value, 0.0), axis=1, keepdims=True)
            columns[k, at, :] = jnp.broadcast_to(found, (CAP, lanes))
        return carry

    def picks(p, carry):
        at = pl.ds(pl.multiple_of(p * CAP, CAP), CAP)
        place = columns[0, at, :] - 1.0
        for b in range(cells_rows // lanes):
            hot[at, b * lanes : (b + 1) * lanes] = jnp.where(
                lane_sq[:CAP] == place - float(b * lanes), 1.0, 0.0
            ).astype(BF16)
        return carry

    def placings(start, k, count):
        for q in range(slots // lanes):
            spot = columns[k, q * lanes : (q + 1) * lanes, :].T - 1.0

            def fill(b, carry):
                base = pl.multiple_of(b * lanes, lanes)
                hot_t[pl.ds(start + base, lanes), q * lanes : (q + 1) * lanes] = jnp.where(
                    row_sq + base.astype(F32) == spot, 1.0, 0.0
                ).astype(BF16)
                return carry

            lax.fori_loop(0, count // lanes, fill, 0)

    def spread_values(k, re, im):
        here = lane_of_slot == columns[k]
        for part_, value in enumerate((re, im)):
            hi, lo = split(jnp.where(here, value, 0.0))
            mis_hi[:, part_ * lanes : (part_ + 1) * lanes] = hi
            mis_lo[:, part_ * lanes : (part_ + 1) * lanes] = lo

    def add_source(start, x0, count, group):
        for comp in range(3):
            for x in range(0, count, group):
                begin_ = start + (comp * count + x) * rows
                block = hot_t[begin_ : begin_ + group * rows, :]
                added = jnp.dot(block, mis_hi[...], preferred_element_type=F32)
                added = added + jnp.dot(block, mis_lo[...], preferred_element_type=F32)
                for c in range(2):
                    basis[0, c, comp, x0 + x : x0 + x + group] = added[:, c * lanes : (c + 1) * lanes].reshape(
                        group, rows, lanes
                    )

    lane_of_slot = lax.broadcasted_iota(jnp.int32, (slots, lanes), 1).astype(F32)

    precondition(0, first)
    precondition(0, last)

    @pl.when(me == 0)
    def _():
        low_in[...] = jnp.zeros(low_in.shape, F32)

    @pl.when(me == n - 1)
    def _():
        high_in[...] = jnp.zeros(high_in.shape, F32)

    pl.semaphore_wait(barrier, n * nf - 1)
    send_down(0, 0)
    send_up(0, 0)
    loads[3].wait()
    loads[4].wait()
    loads[5].wait()
    edge = edge_ref[...]
    pack_ref[...] = jnp.concatenate(
        [
            owner_ref[...].astype(F32), (edge >> 7).astype(F32), (edge & 127).astype(F32), observed_ref[...],
            jnp.zeros((3, lanes), F32),
        ],
        axis=0,
    )
    pack_in[me] = pack_ref[...]
    lax.fori_loop(0, (planes - 2) * chunks, begin_inner, 0, unroll=4)
    send_down(0, 1)
    send_up(0, 1)
    for copy in packs:
        copy.start()

    def nothing():
        pass

    def receive_packs():
        all_sums(2)
        for copy in packs:
            copy.wait()
        lax.fori_loop(0, n, compact, 0)

    last_sums = []

    def near_last():
        all_sums(3)
        last_sums.append(pair_sums(SWEEPS, first + 1, 1, planes - 2, blank_sums(SWEEPS)))

    forward_sweep(0, nothing, nothing)
    forward_sweep(1, nothing, functools.partial(all_sums, 1))
    forward_sweep(2, nothing, receive_packs)
    forward_sweep(3, nothing, near_last)
    keep_sums(SWEEPS, pair_sums(SWEEPS, first, planes - 1, 2, last_sums[0]))
    sums_sent = gram_start(0)
    forward_sent()
    lax.fori_loop(0, n, picks, 0)
    placings(0, 0, cells_rows)
    placings(cells_rows, 4, 3 * side_rows)
    placings(cells_rows + 3 * side_rows, 6, 3 * side_rows)
    for copy in sums_sent:
        copy.wait()

    @pl.when(me > 0)
    def _():
        beside_copy(1).start()

    @pl.when(me < n - 1)
    def _():
        beside_copy(0).start()

    combine(coefficients(0), forward_ref, True)

    picked = jnp.dot(hot[...], field_hi[...], preferred_element_type=F32)
    picked = picked + jnp.dot(hot[...], field_lo[...], preferred_element_type=F32)
    here = lane_of_slot == columns[1]
    re = jnp.sum(jnp.where(here, picked[:, :lanes], 0.0), axis=1, keepdims=True) - columns[2]
    im = columns[3] - jnp.sum(jnp.where(here, picked[:, lanes:], 0.0), axis=1, keepdims=True)
    both = jnp.where(lane_of_slot == 0.0, re, jnp.where(lane_of_slot == 1.0, im, 0.0))
    mis_out[...] = both.T[0:8, :]

    @pl.when(me > 0)
    def _():
        misfit_copy(1).start()
        beside_copy(0).wait_recv()
        for copy in share_copies(0):
            copy.start()

    @pl.when(me < n - 1)
    def _():
        misfit_copy(0).start()
        beside_copy(1).wait_recv()
        for copy in share_copies(1):
            copy.start()

    spread_values(1, re, im)
    add_source(0, first, planes, 4)

    for side, there in enumerate((me > 0, me < n - 1)):
        start = 0 if side == 0 else last + 1

        @pl.when(there)
        def _(side=side, start=start):
            beside_copy(1 - side).wait_send()
            for copy in share_copies(side):
                copy.wait()
            for k in range(WIDTH):
                factors(start + k, inner, omega * beside[side, k * rows : (k + 1) * rows, :])
            misfit_copy(side).wait_recv()
            misfit_copy(1 - side).wait_send()

        @pl.when(jnp.logical_not(there))
        def _(side=side, start=start):
            mis_in[side] = jnp.zeros(mis_in.shape[1:], F32)
            for k in range(WIDTH):
                damp[start + k] = jnp.zeros((rows, lanes), F32)
                real_ref[start + k] = jnp.zeros((rows, lanes), F32)
                imag_ref[start + k] = jnp.zeros((rows, lanes), F32)

        column = jnp.concatenate([mis_in[side]] * (lanes // 8), axis=0).T
        spread_values(5 + 2 * side, column[:, 0:1], column[:, 1:2])
        add_source(cells_rows + side * 3 * side_rows, start, WIDTH, WIDTH)

    for t in range(SWEEPS):
        sweep(t)
    sums_sent = gram_start(1)

    high_iota = lax.broadcasted_iota(jnp.int32, (high_blocks, lanes), 0)
    low_iota = lax.broadcasted_iota(jnp.int32, (LOW, lanes), 0)

    def block_rows(i, carry):
        x, y = i // per, pl.multiple_of(i % per * 8, 8)
        ids = ids_ref[x, pl.ds(y, 8), :]
        high, low = ids >> 4, ids & (LOW - 1)
        hot_block[i] = jnp.concatenate(
            [jnp.where(high[r : r + 1, :] == high_iota, 1.0, 0.0) for r in range(8)], axis=0
        ).astype(BF16)
        for r in range(8):
            low_block[i, r * LOW : (r + 1) * LOW, :] = jnp.where(low[r : r + 1, :] == low_iota, 1.0, 0.0)
        return carry

    def overlaps(i, carry):
        x, y = i // chunks, pl.multiple_of(i % chunks * 16, 16)
        at = pl.ds(y, 16)
        field = [[forward_ref[c, comp, x, at, :] for comp in range(3)] for c in range(2)]
        mr, mi = real_ref[x + first, at, :], imag_ref[x + first, at, :]
        for k in range(SWEEPS):
            qr = jnp.zeros((16, lanes), F32)
            qi = jnp.zeros((16, lanes), F32)
            for comp in range(3):
                br, bi = basis[k, 0, comp, x + first, at, :], basis[k, 1, comp, x + first, at, :]
                qr = qr + (br * field[0][comp] - bi * field[1][comp])
                qi = qi + (br * field[1][comp] + bi * field[0][comp])
            overlap[k, 0, x, at] = mr * qr + mi * qi
            overlap[k, 1, x, at] = mr * qi - mi * qr
        return carry

    lax.fori_loop(0, planes * per, block_rows, 0, unroll=4)
    lax.fori_loop(0, planes * chunks, overlaps, 0, unroll=2)
    for copy in sums_sent:
        copy.wait()
    adjoint_steps = coefficients(1)

    acc[...] = jnp.zeros(acc.shape, F32)

    def cells(i, carry):
        x, y = i // per, pl.multiple_of(i % per * 8, 8)
        at = pl.ds(y, 8)
        value = jnp.zeros((8, lanes), F32)
        for k in range(SWEEPS):
            cr, ci = adjoint_steps[k][0][:8], adjoint_steps[k][1][:8]
            value = value + (cr * overlap[k, 1, x, at, :] + ci * overlap[k, 0, x, at, :])
        value = omega * value
        spot = jnp.concatenate(
            [low_block[i, r * LOW : (r + 1) * LOW, :] * value[r : r + 1, :] for r in range(8)], axis=0
        )
        here = hot_block[i]
        acc[...] += lax.dot_general(
            jnp.concatenate([here, here], axis=1), jnp.concatenate(split(spot), axis=1),
            (((1,), (1,)), ((), ())), preferred_element_type=F32,
        )
        return carry

    lax.fori_loop(0, planes * per, cells, 0, unroll=8)
    wide_lane = lax.broadcasted_iota(jnp.int32, (high_blocks, 8 * LOW), 1)
    folded = jnp.zeros((high_blocks, 8 * LOW), F32)
    for r in range(8):
        inside = (wide_lane >= r * LOW) & (wide_lane < (r + 1) * LOW)
        folded = folded + jnp.where(inside, acc[r * high_blocks : (r + 1) * high_blocks, :], 0.0)
    for shift in (64, 32, 16):
        folded = folded + pltpu.roll(folded, shift, 1)
    fold_lane = lax.broadcasted_iota(jnp.int32, (8, lanes), 1) // LOW
    fold_row = lax.broadcasted_iota(jnp.int32, (8, lanes), 0)
    own = jnp.concatenate(
        [
            jnp.sum(jnp.where(fold_lane == fold_row, folded[8 * k : 8 * k + 8, :], 0.0), axis=0, keepdims=True)
            for k in range(high_blocks // 8)
        ],
        axis=0,
    )
    grad_out[...] = own
    copies = []
    for k in range(1, n * nf):
        copy = pltpu.make_async_remote_copy(
            src_ref=grad_out, dst_ref=grad_in.at[k], send_sem=grad_s.at[k], recv_sem=grad_r.at[k],
            device_id={"slab": lax.rem(me + k // nf, n), "freq": lax.rem(mine + k % nf, nf)}, device_id_type=MESH,
        )
        copy.start()
        copies.append(copy)
    grad_in[0] = own
    combine(adjoint_steps, adjoint_ref, False)
    for copy in copies:
        copy.wait()

    def add_one(k, total):
        a, f = k // nf, k % nf
        return total + grad_in[lax.rem(me - a + n, n) * nf + lax.rem(mine - f + nf, nf)]

    gradient_ref[...] = lax.fori_loop(0, n * nf, add_one, jnp.zeros(own.shape, F32), unroll=4)


def write_kernel(forward_ref, adjoint_ref, gradient_ref, forward_out, adjoint_out, gradient_out, sems):
    copies = [
        pltpu.make_async_copy(src, dst, sems.at[k])
        for k, (src, dst) in enumerate([
            (forward_ref, forward_out), (adjoint_ref, adjoint_out), (gradient_ref, gradient_out),
        ])
    ]
    for copy in copies:
        copy.start()
    for copy in copies:
        copy.wait()


def body(source, omega, sigma_blocks, block_ids, rec_owner, rec_edge, observed):
    n, nf = lax.axis_size("slab"), lax.axis_size("freq")
    planes, rows, lanes = block_ids.shape
    blocks = sigma_blocks.shape[0]
    high_blocks = blocks // LOW
    vmem = pl.BlockSpec(memory_space=pltpu.VMEM)
    smem = pl.BlockSpec(memory_space=pltpu.SMEM)
    anywhere = pl.BlockSpec(memory_space=pl.ANY)
    cells_rows = 3 * planes * rows
    wide_planes = planes + 2 * WIDTH
    slots = n * CAP
    field = (2, 3, planes, rows, lanes)
    halo = pltpu.VMEM((SWEEPS, 4 * rows, lanes), F32)
    dma = pltpu.SemaphoreType.DMA
    grad_shape = (high_blocks // 8, lanes)
    grad = pltpu.VMEM(grad_shape, F32)
    wide = pltpu.VMEM((wide_planes, rows, lanes), F32)
    operands = (
        source[0], sigma_blocks.reshape(-1, lanes), block_ids, rec_owner.reshape(1, -1), rec_edge.reshape(1, -1),
        observed[0],
    )
    operands = [pltpu.with_memory_space_constraint(a, pltpu.HBM) for a in operands]
    results = pl.pallas_call(
        functools.partial(kernel, n, nf, high_blocks),
        out_shape=(pltpu.VMEM(field, F32), pltpu.VMEM(field, F32), pltpu.VMEM(grad_shape, F32)),
        in_specs=[smem] + [anywhere] * 6,
        out_specs=(vmem, vmem, vmem),
        scratch_shapes=[
            pltpu.VMEM(field, BF16),
            pltpu.VMEM((blocks // lanes, lanes), F32),
            pltpu.VMEM((planes, rows, lanes), jnp.int32),
            pltpu.VMEM((1, lanes), jnp.int32),
            pltpu.VMEM((1, lanes), jnp.int32),
            pltpu.VMEM((2, lanes), F32),
            wide, wide, wide,
            pltpu.VMEM((planes * rows, lanes), F32),
            pltpu.VMEM((2, WIDTH * rows, lanes), F32),
            pltpu.VMEM((8, lanes), F32),
            pltpu.VMEM((8, slots), F32),
            pltpu.VMEM((2, 8, slots), F32),
            pltpu.VMEM((SWEEPS + 1, 2, 3, wide_planes, rows, lanes), F32),
            pltpu.VMEM((2, 3, wide_planes, rows + 8, lanes), F32),
            pltpu.VMEM((2, 3, wide_planes, rows + 8, lanes), F32),
            halo, halo, halo, halo,
            pltpu.VMEM((COUNT, lanes), F32),
            pltpu.VMEM((2, 1, lanes), F32),
            pltpu.VMEM((2, n, 1, lanes), F32),
            pltpu.VMEM((n, 8, lanes), F32),
            grad,
            pltpu.VMEM((n * nf,) + grad_shape, F32),
            pltpu.VMEM((8, slots, lanes), F32),
            pltpu.VMEM((slots, cells_rows), BF16),
            pltpu.VMEM((3 * wide_planes * rows, slots), BF16),
            pltpu.VMEM((cells_rows, 2 * lanes), BF16),
            pltpu.VMEM((cells_rows, 2 * lanes), BF16),
            pltpu.VMEM((slots, 2 * lanes), BF16),
            pltpu.VMEM((slots, 2 * lanes), BF16),
            pltpu.VMEM((8 * high_blocks, 8 * LOW), F32),
            pltpu.VMEM((planes * rows // 8, 8 * high_blocks, lanes), BF16),
            pltpu.VMEM((planes * rows // 8, 8 * LOW, lanes), F32),
            pltpu.VMEM((SWEEPS, 2, planes, rows, lanes), F32),
            dma((6,)),
            dma((SWEEPS, 2)), dma((SWEEPS, 2)), dma((SWEEPS, 2)), dma((SWEEPS, 2)),
            dma((2, n)), dma((2, n)),
            dma((n,)), dma((n,)),
            dma((n * nf,)), dma((n * nf,)),
            dma((4,)), dma((4,)),
            dma((2, nf)), dma((2, nf)),
        ],
        compiler_params=pltpu.CompilerParams(
            collective_id=0, has_side_effects=True, vmem_limit_bytes=50 * 1024 * 1024
        ),
        name="solves",
    )(omega, *operands)
    forward, adjoint, gradient = pl.pallas_call(
        write_kernel,
        out_shape=(
            jax.ShapeDtypeStruct(field, F32), jax.ShapeDtypeStruct(field, F32), jax.ShapeDtypeStruct(grad_shape, F32),
        ),
        in_specs=[vmem] * 3,
        out_specs=(anywhere,) * 3,
        scratch_shapes=[dma((3,))],
        name="write",
    )(*[pltpu.with_memory_space_constraint(a, pltpu.VMEM) for a in results])
    return forward[None], adjoint[None], gradient.reshape(blocks)


def solution(mesh):
    return jax.shard_map(
        body,
        mesh=mesh,
        in_specs=(
            P("freq", None, None, "slab", None, None),
            P("freq"),
            P(),
            P("slab", None, None),
            P("slab", None),
            P("slab"),
            P("freq", None, "slab"),
        ),
        out_specs=(
            P("freq", None, None, "slab", None, None),
            P("freq", None, None, "slab", None, None),
            P(),
        ),
        check_vma=False,
    )
```

```python
import functools

import jax
import jax.numpy as jnp
from jax import lax
from jax.experimental import pallas as pl
from jax.experimental.pallas import tpu as pltpu
from jax.sharding import PartitionSpec as P

SWEEPS = 4
EPSILON = 1e-06
LOW = 16
CAP = 32
MESH = pl.DeviceIdType.MESH
F32 = jnp.float32
BF16 = jnp.bfloat16
PAIRS = [(i, j) for j in range(1, SWEEPS + 1) for i in range(j + 1)]
COUNT = sum(1 if i == j else 2 for i, j in PAIRS)
WIDTH = SWEEPS


def split(values):
    high = values.astype(BF16)
    return high, (values - high.astype(F32)).astype(BF16)


def kernel(
    n, nf, high_blocks,
    omega_ref, source_hbm, sigma_hbm, ids_hbm, owner_hbm, edge_hbm, observed_hbm,
    forward_ref, adjoint_ref, gradient_ref,
    source_ref, sigma_ref, ids_ref, owner_ref, edge_ref, observed_ref,
    damp, real_ref, imag_ref, cond, beside, pack_ref, mis_out, mis_in,
    basis, zb, curl, up_out, down_out, low_in, high_in,
    gram_acc, gram_out, gram_in, pack_in, grad_out, grad_in,
    columns, hot, hot_t, field_hi, field_lo, mis_hi, mis_lo, acc, hot_block, low_block, overlap,
    local_s, up_s, up_r, down_s, down_r, gram_s, gram_r, pack_s, pack_r, grad_s, grad_r,
    near_s, near_r, share_s, share_r,
):
    me = lax.axis_index("slab")
    mine = lax.axis_index("freq")
    planes, rows, lanes = ids_ref.shape
    first, last = WIDTH, WIDTH + planes - 1
    wide_planes = planes + 2 * WIDTH
    cells_rows = 3 * planes * rows
    slots = n * CAP
    side_rows = WIDTH * rows
    part = side_rows // nf

    loads = [
        pltpu.make_async_copy(src, dst, local_s.at[k])
        for k, (src, dst) in enumerate([
            (ids_hbm, ids_ref), (sigma_hbm, sigma_ref), (source_hbm, source_ref),
            (owner_hbm, owner_ref), (edge_hbm, edge_ref), (observed_hbm, observed_ref),
        ])
    ]
    for copy in loads:
        copy.start()

    barrier = pltpu.get_barrier_semaphore()
    for k in range(1, n * nf):
        pl.semaphore_signal(
            barrier, inc=1, device_id={"slab": lax.rem(me + k // nf, n), "freq": lax.rem(mine + k % nf, nf)},
            device_id_type=MESH,
        )

    def spread(src, dst, send, recv, axis, count, position):
        copies = []
        for d in range(1, count):
            copy = pltpu.make_async_remote_copy(
                src_ref=src, dst_ref=dst.at[d], send_sem=send.at[d], recv_sem=recv.at[d],
                device_id={axis: lax.rem(position + d, count)}, device_id_type=MESH,
            )
            copy.start()
            copies.append(copy)
        return copies

    def total_of(own, buffer, count, position):
        buffer[0] = own
        total = jnp.zeros(own.shape, F32)
        for p in range(count):
            total = total + buffer[lax.rem(position - p + count, count)]
        return total

    lane = lax.broadcasted_iota(jnp.int32, (rows, lanes), 1)
    inner = slice(0, rows)
    above = slice(1, rows + 1)
    shifted = slice(8, rows + 8)
    under = slice(7, rows + 7)

    def f3(v):
        return jnp.where(lane[: v.shape[0]] == lanes - 1, 0.0, pltpu.roll(v, lanes - 1, 1)) - v

    def g3(v):
        return jnp.where(lane[: v.shape[0]] == 0, 0.0, pltpu.roll(v, 1, 1)) - v

    valid = jnp.where(me > 0, 1.0, 0.0).astype(F32)
    omega = omega_ref[0]

    def factors(x, at, damping):
        inverse = 1.0 / (16.0 + damping * damping)
        damp[x, at] = damping
        real_ref[x, at] = 4.0 * inverse
        imag_ref[x, at] = damping * inverse

    def pad(x, carry):
        for c in range(2):
            for comp in range(3):
                zb[c, comp, x, rows : rows + 8] = jnp.zeros((8, lanes), F32)
                curl[c, comp, x, 0:8] = jnp.zeros((8, lanes), F32)
        return carry

    lax.fori_loop(0, wide_planes, pad, 0)

    chunks = rows // 16
    loads[0].wait()
    loads[1].wait()
    loads[2].wait()
    tables = [jnp.broadcast_to(sigma_ref[k : k + 1, :], (8, lanes)) for k in range(sigma_ref.shape[0])]

    def begin(x, y):
        for half in range(2):
            at = pl.ds(pl.multiple_of(y + 8 * half, 8), 8)
            ids = ids_ref[x, at, :]
            low, high = ids & (lanes - 1), ids >> 7
            value = jnp.take_along_axis(tables[0], low, axis=1)
            for k in range(1, len(tables)):
                value = jnp.where(high == k, jnp.take_along_axis(tables[k], low, axis=1), value)
            cond[pl.ds(pl.multiple_of(x * rows + y + 8 * half, 8), 8), :] = value
            factors(x + first, at, omega * value)
        at = pl.ds(y, 16)
        for c in range(2):
            for comp in range(3):
                basis[0, c, comp, x + first, at] = source_ref[c, comp, x, at, :].astype(F32)

    def begin_ends(i, carry):
        begin(i // chunks * (planes - 1), pl.multiple_of(i % chunks * 16, 16))
        return carry

    def begin_inner(i, carry):
        begin(i // chunks + 1, pl.multiple_of(i % chunks * 16, 16))
        return carry

    lax.fori_loop(0, 2 * chunks, begin_ends, 0, unroll=4)

    def beside_copy(side):
        start, to = (planes * rows - side_rows, me + 1) if side == 0 else (0, me + n - 1)
        return pltpu.make_async_remote_copy(
            src_ref=cond.at[pl.ds(start + mine * part, part)], dst_ref=beside.at[side, pl.ds(mine * part, part)],
            send_sem=near_s.at[side], recv_sem=near_r.at[side], device_id={"slab": lax.rem(to, n)},
            device_id_type=MESH,
        )

    def share_copies(side):
        at = pl.ds(mine * part, part)
        return [
            pltpu.make_async_remote_copy(
                src_ref=beside.at[side, at], dst_ref=beside.at[side, at], send_sem=share_s.at[side, d],
                recv_sem=share_r.at[side, d], device_id={"freq": lax.rem(mine + d, nf)}, device_id_type=MESH,
            )
            for d in range(1, nf)
        ]

    def misfit_copy(side):
        to = me + 1 if side == 0 else me + n - 1
        return pltpu.make_async_remote_copy(
            src_ref=mis_out, dst_ref=mis_in.at[side], send_sem=near_s.at[2 + side],
            recv_sem=near_r.at[2 + side], device_id={"slab": lax.rem(to, n)}, device_id_type=MESH,
        )

    def cut_of(t):
        return rows // 8 // 2 * 8 + 8 * (1 - t)

    def rows_of(t, half):
        return (0, cut_of(t)) if half == 0 else (cut_of(t), rows)

    def span(t, half):
        lo, hi = rows_of(t, half)
        return pl.ds(4 * lo, 4 * (hi - lo))

    def place_of(t, half, c, k):
        lo, hi = rows_of(t, half)
        start = 4 * lo + (2 * c + k) * (hi - lo)
        return slice(start, start + hi - lo)

    def up_copy(t, half):
        at = span(t, half)
        return pltpu.make_async_remote_copy(
            src_ref=up_out.at[t, at], dst_ref=low_in.at[t, at], send_sem=up_s.at[t, half],
            recv_sem=up_r.at[t, half], device_id={"slab": lax.rem(me + 1, n)}, device_id_type=MESH,
        )

    def down_copy(t, half):
        at = span(t, half)
        return pltpu.make_async_remote_copy(
            src_ref=down_out.at[t, at], dst_ref=high_in.at[t, at], send_sem=down_s.at[t, half],
            recv_sem=down_r.at[t, half], device_id={"slab": lax.rem(me + n - 1, n)}, device_id_type=MESH,
        )

    def precondition(t, x, at=inner):
        mr, mi = real_ref[x, at], imag_ref[x, at]
        for comp in range(3):
            br, bi = basis[t, 0, comp, x, at], basis[t, 1, comp, x, at]
            zb[0, comp, x, at] = mr * br + mi * bi
            zb[1, comp, x, at] = mr * bi - mi * br

    def curls(x):
        for c in range(2):
            e1, e2, e3 = zb[c, 0, x, inner], zb[c, 1, x, inner], zb[c, 2, x, inner]
            curl[c, 0, x, shifted] = (zb[c, 2, x, above] - e3) - f3(e2)
            curl[c, 1, x, shifted] = f3(e1) - (zb[c, 2, x + 1, inner] - e3)
            curl[c, 2, x, shifted] = (zb[c, 1, x + 1, inner] - e2) - (zb[c, 0, x, above] - e1)

    def images(t, x):
        damping = damp[x]
        for c in range(2):
            b1, b2, b3 = curl[c, 0, x, shifted], curl[c, 1, x, shifted], curl[c, 2, x, shifted]
            b2p, b3p = curl[c, 1, x - 1, shifted], curl[c, 2, x - 1, shifted]
            parts = (
                g3(b2) - (curl[c, 2, x, under] - b3),
                (b3p - b3) - g3(b1),
                (curl[c, 0, x, under] - b1) - (b2p - b2),
            )
            for comp in range(3):
                turned = damping * zb[1 - c, comp, x, inner]
                basis[t + 1, c, comp, x] = parts[comp] - turned if c == 0 else parts[comp] + turned

    def sweep_inner(t):
        for k in range(1, 4):
            precondition(t, first + k)
        curls(first)
        curls(first + 1)

        def step(x, carry):
            images(t, x)
            curls(x + 1)
            precondition(t, x + 3)
            return carry

        lax.fori_loop(first + 1, last - 3, step, 0)
        images(t, last - 3)
        curls(last - 2)
        images(t, last - 2)
        curls(last - 1)
        images(t, last - 1)
        for c in range(2):
            def turn(x, comp):
                turned = damp[x] * zb[1 - c, comp, x, inner]
                return turned if c else -turned

            b1, b2, b3 = (curl[c, k, first, shifted] for k in range(3))
            basis[t + 1, c, 0, first] = g3(b2) - (curl[c, 2, first, under] - b3) + turn(first, 0)
            basis[t + 1, c, 1, first] = turn(first, 1) - b3 - g3(b1)
            basis[t + 1, c, 2, first] = (curl[c, 0, first, under] - b1) + b2 + turn(first, 2)
            e2, e3 = zb[c, 1, last, inner], zb[c, 2, last, inner]
            b1 = (zb[c, 2, last, above] - e3) - f3(e2)
            curl[c, 0, last, shifted] = b1
            basis[t + 1, c, 0, last] = turn(last, 0)
            basis[t + 1, c, 1, last] = turn(last, 1) + curl[c, 2, last - 1, shifted] - g3(b1)
            basis[t + 1, c, 2, last] = turn(last, 2) - curl[c, 1, last - 1, shifted]
            basis[t + 1, c, 2, last] += curl[c, 0, last, under] - b1

    def send_down(t, half):
        lo, hi = rows_of(t, half)
        for c in range(2):
            for k in range(2):
                down_out[t, place_of(t, half, c, k)] = zb[c, 1 + k, first, lo:hi]

        @pl.when(me > 0)
        def _():
            down_copy(t, half).start()

    def send_up(t, half):
        lo, hi = rows_of(t, half)
        for c in range(2):
            e1 = zb[c, 0, last, lo:hi]
            up_out[t, place_of(t, half, c, 0)] = f3(e1) + zb[c, 2, last, lo:hi]
            up_out[t, place_of(t, half, c, 1)] = (zb[c, 0, last, lo + 1 : hi + 1] - e1) + zb[c, 1, last, lo:hi]

        @pl.when(me < n - 1)
        def _():
            up_copy(t, half).start()

    def receive(t, half):
        lo, hi = rows_of(t, half)
        at = slice(lo, hi)

        @pl.when(me < n - 1)
        def _():
            down_copy(t, half).wait_recv()

        for c in range(2):
            b2 = up_out[t, place_of(t, half, c, 0)] - high_in[t, place_of(t, half, c, 1)]
            b3 = high_in[t, place_of(t, half, c, 0)] - up_out[t, place_of(t, half, c, 1)]
            curl[c, 2, last, lo + 8 : hi + 8] = b3
            basis[t + 1, c, 0, last, at] += g3(b2) - (curl[c, 2, last, lo + 7 : hi + 7] - b3)
            basis[t + 1, c, 1, last, at] -= b3
            basis[t + 1, c, 2, last, at] += b2
        if t < SWEEPS - 1:
            precondition(t + 1, last, at)
            send_up(t + 1, half)

        @pl.when(me > 0)
        def _():
            up_copy(t, half).wait_recv()

        for c in range(2):
            b2p = (low_in[t, place_of(t, half, c, 0)] - zb[c, 2, first, at]) * valid
            b3p = (zb[c, 1, first, at] - low_in[t, place_of(t, half, c, 1)]) * valid
            basis[t + 1, c, 1, first, at] += b3p
            basis[t + 1, c, 2, first, at] -= b2p
        if t < SWEEPS - 1:
            precondition(t + 1, first, at)
            send_down(t + 1, half)

    def forward_sweep(t, before, between):
        sweep_inner(t)
        before()
        receive(t, 0)
        between()
        receive(t, 1)

    def forward_sent():
        for t in range(SWEEPS):
            for half in range(2):
                @pl.when(me > 0)
                def _(t=t, half=half):
                    down_copy(t, half).wait_send()

                @pl.when(me < n - 1)
                def _(t=t, half=half):
                    up_copy(t, half).wait_send()

    per = rows // 8

    def products(j_, x, at, sums):
        sums = list(sums)
        for comp in range(3):
            re = [basis[k, 0, comp, x, at, :] for k in range(j_ + 1)]
            im = [basis[k, 1, comp, x, at, :] for k in range(j_ + 1)]
            for i_ in range(j_ + 1):
                sums[2 * i_] = sums[2 * i_] + (re[i_] * re[j_] + im[i_] * im[j_])
                if i_ != j_:
                    sums[2 * i_ + 1] = sums[2 * i_ + 1] + (re[i_] * im[j_] - im[i_] * re[j_])
        return tuple(sums)

    def blank_sums(j_):
        return (jnp.zeros((8, lanes), F32),) * (2 * j_ + 1)

    def keep_sums(j_, sums):
        for k in range(2 * j_ + 1):
            at = j_ * j_ - 1 + k
            gram_acc[at : at + 1, :] = jnp.sum(sums[k], axis=0, keepdims=True)

    def pair_sums(j_, start, step, count, sums):
        def body_(i, sums):
            return products(j_, i // per * step + start, pl.ds(pl.multiple_of(i % per * 8, 8), 8), sums)

        return lax.fori_loop(0, count * per, body_, sums, unroll=2)

    def all_sums(j_):
        keep_sums(j_, pair_sums(j_, first, 1, planes, blank_sums(j_)))

    def sweep(t):
        lo, hi = t, wide_planes - t - 1
        wanted = [t] if 0 < t < SWEEPS - 1 else [t, t + 1] if t else []
        for k in range(4):
            precondition(t, lo + k)
        curls(lo)
        curls(lo + 1)

        def gather(x, sums):
            return tuple(
                functools.reduce(lambda held, y: products(j, x, slice(y, y + 8), held), range(0, rows, 8), own)
                for j, own in zip(wanted, sums)
            )

        def step(x, carry, inside):
            images(t, x)
            curls(x + 1)
            precondition(t, x + 3)
            return gather(x, carry) if inside else carry

        sums = tuple(blank_sums(j) for j in wanted)
        top = min(hi - 2, last + 1)
        lax.fori_loop(lo + 1, first, lambda x, carry: step(x, carry, False), 0)
        for c in range(2):
            for k in range(1, 3):
                curl[c, k, first - 1, shifted] = curl[c, k, first - 1, shifted] * valid
        sums = lax.fori_loop(first, top, lambda x, carry: step(x, carry, True), sums)
        lax.fori_loop(top, hi - 2, lambda x, carry: step(x, carry, False), 0)
        images(t, hi - 2)
        curls(hi - 1)
        images(t, hi - 1)
        for x in range(top, last + 1):
            sums = gather(x, sums)
        for j, own in zip(wanted, sums):
            keep_sums(j, own)

    gram_lane = lax.broadcasted_iota(jnp.int32, (COUNT, lanes), 1)
    gram_row = lax.broadcasted_iota(jnp.int32, (COUNT, lanes), 0)
    diagonal_of = gram_lane == gram_row

    def gram_start(which):
        local = jnp.sum(gram_acc[...], axis=1, keepdims=True)
        gram_out[which] = jnp.sum(jnp.where(diagonal_of, local, 0.0), axis=0, keepdims=True)
        return spread(gram_out.at[which], gram_in.at[which], gram_s.at[which], gram_r.at[which], "slab", n, me)

    def coefficients(which):
        total = total_of(gram_out[which], gram_in.at[which], n, me)
        total = jnp.sum(jnp.where(diagonal_of, total, 0.0), axis=1, keepdims=True)
        total = jnp.broadcast_to(total, (COUNT, lanes))
        gram, at = {}, 0
        for i, j in PAIRS:
            re = total[at : at + 1, :]
            at += 1
            im = jnp.zeros_like(re)
            if i != j:
                im = total[at : at + 1, :]
                at += 1
            gram[i, j] = (re, im)
            gram[j, i] = (re, -im)
        one = jnp.ones((1, lanes), F32)
        none = jnp.zeros((1, lanes), F32)

        def times(a, b):
            return a[0] * b[0] - a[1] * b[1], a[0] * b[1] + a[1] * b[0]

        poly = [(one, none)]
        coef = [(none, none) for _ in range(SWEEPS)]
        for k in range(SWEEPS):
            up = (none, none)
            below = none
            for i in range(k + 1):
                conj = (poly[i][0], -poly[i][1])
                for j in range(k + 1):
                    both = times(conj, poly[j])
                    term = times(both, gram[i + 1, j])
                    up = (up[0] + term[0], up[1] + term[1])
                    below = below + times(both, gram[i + 1, j + 1])[0]
            below = below + EPSILON
            step = (up[0] / below, up[1] / below)
            moved = [times(step, p) for p in poly]
            for i in range(k + 1):
                coef[i] = (coef[i][0] + moved[i][0], coef[i][1] + moved[i][1])
            grown = poly + [(none, none)]
            for i in range(k + 1):
                grown[i + 1] = (grown[i + 1][0] - moved[i][0], grown[i + 1][1] - moved[i][1])
            poly = grown

        return [(jnp.broadcast_to(a, (16, lanes)), jnp.broadcast_to(b, (16, lanes))) for a, b in coef]

    def combine(wide, out_ref, keep_parts):
        def step(i, carry):
            x, y = i // chunks, pl.multiple_of(i % chunks * 16, 16)
            at = pl.ds(y, 16)
            mr, mi = real_ref[x + first, at, :], imag_ref[x + first, at, :]
            for comp in range(3):
                sr = jnp.zeros((16, lanes), F32)
                si = jnp.zeros((16, lanes), F32)
                for k in range(SWEEPS):
                    br, bi = basis[k, 0, comp, x + first, at, :], basis[k, 1, comp, x + first, at, :]
                    sr = sr + (wide[k][0] * br - wide[k][1] * bi)
                    si = si + (wide[k][0] * bi + wide[k][1] * br)
                for c, value in enumerate((mr * sr + mi * si, mr * si - mi * sr)):
                    out_ref[c, comp, x, at, :] = value
                    if keep_parts:
                        here = pl.ds(pl.multiple_of((comp * planes + x) * rows + y, 16), 16)
                        hi, lo = split(value)
                        field_hi[here, c * lanes : (c + 1) * lanes] = hi
                        field_lo[here, c * lanes : (c + 1) * lanes] = lo
            return carry

        lax.fori_loop(0, planes * chunks, step, 0, unroll=2)

    packs = [
        pltpu.make_async_remote_copy(
            src_ref=pack_ref, dst_ref=pack_in.at[me], send_sem=pack_s.at[d], recv_sem=pack_r.at[d],
            device_id={"slab": lax.rem(me + d, n)}, device_id_type=MESH,
        )
        for d in range(1, n)
    ]

    cap_row = lax.broadcasted_iota(jnp.int32, (CAP, lanes), 0).astype(F32)
    lane_sq = lax.broadcasted_iota(jnp.int32, (lanes, lanes), 1).astype(F32)
    row_sq = lax.broadcasted_iota(jnp.int32, (lanes, lanes), 0).astype(F32)
    earlier = jnp.where(row_sq < lane_sq, 1.0, 0.0).astype(F32)
    self_id = me.astype(F32)

    def compact(p, carry):
        pack = pack_in[p]
        owner, number, spot = pack[0:1, :], pack[1:2, :], pack[2:3, :]
        third = jnp.where(number >= 2.0 * planes * rows, 2.0, jnp.where(number >= 1.0 * planes * rows, 1.0, 0.0))
        inside = number - third * float(planes * rows)
        upper = inside - float((planes - WIDTH) * rows)
        low_place = jnp.where(upper >= 0.0, third * float(side_rows) + upper, -1.0)
        high_place = jnp.where(inside < float(side_rows), third * float(side_rows) + inside, -1.0)
        owned = [jnp.where(owner == self_id + shift, 1.0, 0.0) for shift in (0.0, -1.0, 1.0)]
        owned = jnp.concatenate(owned + [jnp.zeros((5, lanes), F32)], axis=0)
        rank = jnp.dot(owned, earlier, preferred_element_type=F32)
        at = pl.ds(pl.multiple_of(p * CAP, CAP), CAP)
        wanted = (
            (0, 0, number + 1.0), (1, 0, spot), (2, 0, pack[3:4, :]), (3, 0, pack[4:5, :]),
            (4, 1, low_place + 1.0), (5, 1, spot), (6, 2, high_place + 1.0), (7, 2, spot),
        )
        for k, target, value in wanted:
            hit = (cap_row == rank[target : target + 1, :]) & (owned[target : target + 1, :] > 0.0)
            found = jnp.sum(jnp.where(hit, value, 0.0), axis=1, keepdims=True)
            columns[k, at, :] = jnp.broadcast_to(found, (CAP, lanes))
        return carry

    def picks(p, carry):
        at = pl.ds(pl.multiple_of(p * CAP, CAP), CAP)
        place = columns[0, at, :] - 1.0
        for b in range(cells_rows // lanes):
            hot[at, b * lanes : (b + 1) * lanes] = jnp.where(
                lane_sq[:CAP] == place - float(b * lanes), 1.0, 0.0
            ).astype(BF16)
        return carry

    def placings(start, k, count):
        for q in range(slots // lanes):
            spot = columns[k, q * lanes : (q + 1) * lanes, :].T - 1.0

            def fill(b, carry):
                base = pl.multiple_of(b * lanes, lanes)
                hot_t[pl.ds(start + base, lanes), q * lanes : (q + 1) * lanes] = jnp.where(
                    row_sq + base.astype(F32) == spot, 1.0, 0.0
                ).astype(BF16)
                return carry

            lax.fori_loop(0, count // lanes, fill, 0)

    def spread_values(k, re, im):
        here = lane_of_slot == columns[k]
        for part_, value in enumerate((re, im)):
            hi, lo = split(jnp.where(here, value, 0.0))
            mis_hi[:, part_ * lanes : (part_ + 1) * lanes] = hi
            mis_lo[:, part_ * lanes : (part_ + 1) * lanes] = lo

    def add_source(start, x0, count, group):
        for comp in range(3):
            for x in range(0, count, group):
                begin_ = start + (comp * count + x) * rows
                block = hot_t[begin_ : begin_ + group * rows, :]
                added = jnp.dot(block, mis_hi[...], preferred_element_type=F32)
                added = added + jnp.dot(block, mis_lo[...], preferred_element_type=F32)
                for c in range(2):
                    basis[0, c, comp, x0 + x : x0 + x + group] = added[:, c * lanes : (c + 1) * lanes].reshape(
                        group, rows, lanes
                    )

    lane_of_slot = lax.broadcasted_iota(jnp.int32, (slots, lanes), 1).astype(F32)

    precondition(0, first)
    precondition(0, last)

    @pl.when(me == 0)
    def _():
        low_in[...] = jnp.zeros(low_in.shape, F32)

    @pl.when(me == n - 1)
    def _():
        high_in[...] = jnp.zeros(high_in.shape, F32)

    pl.semaphore_wait(barrier, n * nf - 1)
    send_down(0, 0)
    send_up(0, 0)
    loads[3].wait()
    loads[4].wait()
    loads[5].wait()
    edge = edge_ref[...]
    pack_ref[...] = jnp.concatenate(
        [
            owner_ref[...].astype(F32), (edge >> 7).astype(F32), (edge & 127).astype(F32), observed_ref[...],
            jnp.zeros((3, lanes), F32),
        ],
        axis=0,
    )
    pack_in[me] = pack_ref[...]
    half_way = (planes - 2) // 2 * chunks
    lax.fori_loop(0, half_way, begin_inner, 0, unroll=4)
    send_down(0, 1)
    send_up(0, 1)
    lax.fori_loop(half_way, (planes - 2) * chunks, begin_inner, 0, unroll=4)
    for copy in packs:
        copy.start()

    def nothing():
        pass

    def receive_packs():
        all_sums(2)
        for copy in packs:
            copy.wait()
        lax.fori_loop(0, n, compact, 0)

    last_sums = []

    def near_last():
        all_sums(3)
        last_sums.append(pair_sums(SWEEPS, first + 1, 1, planes - 2, blank_sums(SWEEPS)))

    forward_sweep(0, nothing, nothing)
    forward_sweep(1, nothing, functools.partial(all_sums, 1))
    forward_sweep(2, nothing, receive_packs)
    forward_sweep(3, nothing, near_last)
    keep_sums(SWEEPS, pair_sums(SWEEPS, first, planes - 1, 2, last_sums[0]))
    sums_sent = gram_start(0)
    forward_sent()
    lax.fori_loop(0, n, picks, 0)
    placings(0, 0, cells_rows)
    placings(cells_rows, 4, 3 * side_rows)
    placings(cells_rows + 3 * side_rows, 6, 3 * side_rows)
    for copy in sums_sent:
        copy.wait()

    @pl.when(me > 0)
    def _():
        beside_copy(1).start()

    @pl.when(me < n - 1)
    def _():
        beside_copy(0).start()

    combine(coefficients(0), forward_ref, True)

    picked = jnp.dot(hot[...], field_hi[...], preferred_element_type=F32)
    picked = picked + jnp.dot(hot[...], field_lo[...], preferred_element_type=F32)
    here = lane_of_slot == columns[1]
    re = jnp.sum(jnp.where(here, picked[:, :lanes], 0.0), axis=1, keepdims=True) - columns[2]
    im = columns[3] - jnp.sum(jnp.where(here, picked[:, lanes:], 0.0), axis=1, keepdims=True)
    both = jnp.where(lane_of_slot == 0.0, re, jnp.where(lane_of_slot == 1.0, im, 0.0))
    mis_out[...] = both.T[0:8, :]

    @pl.when(me > 0)
    def _():
        misfit_copy(1).start()
        beside_copy(0).wait_recv()
        for copy in share_copies(0):
            copy.start()

    @pl.when(me < n - 1)
    def _():
        misfit_copy(0).start()
        beside_copy(1).wait_recv()
        for copy in share_copies(1):
            copy.start()

    spread_values(1, re, im)
    add_source(0, first, planes, 4)

    for side, there in enumerate((me > 0, me < n - 1)):
        start = 0 if side == 0 else last + 1

        @pl.when(there)
        def _(side=side, start=start):
            beside_copy(1 - side).wait_send()
            for copy in share_copies(side):
                copy.wait()
            for k in range(WIDTH):
                factors(start + k, inner, omega * beside[side, k * rows : (k + 1) * rows, :])
            misfit_copy(side).wait_recv()
            misfit_copy(1 - side).wait_send()

        @pl.when(jnp.logical_not(there))
        def _(side=side, start=start):
            mis_in[side] = jnp.zeros(mis_in.shape[1:], F32)
            for k in range(WIDTH):
                damp[start + k] = jnp.zeros((rows, lanes), F32)
                real_ref[start + k] = jnp.zeros((rows, lanes), F32)
                imag_ref[start + k] = jnp.zeros((rows, lanes), F32)

        column = jnp.concatenate([mis_in[side]] * (lanes // 8), axis=0).T
        spread_values(5 + 2 * side, column[:, 0:1], column[:, 1:2])
        add_source(cells_rows + side * 3 * side_rows, start, WIDTH, WIDTH)

    for t in range(SWEEPS):
        sweep(t)
    sums_sent = gram_start(1)

    high_iota = lax.broadcasted_iota(jnp.int32, (high_blocks, lanes), 0)
    low_iota = lax.broadcasted_iota(jnp.int32, (LOW, lanes), 0)

    def block_rows(i, carry):
        x, y = i // per, pl.multiple_of(i % per * 8, 8)
        ids = ids_ref[x, pl.ds(y, 8), :]
        high, low = ids >> 4, ids & (LOW - 1)
        hot_block[i] = jnp.concatenate(
            [jnp.where(high[r : r + 1, :] == high_iota, 1.0, 0.0) for r in range(8)], axis=0
        ).astype(BF16)
        for r in range(8):
            low_block[i, r * LOW : (r + 1) * LOW, :] = jnp.where(low[r : r + 1, :] == low_iota, 1.0, 0.0)
        return carry

    def overlaps(i, carry):
        x, y = i // chunks, pl.multiple_of(i % chunks * 16, 16)
        at = pl.ds(y, 16)
        field = [[forward_ref[c, comp, x, at, :] for comp in range(3)] for c in range(2)]
        mr, mi = real_ref[x + first, at, :], imag_ref[x + first, at, :]
        for k in range(SWEEPS):
            qr = jnp.zeros((16, lanes), F32)
            qi = jnp.zeros((16, lanes), F32)
            for comp in range(3):
                br, bi = basis[k, 0, comp, x + first, at, :], basis[k, 1, comp, x + first, at, :]
                qr = qr + (br * field[0][comp] - bi * field[1][comp])
                qi = qi + (br * field[1][comp] + bi * field[0][comp])
            overlap[k, 0, x, at] = mr * qr + mi * qi
            overlap[k, 1, x, at] = mr * qi - mi * qr
        return carry

    lax.fori_loop(0, planes * per, block_rows, 0, unroll=4)
    lax.fori_loop(0, planes * chunks, overlaps, 0, unroll=2)
    for copy in sums_sent:
        copy.wait()
    adjoint_steps = coefficients(1)

    acc[...] = jnp.zeros(acc.shape, F32)

    def cells(i, carry):
        x, y = i // per, pl.multiple_of(i % per * 8, 8)
        at = pl.ds(y, 8)
        value = jnp.zeros((8, lanes), F32)
        for k in range(SWEEPS):
            cr, ci = adjoint_steps[k][0][:8], adjoint_steps[k][1][:8]
            value = value + (cr * overlap[k, 1, x, at, :] + ci * overlap[k, 0, x, at, :])
        value = omega * value
        spot = jnp.concatenate(
            [low_block[i, r * LOW : (r + 1) * LOW, :] * value[r : r + 1, :] for r in range(8)], axis=0
        )
        here = hot_block[i]
        acc[...] += lax.dot_general(
            jnp.concatenate([here, here], axis=1), jnp.concatenate(split(spot), axis=1),
            (((1,), (1,)), ((), ())), preferred_element_type=F32,
        )
        return carry

    lax.fori_loop(0, planes * per, cells, 0, unroll=8)
    wide_lane = lax.broadcasted_iota(jnp.int32, (high_blocks, 8 * LOW), 1)
    folded = jnp.zeros((high_blocks, 8 * LOW), F32)
    for r in range(8):
        inside = (wide_lane >= r * LOW) & (wide_lane < (r + 1) * LOW)
        folded = folded + jnp.where(inside, acc[r * high_blocks : (r + 1) * high_blocks, :], 0.0)
    for shift in (64, 32, 16):
        folded = folded + pltpu.roll(folded, shift, 1)
    fold_lane = lax.broadcasted_iota(jnp.int32, (8, lanes), 1) // LOW
    fold_row = lax.broadcasted_iota(jnp.int32, (8, lanes), 0)
    own = jnp.concatenate(
        [
            jnp.sum(jnp.where(fold_lane == fold_row, folded[8 * k : 8 * k + 8, :], 0.0), axis=0, keepdims=True)
            for k in range(high_blocks // 8)
        ],
        axis=0,
    )
    grad_out[...] = own
    copies = []
    for k in range(1, n * nf):
        copy = pltpu.make_async_remote_copy(
            src_ref=grad_out, dst_ref=grad_in.at[k], send_sem=grad_s.at[k], recv_sem=grad_r.at[k],
            device_id={"slab": lax.rem(me + k // nf, n), "freq": lax.rem(mine + k % nf, nf)}, device_id_type=MESH,
        )
        copy.start()
        copies.append(copy)
    grad_in[0] = own
    combine(adjoint_steps, adjoint_ref, False)
    for copy in copies:
        copy.wait()

    def add_one(k, total):
        a, f = k // nf, k % nf
        return total + grad_in[lax.rem(me - a + n, n) * nf + lax.rem(mine - f + nf, nf)]

    gradient_ref[...] = lax.fori_loop(0, n * nf, add_one, jnp.zeros(own.shape, F32), unroll=4)


def write_kernel(forward_ref, adjoint_ref, gradient_ref, forward_out, adjoint_out, gradient_out, sems):
    copies = [
        pltpu.make_async_copy(src, dst, sems.at[k])
        for k, (src, dst) in enumerate([
            (forward_ref, forward_out), (adjoint_ref, adjoint_out), (gradient_ref, gradient_out),
        ])
    ]
    for copy in copies:
        copy.start()
    for copy in copies:
        copy.wait()


def body(source, omega, sigma_blocks, block_ids, rec_owner, rec_edge, observed):
    n, nf = lax.axis_size("slab"), lax.axis_size("freq")
    planes, rows, lanes = block_ids.shape
    blocks = sigma_blocks.shape[0]
    high_blocks = blocks // LOW
    vmem = pl.BlockSpec(memory_space=pltpu.VMEM)
    smem = pl.BlockSpec(memory_space=pltpu.SMEM)
    anywhere = pl.BlockSpec(memory_space=pl.ANY)
    cells_rows = 3 * planes * rows
    wide_planes = planes + 2 * WIDTH
    slots = n * CAP
    field = (2, 3, planes, rows, lanes)
    halo = pltpu.VMEM((SWEEPS, 4 * rows, lanes), F32)
    dma = pltpu.SemaphoreType.DMA
    grad_shape = (high_blocks // 8, lanes)
    grad = pltpu.VMEM(grad_shape, F32)
    wide = pltpu.VMEM((wide_planes, rows, lanes), F32)
    operands = (
        source[0], sigma_blocks.reshape(-1, lanes), block_ids, rec_owner.reshape(1, -1), rec_edge.reshape(1, -1),
        observed[0],
    )
    operands = [pltpu.with_memory_space_constraint(a, pltpu.HBM) for a in operands]
    results = pl.pallas_call(
        functools.partial(kernel, n, nf, high_blocks),
        out_shape=(pltpu.VMEM(field, F32), pltpu.VMEM(field, F32), pltpu.VMEM(grad_shape, F32)),
        in_specs=[smem] + [anywhere] * 6,
        out_specs=(vmem, vmem, vmem),
        scratch_shapes=[
            pltpu.VMEM(field, BF16),
            pltpu.VMEM((blocks // lanes, lanes), F32),
            pltpu.VMEM((planes, rows, lanes), jnp.int32),
            pltpu.VMEM((1, lanes), jnp.int32),
            pltpu.VMEM((1, lanes), jnp.int32),
            pltpu.VMEM((2, lanes), F32),
            wide, wide, wide,
            pltpu.VMEM((planes * rows, lanes), F32),
            pltpu.VMEM((2, WIDTH * rows, lanes), F32),
            pltpu.VMEM((8, lanes), F32),
            pltpu.VMEM((8, slots), F32),
            pltpu.VMEM((2, 8, slots), F32),
            pltpu.VMEM((SWEEPS + 1, 2, 3, wide_planes, rows, lanes), F32),
            pltpu.VMEM((2, 3, wide_planes, rows + 8, lanes), F32),
            pltpu.VMEM((2, 3, wide_planes, rows + 8, lanes), F32),
            halo, halo, halo, halo,
            pltpu.VMEM((COUNT, lanes), F32),
            pltpu.VMEM((2, 1, lanes), F32),
            pltpu.VMEM((2, n, 1, lanes), F32),
            pltpu.VMEM((n, 8, lanes), F32),
            grad,
            pltpu.VMEM((n * nf,) + grad_shape, F32),
            pltpu.VMEM((8, slots, lanes), F32),
            pltpu.VMEM((slots, cells_rows), BF16),
            pltpu.VMEM((3 * wide_planes * rows, slots), BF16),
            pltpu.VMEM((cells_rows, 2 * lanes), BF16),
            pltpu.VMEM((cells_rows, 2 * lanes), BF16),
            pltpu.VMEM((slots, 2 * lanes), BF16),
            pltpu.VMEM((slots, 2 * lanes), BF16),
            pltpu.VMEM((8 * high_blocks, 8 * LOW), F32),
            pltpu.VMEM((planes * rows // 8, 8 * high_blocks, lanes), BF16),
            pltpu.VMEM((planes * rows // 8, 8 * LOW, lanes), F32),
            pltpu.VMEM((SWEEPS, 2, planes, rows, lanes), F32),
            dma((6,)),
            dma((SWEEPS, 2)), dma((SWEEPS, 2)), dma((SWEEPS, 2)), dma((SWEEPS, 2)),
            dma((2, n)), dma((2, n)),
            dma((n,)), dma((n,)),
            dma((n * nf,)), dma((n * nf,)),
            dma((4,)), dma((4,)),
            dma((2, nf)), dma((2, nf)),
        ],
        compiler_params=pltpu.CompilerParams(
            collective_id=0, has_side_effects=True, vmem_limit_bytes=50 * 1024 * 1024
        ),
        name="solves",
    )(omega, *operands)
    forward, adjoint, gradient = pl.pallas_call(
        write_kernel,
        out_shape=(
            jax.ShapeDtypeStruct(field, F32), jax.ShapeDtypeStruct(field, F32), jax.ShapeDtypeStruct(grad_shape, F32),
        ),
        in_specs=[vmem] * 3,
        out_specs=(anywhere,) * 3,
        scratch_shapes=[dma((3,))],
        name="write",
    )(*[pltpu.with_memory_space_constraint(a, pltpu.VMEM) for a in results])
    return forward[None], adjoint[None], gradient.reshape(blocks)


def solution(mesh):
    return jax.shard_map(
        body,
        mesh=mesh,
        in_specs=(
            P("freq", None, None, "slab", None, None),
            P("freq"),
            P(),
            P("slab", None, None),
            P("slab", None),
            P("slab"),
            P("freq", None, "slab"),
        ),
        out_specs=(
            P("freq", None, None, "slab", None, None),
            P("freq", None, None, "slab", None, None),
            P(),
        ),
        check_vma=False,
    )
```
